32 devices in a mesh: dp: 8 (over z, x), tensor: 4 (over y, core).
Axes of the slice: x: 2, y: 2, z: 4, core: 2. Of those that a mesh axis runs over, the one named last changes fastest.
Arguments:
- tokens: bfloat16 [14336, 768], P('dp'), may hold values from -6 to 6
- clip_starts: int32 [16, 4], P('dp'), may hold values from 0 to 896, as said below
- cls_index: int32 [16, 4], P('dp'), may hold values from 0 to 896, as said below
- norm_gains: bfloat16 [2, 768], replicated, may hold values from 0.5 to 1.5
- shifts: bfloat16 [4, 768], replicated, may hold values from -3 to 3
- qkv_weight: bfloat16 [768, 3, 768], P(None, None, 'tensor'), may hold values from -0.3125 to 0.3125
- qv_bias: bfloat16 [2, 768], P(None, 'tensor'), may hold values from -3 to 3
- out_weight: bfloat16 [768, 768], P('tensor'), may hold values from -0.625 to 0.625
- fc1_weight: bfloat16 [768, 3072], P(None, 'tensor'), may hold values from -0.21875 to 0.21875
- fc1_bias: bfloat16 [3072], P('tensor'), may hold values from -3 to 3
- fc2_weight: bfloat16 [3072, 768], P('tensor'), may hold values from -0.15625 to 0.15625
- cotangent: bfloat16 [14336, 768], P('dp'), may hold values from -6 to 6
Outputs:
- layer_out: bfloat16 [14336, 768], P('dp')
- input_grad: bfloat16 [14336, 768], P('dp')
- norm_gain_grad: float32 [2, 768], replicated
- shift_grad: float32 [4, 768], replicated
- qkv_grad: float32 [768, 3, 768], P(None, None, 'tensor')
- qv_bias_grad: float32 [2, 768], P(None, 'tensor')
- out_weight_grad: float32 [768, 768], P('tensor')
- fc1_weight_grad: float32 [768, 3072], P(None, 'tensor')
- fc1_bias_grad: float32 [3072], P('tensor')
- fc2_weight_grad: float32 [3072, 768], P('tensor')
The draws below stay inside these ranges and needn't reach their ends.
Inputs may be any that keep to these rules, and one draw needn't show every extreme that they name: `clip_starts`: row s gives where the clips of sequence s begin: entry 0 is 0, the entries below 896 rise strictly, and entries equal to 896 mark absent clips; every sequence has two to four clips. `cls_index`: entry c is the position of clip c's CLS token in its sequence, inside clip c; 896 where clip c is absent.
All inputs are finite; a program needn't handle non-finite values.
Results may differ from the reference program's by a relative error of at most 0.019.
Values may be sent and summed in bfloat16 or wider, within the bound.
A program may use at most 192 MiB of HBM per device.

```python
import jax
import jax.numpy as jnp
from jax import lax

D = 768
HEADS = 12
HEAD_DIM = 64
FF = 3072
LENGTH = 896
CLIPS = 4
SEQS = 16
TOKENS = 14336
N_TENSOR = 4


def clip_layout(key):
    count_key, shift_key, mark_key = jax.random.split(key, 3)
    sequence = jnp.arange(SEQS, dtype=jnp.int32)
    clip_count = jax.random.randint(count_key, (SEQS,), 2, 5)
    clip_count = jnp.where(sequence == 0, 2, clip_count)
    ordinal = jnp.arange(1, CLIPS, dtype=jnp.int32)
    jitter = jax.random.randint(shift_key, (SEQS, CLIPS - 1), -(LENGTH // 8), LENGTH // 8)
    cuts = ordinal[None, :] * LENGTH // clip_count[:, None] + jitter
    cuts = jnp.where(ordinal[None, :] < clip_count[:, None], cuts, LENGTH)
    starts = jnp.concatenate([jnp.zeros((SEQS, 1), jnp.int32), cuts.astype(jnp.int32)], axis=1)
    ends = jnp.concatenate([cuts.astype(jnp.int32), jnp.full((SEQS, 1), LENGTH, jnp.int32)], axis=1)
    widths = ends - starts
    offset = jax.random.randint(mark_key, (SEQS, CLIPS), 0, jnp.maximum(widths, 1))
    marks = jnp.where(widths > 0, starts + offset, LENGTH)
    return (starts.astype(jnp.int32), marks.astype(jnp.int32))


def draw_clip_starts(key, part):
    return clip_layout(key)[0]


def draw_cls_index(key, part):
    return clip_layout(key)[1]


def steps_of(stream_key, shape, shards, low, high):
    gain, own = 1.0, jax.random.fold_in(stream_key, 6)
    for dim, blocks in shards:
        draws = jnp.exp(jax.random.uniform(jax.random.fold_in(own, dim), (blocks,), jnp.float32, low / len(shards), high / len(shards)))
        gain = gain * jnp.repeat(draws, shape[dim] // blocks).reshape([-1 if axis == dim else 1 for axis in range(len(shape))])
    return gain


def bell_draw(own_key, extent, width, bound, cuts=(), kind=jnp.bfloat16):
    level = steps_of(own_key, extent, cuts, -0.22, 0.18) if cuts else 1.0
    entries = jax.random.normal(own_key, extent, jnp.float32) * width * level
    return jnp.minimum(jnp.maximum(entries, -bound), bound).astype(kind)


def setup_inputs(seed: int = 0) -> dict:
    seeds = jax.random.split(jax.random.key(seed), 13)
    tokens = bell_draw(seeds[0], (TOKENS, D), 1.0, 6.0, ((0, 8),))
    clip_starts = draw_clip_starts(jax.random.fold_in(seeds[12], 71), 0)
    cls_index = draw_cls_index(jax.random.fold_in(seeds[12], 71), 0)
    norm_gains = jnp.clip(1.0 + 0.1 * jax.random.normal(seeds[3], (2, D), jnp.float32), 0.5, 1.5).astype(jnp.bfloat16)
    shifts = bell_draw(seeds[4], (4, D), 0.5, 3.0)
    qkv_weight = bell_draw(seeds[5], (D, 3, D), (D // 2) ** -0.5, 0.3125, ((2, 4),))
    qv_bias = bell_draw(seeds[6], (2, D), 0.5, 3.0, ((1, 4),))
    out_weight = bell_draw(seeds[7], (D, D), (D // 8) ** -0.5, 0.625, ((0, 4),))
    fc1_weight = bell_draw(seeds[8], (D, FF), D ** -0.5, 0.21875, ((1, 4),))
    fc1_bias = bell_draw(seeds[9], (FF,), 0.5, 3.0, ((0, 4),))
    fc2_weight = bell_draw(seeds[10], (FF, D), (FF // 2) ** -0.5, 0.15625, ((0, 4),))
    cotangent = bell_draw(seeds[11], (TOKENS, D), 1.0, 6.0, ((0, 8),))
    return dict(tokens=tokens, clip_starts=clip_starts, cls_index=cls_index, norm_gains=norm_gains, shifts=shifts, qkv_weight=qkv_weight, qv_bias=qv_bias, out_weight=out_weight, fc1_weight=fc1_weight, fc1_bias=fc1_bias, fc2_weight=fc2_weight, cotangent=cotangent)


@jax.custom_vjp
def low(v):
    return lax.optimization_barrier(v.astype(jnp.bfloat16)).astype(jnp.float32)

@jax.custom_vjp
def low_back(v):
    return v

def low_keep(v):
    return (low(v), None)

def low_pass(kept, grad):
    return (grad,)

def back_keep(v):
    return (v, None)

def back_low(kept, grad):
    return (low(grad),)
low.defvjp(low_keep, low_pass)
low_back.defvjp(back_keep, back_low)

def normalize(values):
    centre = values - lax.optimization_barrier(jnp.mean(values, axis=-1, keepdims=True))
    return centre * lax.rsqrt(lax.optimization_barrier(jnp.mean(centre * centre, axis=-1, keepdims=True)) + 1e-06)

def visible(starts, marks):
    position = jnp.arange(LENGTH, dtype=jnp.int32)
    clip_of = lax.optimization_barrier(jnp.sum((position[:, None] >= starts[None, :]).astype(jnp.int32), axis=1)) - 1
    marked = jnp.any(position[:, None] == marks[None, :], axis=1)
    return (clip_of[:, None] == clip_of[None, :]) | marked[None, :]

def layer(inputs, starts, marks, params):
    gain_rows, offsets, qkv_matrix, qv_shift, out_matrix, up_matrix, up_shift, down_matrix = params
    highest = lax.Precision.HIGHEST
    normed_one = low(normalize(inputs) * gain_rows[0] + offsets[0])
    projected = jnp.einsum('td,dce->tce', normed_one, qkv_matrix, precision=highest)
    head_shape = (LENGTH, HEADS, HEAD_DIM)
    queries = low(low_back(projected[:, 0] + qv_shift[0])).reshape(head_shape)
    key_rows = low(low_back(projected[:, 1])).reshape(head_shape)
    value_rows = low(low_back(projected[:, 2] + qv_shift[1])).reshape(head_shape)
    scores = low_back(jnp.einsum('qhd,khd->hqk', queries, key_rows, precision=highest) * 0.125)
    scores = jnp.where(visible(starts, marks)[None], scores, -1e+30)
    row_max = lax.optimization_barrier(jnp.max(scores, axis=-1, keepdims=True))
    exponent = jnp.exp(scores - row_max)
    attn_prob = exponent / lax.optimization_barrier(jnp.sum(exponent, axis=-1, keepdims=True))
    context = jnp.einsum('hqk,khd->qhd', low(attn_prob), value_rows, precision=highest).reshape(LENGTH, D)
    context = low(low_back(context))
    group_width = D // N_TENSOR
    partial_value = jnp.einsum('tge,gef->gtf', context.reshape(LENGTH, N_TENSOR, group_width), out_matrix.reshape(N_TENSOR, group_width, D), precision=highest)
    mixed = inputs + low_back(lax.optimization_barrier(jnp.sum(low(partial_value), axis=0))) + offsets[2]
    normed_two = low(normalize(mixed) * gain_rows[1] + offsets[1])
    pre_act = low_back(jnp.dot(normed_two, up_matrix, precision=highest) + up_shift)
    activated = low(jax.nn.gelu(pre_act, approximate=False))
    hidden_width = FF // N_TENSOR
    pieces = jnp.einsum('tgh,ghf->gtf', activated.reshape(LENGTH, N_TENSOR, hidden_width), down_matrix.reshape(N_TENSOR, hidden_width, D), precision=highest)
    return mixed + lax.optimization_barrier(jnp.sum(low(pieces), axis=0)) + offsets[3]

def reference(tokens, clip_starts, cls_index, norm_gains, shifts, qkv_weight, qv_bias, out_weight, fc1_weight, fc1_bias, fc2_weight, cotangent):
    params = tuple((item.astype(jnp.float32) for item in (norm_gains, shifts, qkv_weight, qv_bias, out_weight, fc1_weight, fc1_bias, fc2_weight)))
    inputs = tokens.astype(jnp.float32).reshape(SEQS, LENGTH, D)
    checked = jax.checkpoint(layer)

    def forward(values, weights):

        def one_sequence(pieces):
            return checked(pieces[0], pieces[1], pieces[2], weights)
        return lax.map(one_sequence, (values, clip_starts, cls_index))
    outputs, pullback = jax.vjp(forward, inputs, params)
    grad_inputs, grad_params = pullback(cotangent.astype(jnp.float32).reshape(SEQS, LENGTH, D))
    layer_out = outputs.reshape(TOKENS, D).astype(jnp.bfloat16)
    input_grad = grad_inputs.reshape(TOKENS, D).astype(jnp.bfloat16)
    return (layer_out, input_grad, grad_params[0], grad_params[1], grad_params[2], grad_params[3], grad_params[4], grad_params[5], grad_params[6], grad_params[7])
```

```python
import functools

import jax
import jax.numpy as jnp
from jax import lax
from jax.experimental import pallas as pl
from jax.experimental.pallas import tpu as pltpu
from jax.sharding import PartitionSpec as P

HEAD = 64
EPS = 1e-06
F32 = jnp.float32
BF16 = jnp.bfloat16
VMEM_LIMIT = 40 * 1024 * 1024


def nn(a, b):
    return lax.dot_general(a, b, (((1,), (0,)), ((), ())), preferred_element_type=F32)


def nt(a, b):
    return lax.dot_general(a, b, (((1,), (1,)), ((), ())), preferred_element_type=F32)


def tn(a, b):
    return lax.dot_general(a, b, (((0,), (0,)), ((), ())), preferred_element_type=F32)


def normalize(x):
    centre = x - jnp.mean(x, axis=-1, keepdims=True)
    factor = lax.rsqrt(jnp.mean(centre * centre, axis=-1, keepdims=True) + EPS)
    return centre * factor, factor


def norm_back(grad, scaled, factor, gain):
    inner = grad * gain
    return factor * (
        inner
        - jnp.mean(inner, axis=-1, keepdims=True)
        - scaled * jnp.mean(inner * scaled, axis=-1, keepdims=True)
    )


def spec(shape, index_map):
    return pl.BlockSpec(shape, index_map)


def whole(shape):
    return pl.BlockSpec(shape, lambda *_: (0,) * len(shape))


def params(n=1):
    return pltpu.CompilerParams(
        dimension_semantics=("arbitrary",) * n, vmem_limit_bytes=VMEM_LIMIT
    )


def struct(shape, dtype):
    return jax.ShapeDtypeStruct(shape, dtype)


def front_kernel(
    seq, length, heads, c_ref, st_ref, mk_ref, tok_ref, gain_ref, shift_ref, w_ref, qvb_ref,
    ow_ref, h1_ref, qkv_ref, e_ref, ctxt_ref, linv_ref, keep_ref, send_ref,
    qf, kf, st_s, ct_s, ctx_s,
):
    step = pl.program_id(0)
    half = length // 2
    clips = st_ref.shape[1]

    @pl.when(step == 0)
    def _():
        gain = gain_ref[0:1, :].astype(F32)
        shift = shift_ref[0:1, :].astype(F32)
        rows = 128
        for r in range(0, length, rows):
            x = tok_ref[r : r + rows, :].astype(F32)
            scaled, _ = normalize(x)
            h1_ref[r : r + rows, :] = (scaled * gain + shift).astype(BF16)
        h1 = h1_ref[...]
        qvb = qvb_ref[...].astype(F32)
        q = (nn(h1, w_ref[0]) + qvb[0:1]).astype(BF16)
        qkv_ref[0] = (q.astype(F32) * 0.125).astype(BF16)
        qkv_ref[1] = nn(h1, w_ref[1]).astype(BF16)
        qkv_ref[2] = (nn(h1, w_ref[2]) + qvb[1:2]).astype(BF16)
        pos = lax.broadcasted_iota(jnp.int32, (length, HEAD), 0)
        lane = lax.broadcasted_iota(jnp.int32, (length, HEAD), 1)
        clip = jnp.zeros((length, HEAD), jnp.int32) - 1
        mark = jnp.zeros((length, HEAD), jnp.int32)
        for k in range(clips):
            clip = clip + jnp.where(pos >= st_ref[seq, k], 1, 0)
            mark = mark + jnp.where(pos == mk_ref[seq, k], 1, 0)
        qf[...] = jnp.where(lane == clip, 1.0, 0.0).astype(BF16)
        hide = (lane < clips) & (lane != clip) & (mark == 0)
        kf[...] = jnp.where(hide, -1e30, 0.0).astype(BF16)

    def head(h):
        lo = h * HEAD
        k_aug = jnp.concatenate([qkv_ref[1, :, lo : lo + HEAD], kf[...]], axis=1)
        q_aug = jnp.concatenate([qkv_ref[0, :, lo : lo + HEAD], qf[...]], axis=1)
        v = qkv_ref[2, :, lo : lo + HEAD]
        width = 256
        for i, t in enumerate(range(0, length, width)):
            w = min(width, length - t)
            slot = i % 2
            st_s[slot, :, :w] = nt(k_aug, q_aug[t : t + w])
            ch = 64
            m = None
            for u in range(0, length, ch):
                x = jnp.max(st_s[slot, u : u + ch, :w].reshape(ch // 8, 8, w), axis=0)
                m = x if m is None else jnp.maximum(m, x)
            m = jnp.max(m, axis=0, keepdims=True)
            tot = None
            for u in range(0, length, ch):
                x = jnp.exp(st_s[slot, u : u + ch, :w] - m)
                e_ref[0, u : u + ch, t : t + w] = x.astype(BF16)
                x = jnp.sum(x.reshape(ch // 8, 8, w), axis=0)
                tot = x if tot is None else tot + x
            inv = 1.0 / jnp.sum(tot, axis=0, keepdims=True)
            linv_ref[h : h + 1, t : t + w] = inv
            ct_s[lo : lo + HEAD, t : t + w] = tn(v, e_ref[0, :, t : t + w]) * inv

    for h in range(heads):
        pl.when(step == h)(functools.partial(head, h))

    @pl.when(step == heads - 1)
    def _():
        ctxt_ref[...] = ct_s[...].astype(BF16)
        ctx_s[...] = jnp.transpose(ct_s[...]).astype(BF16)
        c = c_ref[0]
        own = pl.multiple_of(c * half, half)
        other = pl.multiple_of((1 - c) * half, half)
        send_ref[...] = nn(ctx_s[pl.ds(other, half), :], ow_ref[...]).astype(BF16)
        keep_ref[...] = nn(ctx_s[pl.ds(own, half), :], ow_ref[...]).astype(BF16)


def front(seq, length, c, starts, marks, tokens, gains, shifts, w, qvb, ow):
    width = tokens.shape[1]
    local = w.shape[2]
    heads = local // HEAD
    half = length // 2
    smem = pl.BlockSpec(memory_space=pltpu.SMEM)
    return pl.pallas_call(
        functools.partial(front_kernel, seq, length, heads),
        grid_spec=pltpu.PrefetchScalarGridSpec(
            num_scalar_prefetch=1,
            grid=(heads,),
            in_specs=[
                smem,
                smem,
                spec((length, width), lambda i, *_: (seq, 0)),
                whole(gains.shape),
                whole(shifts.shape),
                whole(w.shape),
                whole(qvb.shape),
                whole(ow.shape),
            ],
            out_specs=[
                whole((length, width)),
                whole((3, length, local)),
                spec((1, length, length), lambda i, *_: (i, 0, 0)),
                whole((local, length)),
                whole((8, length)),
                whole((half, width)),
                whole((half, width)),
            ],
            scratch_shapes=[
                pltpu.VMEM((length, HEAD), BF16),
                pltpu.VMEM((length, HEAD), BF16),
                pltpu.VMEM((2, length, 256), F32),
                pltpu.VMEM((local, length), F32),
                pltpu.VMEM((length, local), BF16),
            ],
        ),
        out_shape=[
            struct((length, width), BF16),
            struct((3, length, local), BF16),
            struct((heads, length, length), BF16),
            struct((local, length), BF16),
            struct((8, length), F32),
            struct((half, width), BF16),
            struct((half, width), BF16),
        ],
        compiler_params=params(),
        name="attend",
        cost_estimate=pl.CostEstimate(flops=4 * 10**9, bytes_accessed=10 * 10**6, transcendentals=3 * 10**6),
    )(c, starts, marks, tokens, gains, shifts, w, qvb, ow)


def norm_two_kernel(c_ref, tok_ref, a_ref, b_ref, gain_ref, shift_ref, x1_ref, h2_ref):
    total = a_ref[...].astype(F32) + b_ref[...].astype(F32)
    x1 = tok_ref[...].astype(F32) + total + shift_ref[2:3, :].astype(F32)
    x1_ref[...] = x1
    scaled, _ = normalize(x1)
    h2_ref[...] = (scaled * gain_ref[1:2, :].astype(F32) + shift_ref[1:2, :].astype(F32)).astype(BF16)


BLOCK = 112


def norm_two(seq, c, tokens, a, b, gains, shifts):
    half, width = a.shape
    n = half // BLOCK
    row = spec((BLOCK, width), lambda i, *_: (i, 0))
    return pl.pallas_call(
        norm_two_kernel,
        grid_spec=pltpu.PrefetchScalarGridSpec(
            num_scalar_prefetch=1,
            grid=(n,),
            in_specs=[
                spec((BLOCK, width), lambda i, c: ((seq * 2 + c[0]) * n + i, 0)),
                row,
                row,
                whole(gains.shape),
                whole(shifts.shape),
            ],
            out_specs=[row, row],
        ),
        out_shape=[struct((half, width), F32), struct((half, width), BF16)],
        compiler_params=params(),
        name="norm_two",
    )(c, tokens, a, b, gains, shifts)


def mlp_kernel(
    aliased, c_ref, own_ref, recv_ref, cot_ref, fc1_ref, b1_ref, fc2_ref, *rest
):
    outs = rest[3 * aliased :]
    h2_ref, act_ref, dpre_ref, mk_ref, ms_ref, dk_ref, ds_ref, bias_ref = outs
    j, r = pl.program_id(0), pl.program_id(1)
    h2 = jnp.where(j == 0, own_ref[...], recv_ref[...])
    h2_ref[...] = h2
    pre = nn(h2, fc1_ref[...]) + b1_ref[...].astype(F32)
    phi = 0.5 * (1.0 + lax.erf(pre * 0.7071067811865476))
    act = (pre * phi).astype(BF16)
    act_ref[...] = act
    slope = phi + pre * (0.3989422804014327 * jnp.exp(-0.5 * pre * pre))
    dact = nt(cot_ref[...], fc2_ref[...])
    dpre32 = dact * slope
    dpre = dpre32.astype(BF16)
    dpre_ref[...] = dpre
    part = jnp.sum(dpre.astype(F32), axis=0, keepdims=True)

    @pl.when((j == 0) & (r == 0))
    def _():
        bias_ref[...] = jnp.zeros_like(bias_ref)

    bias_ref[0:1, :] += part
    dh2 = nt(dpre, fc1_ref[...]).astype(BF16)
    out = nn(act, fc2_ref[...]).astype(BF16)

    @pl.when(j == 0)
    def _():
        mk_ref[...] = out
        dk_ref[...] = dh2

    @pl.when(j == 1)
    def _():
        ms_ref[...] = out
        ds_ref[...] = dh2


def mlp(seq, c, own, recv, cot, fc1, b1, fc2, prev):
    half, width = own.shape
    rows = cot.shape[0]
    hidden = fc1.shape[1]
    n = 2
    block = half // n
    aliased = prev is not None
    half_in = spec((block, width), lambda j, r, *_: (r, 0))
    natural = lambda w: spec(
        (block, w), lambda j, r, c: ((seq * 2 + c[0] + j - 2 * c[0] * j) * n + r, 0)
    )
    keep = spec((block, width), lambda j, r, *_: (jnp.where(j == 0, r, n - 1), 0))
    send = spec((block, width), lambda j, r, *_: (jnp.where(j == 0, 0, r), 0))
    any_spec = pl.BlockSpec(memory_space=pl.ANY)
    shared = [struct((rows, width), BF16), struct((rows, hidden), BF16), struct((rows, hidden), BF16)]
    part = struct((half, width), BF16)
    return pl.pallas_call(
        functools.partial(mlp_kernel, int(aliased)),
        grid_spec=pltpu.PrefetchScalarGridSpec(
            num_scalar_prefetch=1,
            grid=(2, n),
            in_specs=[
                half_in,
                half_in,
                natural(width),
                whole(fc1.shape),
                whole(b1.shape),
                whole(fc2.shape),
            ]
            + [any_spec] * (3 * aliased),
            out_specs=[natural(width), natural(hidden), natural(hidden), keep, send, keep, send, whole((8, hidden))],
        ),
        out_shape=shared + [part] * 4 + [struct((8, hidden), F32)],
        input_output_aliases={7 + k: k for k in range(3 * aliased)},
        compiler_params=params(2),
        name="feed_forward",
        cost_estimate=pl.CostEstimate(flops=5 * 10**9, bytes_accessed=10 * 10**6, transcendentals=2 * 10**6),
    )(c, own, recv, cot, fc1, b1, fc2, *(prev if aliased else ()))


def mid_kernel(c_ref, cot_ref, x1_ref, a_ref, b_ref, gain_ref, dx_ref, dxr_ref, sums_ref):
    dh2 = a_ref[...].astype(F32) + b_ref[...].astype(F32)
    scaled, factor = normalize(x1_ref[...])
    dy = cot_ref[...].astype(F32)
    dx = dy + norm_back(dh2, scaled, factor, gain_ref[1:2, :].astype(F32))
    dx_ref[...] = dx
    dxr_ref[...] = dx.astype(BF16)

    @pl.when(pl.program_id(0) == 0)
    def _():
        sums_ref[...] = jnp.zeros_like(sums_ref)

    sums_ref[0:1, :] += jnp.sum(dh2 * scaled, axis=0, keepdims=True)
    sums_ref[1:2, :] += jnp.sum(dh2, axis=0, keepdims=True)
    sums_ref[2:3, :] += jnp.sum(dx, axis=0, keepdims=True)
    sums_ref[3:4, :] += jnp.sum(dy, axis=0, keepdims=True)


def mid(seq, c, cot, x1, a, b, gains):
    half, width = a.shape
    n = half // BLOCK
    row = spec((BLOCK, width), lambda i, *_: (i, 0))
    return pl.pallas_call(
        mid_kernel,
        grid_spec=pltpu.PrefetchScalarGridSpec(
            num_scalar_prefetch=1,
            grid=(n,),
            in_specs=[
                spec((BLOCK, width), lambda i, c: ((seq * 2 + c[0]) * n + i, 0)),
                row,
                row,
                row,
                whole(gains.shape),
            ],
            out_specs=[row, row, whole((8, width))],
        ),
        out_shape=[struct((half, width), F32), struct((half, width), BF16), struct((8, width), F32)],
        compiler_params=params(),
        name="mid_grad",
    )(c, cot, x1, a, b, gains)


def back_kernel(
    length, heads, first, c_ref, own_ref, recv_ref, h1_ref, qkv_ref, e_ref, ctxt_ref, linv_ref,
    w_ref, ow_ref, *rest,
):
    if first:
        grads_ref, keep_ref, send_ref, bias_ref = rest[:4]
        prev_ref = None
        scratch = rest[4:]
    else:
        prev_ref, grads_ref, keep_ref, send_ref, bias_ref = rest[:5]
        scratch = rest[5:]
    dx_s, dct_s, dcx_s, da_s, ds_s, dqt_s, dq_s, dk_s, dv_s = scratch
    step = pl.program_id(0)
    half = length // 2
    local = heads * HEAD
    c = c_ref[0]
    own = pl.multiple_of(c * half, half)
    other = pl.multiple_of((1 - c) * half, half)

    @pl.when(step == 0)
    def _():
        dx_s[pl.ds(own, half), :] = own_ref[...]
        dx_s[pl.ds(other, half), :] = recv_ref[...]
        dct = nt(ow_ref[...], dx_s[...]).astype(BF16).astype(F32)
        for h in range(heads):
            lo = h * HEAD
            inv = linv_ref[h : h + 1, :]
            part = dct[lo : lo + HEAD]
            delta = jnp.sum(part * ctxt_ref[lo : lo + HEAD, :].astype(F32), axis=0, keepdims=True) * inv
            high = delta.astype(BF16).astype(F32)
            low = delta - high
            dct_s[lo : lo + HEAD, :] = part * inv
            row = lax.broadcasted_iota(jnp.int32, (HEAD, length), 0)
            feat = jnp.where(row == 0, -high, jnp.where(row == 1, -low, 0.0))
            da_s[h, :HEAD, :] = (part * inv).astype(BF16)
            da_s[h, HEAD:, :] = feat.astype(BF16)
        dcx_s[...] = jnp.transpose(dct_s[...]).astype(BF16)

    def head(h):
        lo = h * HEAD
        lane = lax.broadcasted_iota(jnp.int32, (length, HEAD), 1)
        ones = jnp.where(lane < 2, 1.0, 0.0).astype(BF16)
        v_aug = jnp.concatenate([qkv_ref[2, :, lo : lo + HEAD], ones], axis=1)
        q = qkv_ref[0, :, lo : lo + HEAD]
        k = qkv_ref[1, :, lo : lo + HEAD]
        width = 256
        for t in range(0, length, width):
            w = min(width, length - t)
            dp = nn(v_aug, da_s[h, :, t : t + w])
            ds = (e_ref[0, :, t : t + w].astype(F32) * dp).astype(BF16)
            ds_s[:, t : t + w] = ds
            dqt_s[lo : lo + HEAD, t : t + w] = tn(k, ds) * 0.125
        dv_s[h] = nn(e_ref[0], dcx_s[:, lo : lo + HEAD]).astype(BF16)
        dk_s[h] = nn(ds_s[...], q).astype(BF16)

    for h in range(heads):
        pl.when(step == h)(functools.partial(head, h))

    @pl.when(step == heads - 1)
    def _():
        dq_s[0] = jnp.transpose(dqt_s[...]).astype(BF16)
        dq_s[1] = jnp.concatenate([dk_s[h] for h in range(heads)], axis=1)
        dq_s[2] = jnp.concatenate([dv_s[h] for h in range(heads)], axis=1)
        for dst, ref in ((other, send_ref), (own, keep_ref)):
            rows = pl.ds(dst, half)
            ref[...] = (
                nt(dq_s[0, rows, :], w_ref[0]) + nt(dq_s[1, rows, :], w_ref[1]) + nt(dq_s[2, rows, :], w_ref[2])
            ).astype(BF16)
        bias_ref[...] = jnp.zeros_like(bias_ref)
        bias_ref[0:1, :] = jnp.sum(dq_s[0].astype(F32), axis=0, keepdims=True)
        bias_ref[1:2, :] = jnp.sum(dq_s[2].astype(F32), axis=0, keepdims=True)
        h1 = h1_ref[...]
        parts = [tn(dq_s[i], h1) for i in range(3)]
        parts.append(nn(ctxt_ref[...], dx_s[...]))
        for i, p in enumerate(parts):
            if prev_ref is not None:
                p = p + prev_ref[i * local : (i + 1) * local, :]
            grads_ref[i * local : (i + 1) * local, :] = p.astype(grads_ref.dtype)


def back(length, c, own, recv, h1, qkv, e, ctxt, linv, w, ow, prev):
    half, width = own.shape
    local = w.shape[2]
    heads = local // HEAD
    first = prev is None
    gshape = (4 * local, width)
    return pl.pallas_call(
        functools.partial(back_kernel, length, heads, first),
        grid_spec=pltpu.PrefetchScalarGridSpec(
            num_scalar_prefetch=1,
            grid=(heads,),
            in_specs=[
                whole((half, width)),
                whole((half, width)),
                whole(h1.shape),
                whole(qkv.shape),
                spec((1, length, length), lambda i, *_: (i, 0, 0)),
                whole(ctxt.shape),
                whole(linv.shape),
                whole(w.shape),
                whole(ow.shape),
            ]
            + ([] if first else [whole(gshape)]),
            out_specs=[
                whole(gshape),
                whole((half, width)),
                whole((half, width)),
                whole((8, local)),
            ],
            scratch_shapes=[
                pltpu.VMEM((length, width), BF16),
                pltpu.VMEM((local, length), F32),
                pltpu.VMEM((length, local), BF16),
                pltpu.VMEM((heads, 2 * HEAD, length), BF16),
                pltpu.VMEM((length, length), BF16),
                pltpu.VMEM((local, length), F32),
                pltpu.VMEM((3, length, local), BF16),
                pltpu.VMEM((heads, length, HEAD), BF16),
                pltpu.VMEM((heads, length, HEAD), BF16),
            ],
        ),
        out_shape=[
            struct(gshape, F32 if first else BF16),
            struct((half, width), BF16),
            struct((half, width), BF16),
            struct((8, local), F32),
        ],
        compiler_params=params(),
        name="attend_back",
        cost_estimate=pl.CostEstimate(flops=6 * 10**9, bytes_accessed=12 * 10**6, transcendentals=0),
    )(c, own, recv, h1, qkv, e, ctxt, linv, w, ow, *(() if first else (prev,)))


def last_kernel(c_ref, tok_ref, dx_ref, a_ref, b_ref, gain_ref, out_ref, sums_ref):
    dh1 = a_ref[...].astype(F32) + b_ref[...].astype(F32)
    scaled, factor = normalize(tok_ref[...].astype(F32))
    grad = dx_ref[...] + norm_back(dh1, scaled, factor, gain_ref[0:1, :].astype(F32))
    out_ref[...] = grad.astype(BF16)

    @pl.when(pl.program_id(0) == 0)
    def _():
        sums_ref[...] = jnp.zeros_like(sums_ref)

    sums_ref[0:1, :] += jnp.sum(dh1 * scaled, axis=0, keepdims=True)
    sums_ref[1:2, :] += jnp.sum(dh1, axis=0, keepdims=True)


def last(seq, c, tokens, dx, a, b, gains):
    half, width = a.shape
    n = half // BLOCK
    row = spec((BLOCK, width), lambda i, *_: (i, 0))
    return pl.pallas_call(
        last_kernel,
        grid_spec=pltpu.PrefetchScalarGridSpec(
            num_scalar_prefetch=1,
            grid=(n,),
            in_specs=[
                spec((BLOCK, width), lambda i, c: ((seq * 2 + c[0]) * n + i, 0)),
                row,
                row,
                row,
                whole(gains.shape),
            ],
            out_specs=[row, whole((8, width))],
        ),
        out_shape=[struct((half, width), BF16), struct((8, width), F32)],
        compiler_params=params(),
        name="input_grad",
    )(c, tokens, dx, a, b, gains)


def swap(x, axis, bit, size):
    return lax.ppermute(x, axis, [(i, i ^ bit) for i in range(size)])


def add_low(a, b):
    return (a.astype(F32) + b.astype(F32)).astype(BF16)


def bits_of(size):
    out, bit = [], 1
    while bit < size:
        out.append(bit)
        bit *= 2
    return out


def reduce_over(buf, axis, size):
    me = lax.axis_index(axis)
    cur = buf
    for bit in bits_of(size):
        rows = cur.shape[0] // 2
        mine = (me // bit) % 2
        give = lax.dynamic_slice_in_dim(cur, (1 - mine) * rows, rows, 0)
        keep = lax.dynamic_slice_in_dim(cur, mine * rows, rows, 0)
        cur = add_low(keep, swap(give, axis, bit, size))
    for bit in reversed(bits_of(size)):
        mine = (me // bit) % 2
        got = swap(cur, axis, bit, size)
        cur = jnp.where(mine == 0, jnp.concatenate([cur, got]), jnp.concatenate([got, cur]))
    return cur


def shards(
    n_dp, n_tensor, tokens, clip_starts, cls_index, norm_gains, shifts, qkv_weight, qv_bias,
    out_weight, fc1_weight, fc1_bias, fc2_weight, cotangent,
):
    seqs = clip_starts.shape[0]
    length = tokens.shape[0] // seqs
    half = length // 2
    width = tokens.shape[1]
    core = lax.axis_index("tensor") % 2
    c = core.reshape(1).astype(jnp.int32)
    swap_core = lambda x: swap(x, "tensor", 1, n_tensor)

    def over_chips(x):
        total = None
        for k in range(1, n_tensor // 2):
            got = lax.ppermute(x, "tensor", [(i, (i + 2 * k) % n_tensor) for i in range(n_tensor)])
            total = got if total is None else add_low(total, got)
        return total

    w = jnp.transpose(qkv_weight, (1, 0, 2))
    b1 = fc1_bias.reshape(1, -1)

    fronts, sums_a = [], []
    for s in range(seqs):
        f = front(s, length, c, clip_starts, cls_index, tokens, norm_gains, shifts, w, qv_bias, out_weight)
        h1, qkv, e, ctxt, linv, keep, send = f
        fronts.append((h1, qkv, e, ctxt, linv))
        mine = add_low(keep, swap_core(send))
        sums_a.append((mine, over_chips(mine)))

    prev = None
    x1s, mlps, dh2s, bias1 = [], [], [], []
    for s in range(seqs):
        x1, h2 = norm_two(s, c, tokens, *sums_a[s], norm_gains, shifts)
        got = swap_core(h2)
        res = mlp(s, c, h2, got, cotangent, fc1_weight, b1, fc2_weight, prev)
        prev = tuple(res[:3])
        mk, ms, dk, ds, bias = res[3:]
        x1s.append(x1)
        bias1.append(bias)
        mine = add_low(dk, swap_core(ds))
        dh2s.append((mine, over_chips(mine)))
        mlps.append(add_low(mk, swap_core(ms)))
    h2_all, act_all, dpre_all = prev

    fc2_grad = reduce_over(tn(act_all, cotangent).astype(BF16), "dp", n_dp)
    fc1_grad = reduce_over(tn(h2_all, dpre_all).astype(BF16), "dp", n_dp)

    prev = None
    mids, dh1s, qvs = [], [], []
    for s in range(seqs):
        dx, dxr, sums = mid(s, c, cotangent, x1s[s], *dh2s[s], norm_gains)
        got = swap_core(dxr)
        prev, keep, send, qv = back(length, c, dxr, got, *fronts[s], w, out_weight, prev)
        mids.append((dx, sums))
        qvs.append(qv)
        mine = add_low(keep, swap_core(send))
        dh1s.append((mine, over_chips(mine)))
    attn_grad = reduce_over(prev, "dp", n_dp)

    out_halves = []
    for s in range(seqs):
        other = over_chips(mlps[s])
        total = mlps[s].astype(F32) + other.astype(F32)
        out_halves.append((x1s[s] + total + shifts[3].astype(F32)).astype(BF16))

    grad_halves, lasts = [], []
    for s in range(seqs):
        g, sums = last(s, c, tokens, mids[s][0], *dh1s[s], norm_gains)
        grad_halves.append(g)
        lasts.append(sums)

    def joined(halves):
        rows = []
        for own in halves:
            got = swap_core(own)
            rows.append(jnp.where(core == 0, own, got))
            rows.append(jnp.where(core == 0, got, own))
        return jnp.concatenate(rows, axis=0)

    layer_out = joined(out_halves)
    input_grad = joined(grad_halves)

    s_mid = sum(m[1] for m in mids)
    s_last = sum(lasts)
    local = qv_bias.shape[1]
    qv = sum(qvs)[:2]
    qv_row = jnp.pad(qv.reshape(1, 2 * local), ((0, 0), (0, width - 2 * local)))
    hidden = b1.shape[1]
    bias_row = sum(bias1)[0:1]
    small = jnp.concatenate([s_last[0:1], s_mid[0:1], s_last[1:2], s_mid[1:4], bias_row, qv_row], axis=0)
    for bit in bits_of(n_dp):
        small = small + swap(small, "dp", bit, n_dp)
    both = small[:6] + swap_core(small[:6])

    grads = attn_grad.astype(F32).reshape(4, local, width)
    return (
        layer_out,
        input_grad,
        both[:2],
        both[2:6],
        jnp.transpose(grads[:3], (2, 0, 1)),
        small[7, : 2 * local].reshape(2, local),
        grads[3],
        fc1_grad.astype(F32),
        small[6, :hidden],
        fc2_grad.astype(F32),
    )


def solution(mesh):
    row = P("dp", None)
    return jax.shard_map(
        functools.partial(shards, mesh.shape["dp"], mesh.shape["tensor"]),
        mesh=mesh,
        in_specs=(
            row,
            row,
            row,
            P(),
            P(),
            P(None, None, "tensor"),
            P(None, "tensor"),
            P("tensor", None),
            P(None, "tensor"),
            P("tensor"),
            P("tensor", None),
            row,
        ),
        out_specs=(
            row,
            row,
            P(),
            P(),
            P(None, None, "tensor"),
            P(None, "tensor"),
            P("tensor", None),
            P(None, "tensor"),
            P("tensor"),
            P("tensor", None),
        ),
        check_vma=False,
    )
```

```python
import functools

import jax
import jax.numpy as jnp
from jax import lax
from jax.experimental import pallas as pl
from jax.experimental.pallas import tpu as pltpu
from jax.sharding import PartitionSpec as P

HEAD = 64
EPS = 1e-06
F32 = jnp.float32
BF16 = jnp.bfloat16
VMEM_LIMIT = 40 * 1024 * 1024


def nn(a, b):
    return lax.dot_general(a, b, (((1,), (0,)), ((), ())), preferred_element_type=F32)


def nt(a, b):
    return lax.dot_general(a, b, (((1,), (1,)), ((), ())), preferred_element_type=F32)


def tn(a, b):
    return lax.dot_general(a, b, (((0,), (0,)), ((), ())), preferred_element_type=F32)


def normalize(x):
    centre = x - jnp.mean(x, axis=-1, keepdims=True)
    factor = lax.rsqrt(jnp.mean(centre * centre, axis=-1, keepdims=True) + EPS)
    return centre * factor, factor


def norm_back(grad, scaled, factor, gain):
    inner = grad * gain
    return factor * (
        inner
        - jnp.mean(inner, axis=-1, keepdims=True)
        - scaled * jnp.mean(inner * scaled, axis=-1, keepdims=True)
    )


def spec(shape, index_map):
    return pl.BlockSpec(shape, index_map)


def whole(shape):
    return pl.BlockSpec(shape, lambda *_: (0,) * len(shape))


def params(n=1):
    return pltpu.CompilerParams(
        dimension_semantics=("arbitrary",) * n, vmem_limit_bytes=VMEM_LIMIT
    )


def struct(shape, dtype):
    return jax.ShapeDtypeStruct(shape, dtype)


BLOCK = 112
MESH = pl.DeviceIdType.MESH


def loop(n, body):
    lax.fori_loop(0, n, lambda i, carry: (body(i), carry)[1], 0)


def rows_at(i, size):
    return pl.ds(pl.multiple_of(i * size, size), size)


class Pair:
    def __init__(self, send, mine, from_core, from_chip, sems, core, chip):
        self.send, self.mine, self.from_core, self.from_chip = send, mine, from_core, from_chip
        self.to_core = pltpu.make_async_remote_copy(
            src_ref=send, dst_ref=from_core, send_sem=sems.at[0], recv_sem=sems.at[1],
            device_id={"tensor": core}, device_id_type=MESH,
        )
        self.to_chip = pltpu.make_async_remote_copy(
            src_ref=mine, dst_ref=from_chip, send_sem=sems.at[2], recv_sem=sems.at[3],
            device_id={"tensor": chip}, device_id_type=MESH,
        )

    def start(self):
        self.to_core.start()

    def middle(self):
        self.to_core.wait()

        def body(i):
            r = rows_at(i, BLOCK)
            self.mine[r, :] = (self.mine[r, :].astype(F32) + self.from_core[r, :].astype(F32)).astype(BF16)

        loop(self.mine.shape[0] // BLOCK, body)
        self.to_chip.start()

    def finish(self):
        self.to_chip.wait()

    def total(self, r):
        return self.mine[r, :].astype(F32) + self.from_chip[r, :].astype(F32)


def front_kernel(
    seqs, length, heads, st_ref, mk_ref, tok_h, gain_ref, shift_ref, w_ref, qvb_ref, ow_ref,
    h1_ref, qa, ka, va, e_h, ctxt_ref, linv_ref, x1_ref, h2_ref,
    tok, st_s, ct_s, ctx_s, es, send, mine, fcore, fchip, load_sem, e_sem, pair_sem, h2_sem,
):
    half = length // 2
    clips = st_ref.shape[1]
    t = lax.axis_index("tensor")
    c = t % 2
    core = t + 1 - 2 * c
    chip = (t + 2) % 4
    own = pl.multiple_of(c * half, half)
    other = pl.multiple_of((1 - c) * half, half)
    loads = [
        pltpu.make_async_copy(tok_h.at[pl.ds(s * length, length)], tok.at[pl.ds(s * length, length)], load_sem.at[s])
        for s in range(seqs)
    ]
    for x in loads:
        x.start()
    barrier = pltpu.get_barrier_semaphore()
    for peer in (core, chip):
        pl.semaphore_signal(barrier, inc=1, device_id={"tensor": peer}, device_id_type=MESH)
    pl.semaphore_wait(barrier, 2)
    pairs = [
        Pair(send.at[s], mine.at[s], fcore.at[s], fchip.at[s], pair_sem.at[s], core, chip) for s in range(seqs)
    ]

    def spill(j, slot):
        return pltpu.make_async_copy(es.at[slot], e_h.at[j], e_sem.at[slot])

    def project(s):
        gain = gain_ref[0:1, :].astype(F32)
        shift = shift_ref[0:1, :].astype(F32)
        qvb = qvb_ref[...].astype(F32)
        size = 128

        def body(i):
            r = rows_at(i, size)
            x = tok[pl.ds(pl.multiple_of(s * length + i * size, size), size), :].astype(F32)
            scaled, _ = normalize(x)
            h1 = (scaled * gain + shift).astype(BF16)
            h1_ref[s, r, :] = h1
            q = (nn(h1, w_ref[0]) + qvb[0:1]).astype(BF16).astype(F32) * 0.125
            q = q.astype(BF16)
            k = nn(h1, w_ref[1]).astype(BF16)
            v = (nn(h1, w_ref[2]) + qvb[1:2]).astype(BF16)
            pos = lax.broadcasted_iota(jnp.int32, (size, HEAD), 0) + i * size
            lane = lax.broadcasted_iota(jnp.int32, (size, HEAD), 1)
            clip = jnp.zeros((size, HEAD), jnp.int32) - 1
            mark = jnp.zeros((size, HEAD), jnp.int32)
            for n in range(clips):
                clip = clip + jnp.where(pos >= st_ref[s, n], 1, 0)
                mark = mark + jnp.where(pos == mk_ref[s, n], 1, 0)
            qf = jnp.where(lane == clip, 1.0, 0.0).astype(BF16)
            hide = (lane < clips) & (lane != clip) & (mark == 0)
            kf = jnp.where(hide, -1e30, 0.0).astype(BF16)
            vf = jnp.where(lane < 2, 1.0, 0.0).astype(BF16)
            for h in range(heads):
                cols = slice(h * HEAD, h * HEAD + HEAD)
                qa[s, h, r, :] = jnp.concatenate([q[:, cols], qf], axis=1)
                ka[s, h, r, :] = jnp.concatenate([k[:, cols], kf], axis=1)
                va[s, h, r, :] = jnp.concatenate([v[:, cols], vf], axis=1)

        loop(length // size, body)

    def attend(s):
        def head(h):
            j = s * heads + h
            slot = lax.rem(j, 2)

            @pl.when(j >= 2)
            def _():
                spill(j, slot).wait()

            v = va[s, h, :, :HEAD]
            width = 256
            for i, t0 in enumerate(range(0, length, width)):
                w = min(width, length - t0)
                sl = i % 2
                st_s[sl, :, :w] = nt(ka[s, h], qa[s, h, t0 : t0 + w])
                ch = 64
                m = None
                for u in range(0, length, ch):
                    x = jnp.max(st_s[sl, u : u + ch, :w].reshape(ch // 8, 8, w), axis=0)
                    m = x if m is None else jnp.maximum(m, x)
                m = jnp.max(m, axis=0, keepdims=True)
                tot = None
                for u in range(0, length, ch):
                    x = jnp.exp(st_s[sl, u : u + ch, :w] - m)
                    es[slot, u : u + ch, t0 : t0 + w] = x.astype(BF16)
                    x = jnp.sum(x.reshape(ch // 8, 8, w), axis=0)
                    tot = x if tot is None else tot + x
                inv = 1.0 / jnp.sum(tot, axis=0, keepdims=True)
                linv_ref[s, h, :, t0 : t0 + w] = jnp.broadcast_to(inv, (8, w))
                ct_s[rows_at(h, HEAD), t0 : t0 + w] = tn(v, es[slot, :, t0 : t0 + w]) * inv
            spill(j, slot).start()

        loop(heads, head)
        ctxt_ref[s] = ct_s[...].astype(BF16)
        ctx_s[...] = jnp.transpose(ct_s[...]).astype(BF16)
        send[s] = nn(ctx_s[pl.ds(other, half), :], ow_ref[...]).astype(BF16)
        pairs[s].start()
        mine[s] = nn(ctx_s[pl.ds(own, half), :], ow_ref[...]).astype(BF16)

    h2_copies = []

    def norm_two(s):
        pairs[s].finish()
        g = gain_ref[1:2, :].astype(F32)
        b1 = shift_ref[1:2, :].astype(F32)
        b2 = shift_ref[2:3, :].astype(F32)

        def body(i):
            r = rows_at(i, BLOCK)
            rr = pl.ds(pl.multiple_of(own + i * BLOCK, 16), BLOCK)
            x = tok[pl.ds(pl.multiple_of(s * length + own + i * BLOCK, 16), BLOCK), :].astype(F32)
            x1 = x + pairs[s].total(r) + b2
            x1_ref[s, r, :] = x1
            scaled, _ = normalize(x1)
            h2_ref[s, rr, :] = (scaled * g + b1).astype(BF16)

        loop(half // BLOCK, body)
        cp = pltpu.make_async_remote_copy(
            src_ref=h2_ref.at[s, pl.ds(own, half)], dst_ref=h2_ref.at[s, pl.ds(own, half)],
            send_sem=h2_sem.at[s, 0], recv_sem=h2_sem.at[s, 1],
            device_id={"tensor": core}, device_id_type=MESH,
        )
        cp.start()
        h2_copies.append(cp)

    for s in range(seqs):
        loads[s].wait()
        project(s)
        if s > 0:
            pairs[s - 1].middle()
        attend(s)
    pairs[seqs - 1].middle()
    for s in range(seqs):
        norm_two(s)
    for k in (seqs * heads - 2, seqs * heads - 1):
        spill(k, k % 2).wait()
    for cp in h2_copies:
        cp.wait()


def front(seqs, length, starts, marks, tokens, gains, shifts, w, qvb, ow):
    width = tokens.shape[1]
    local = w.shape[2]
    heads = local // HEAD
    half = length // 2
    smem = pl.BlockSpec(memory_space=pltpu.SMEM)
    vmem = pl.BlockSpec(memory_space=pltpu.VMEM)
    hbm = pl.BlockSpec(memory_space=pl.ANY)
    return pl.pallas_call(
        functools.partial(front_kernel, seqs, length, heads),
        in_specs=[smem, smem, hbm, vmem, vmem, vmem, vmem, vmem],
        out_specs=[vmem, vmem, vmem, vmem, hbm, vmem, vmem, vmem, vmem],
        scratch_shapes=[
            pltpu.VMEM((seqs * length, width), BF16),
            pltpu.VMEM((2, length, 256), F32),
            pltpu.VMEM((local, length), F32),
            pltpu.VMEM((length, local), BF16),
            pltpu.VMEM((2, length, length), BF16),
        ]
        + [pltpu.VMEM((seqs, half, width), BF16)] * 4
        + [
            pltpu.SemaphoreType.DMA((seqs,)),
            pltpu.SemaphoreType.DMA((2,)),
            pltpu.SemaphoreType.DMA((seqs, 4)),
            pltpu.SemaphoreType.DMA((seqs, 2)),
        ],
        out_shape=[
            struct((seqs, length, width), BF16),
            struct((seqs, heads, length, 2 * HEAD), BF16),
            struct((seqs, heads, length, 2 * HEAD), BF16),
            struct((seqs, heads, length, 2 * HEAD), BF16),
            struct((seqs * heads, length, length), BF16),
            struct((seqs, local, length), BF16),
            struct((seqs, heads, 8, length), F32),
            struct((seqs, half, width), F32),
            struct((seqs, length, width), BF16),
        ],
        compiler_params=pltpu.CompilerParams(
            collective_id=1, has_side_effects=True, vmem_limit_bytes=56 * 1024 * 1024
        ),
        name="attend",
        cost_estimate=pl.CostEstimate(flops=8 * 10**9, bytes_accessed=20 * 10**6, transcendentals=6 * 10**6),
    )(starts, marks, tokens, gains, shifts, w, qvb, ow)


def mlp_kernel(
    aliased, c_ref, own_ref, recv_ref, cot_ref, fc1_ref, b1_ref, fc2_ref, *rest
):
    outs = rest[3 * aliased :]
    h2_ref, act_ref, dpre_ref, mk_ref, ms_ref, dk_ref, ds_ref, bias_ref = outs
    j, r = pl.program_id(0), pl.program_id(1)
    h2 = jnp.where(j == 0, own_ref[...], recv_ref[...])
    h2_ref[...] = h2
    pre = nn(h2, fc1_ref[...]) + b1_ref[...].astype(F32)
    phi = 0.5 * (1.0 + lax.erf(pre * 0.7071067811865476))
    act = (pre * phi).astype(BF16)
    act_ref[...] = act
    slope = phi + pre * (0.3989422804014327 * jnp.exp(-0.5 * pre * pre))
    dact = nt(cot_ref[...], fc2_ref[...])
    dpre32 = dact * slope
    dpre = dpre32.astype(BF16)
    dpre_ref[...] = dpre
    part = jnp.sum(dpre.astype(F32), axis=0, keepdims=True)

    @pl.when((j == 0) & (r == 0))
    def _():
        bias_ref[...] = jnp.zeros_like(bias_ref)

    bias_ref[0:1, :] += part
    dh2 = nt(dpre, fc1_ref[...]).astype(BF16)
    out = nn(act, fc2_ref[...]).astype(BF16)

    @pl.when(j == 0)
    def _():
        mk_ref[...] = out
        dk_ref[...] = dh2

    @pl.when(j == 1)
    def _():
        ms_ref[...] = out
        ds_ref[...] = dh2


def mlp(seq, c, own, recv, cot, fc1, b1, fc2, prev):
    half, width = own.shape
    rows = cot.shape[0]
    hidden = fc1.shape[1]
    n = 2
    block = half // n
    aliased = prev is not None
    half_in = spec((block, width), lambda j, r, *_: (r, 0))
    natural = lambda w: spec(
        (block, w), lambda j, r, c: ((seq * 2 + c[0] + j - 2 * c[0] * j) * n + r, 0)
    )
    keep = spec((block, width), lambda j, r, *_: (jnp.where(j == 0, r, n - 1), 0))
    send = spec((block, width), lambda j, r, *_: (jnp.where(j == 0, 0, r), 0))
    any_spec = pl.BlockSpec(memory_space=pl.ANY)
    shared = [struct((rows, width), BF16), struct((rows, hidden), BF16), struct((rows, hidden), BF16)]
    part = struct((half, width), BF16)
    return pl.pallas_call(
        functools.partial(mlp_kernel, int(aliased)),
        grid_spec=pltpu.PrefetchScalarGridSpec(
            num_scalar_prefetch=1,
            grid=(2, n),
            in_specs=[
                half_in,
                half_in,
                natural(width),
                whole(fc1.shape),
                whole(b1.shape),
                whole(fc2.shape),
            ]
            + [any_spec] * (3 * aliased),
            out_specs=[natural(width), natural(hidden), natural(hidden), keep, send, keep, send, whole((8, hidden))],
        ),
        out_shape=shared + [part] * 4 + [struct((8, hidden), F32)],
        input_output_aliases={7 + k: k for k in range(3 * aliased)},
        compiler_params=params(2),
        name="feed_forward",
        cost_estimate=pl.CostEstimate(flops=5 * 10**9, bytes_accessed=10 * 10**6, transcendentals=2 * 10**6),
    )(c, own, recv, cot, fc1, b1, fc2, *(prev if aliased else ()))


def mid_kernel(c_ref, cot_ref, x1_ref, a_ref, b_ref, gain_ref, dx_ref, dxr_ref, sums_ref):
    dh2 = a_ref[...].astype(F32) + b_ref[...].astype(F32)
    scaled, factor = normalize(x1_ref[...])
    dy = cot_ref[...].astype(F32)
    dx = dy + norm_back(dh2, scaled, factor, gain_ref[1:2, :].astype(F32))
    dx_ref[...] = dx
    dxr_ref[...] = dx.astype(BF16)

    @pl.when(pl.program_id(0) == 0)
    def _():
        sums_ref[...] = jnp.zeros_like(sums_ref)

    sums_ref[0:1, :] += jnp.sum(dh2 * scaled, axis=0, keepdims=True)
    sums_ref[1:2, :] += jnp.sum(dh2, axis=0, keepdims=True)
    sums_ref[2:3, :] += jnp.sum(dx, axis=0, keepdims=True)
    sums_ref[3:4, :] += jnp.sum(dy, axis=0, keepdims=True)


def mid(seq, c, cot, x1, a, b, gains):
    half, width = a.shape
    n = half // BLOCK
    row = spec((BLOCK, width), lambda i, *_: (i, 0))
    return pl.pallas_call(
        mid_kernel,
        grid_spec=pltpu.PrefetchScalarGridSpec(
            num_scalar_prefetch=1,
            grid=(n,),
            in_specs=[
                spec((BLOCK, width), lambda i, c: ((seq * 2 + c[0]) * n + i, 0)),
                row,
                row,
                row,
                whole(gains.shape),
            ],
            out_specs=[row, row, whole((8, width))],
        ),
        out_shape=[struct((half, width), F32), struct((half, width), BF16), struct((8, width), F32)],
        compiler_params=params(),
        name="mid_grad",
    )(c, cot, x1, a, b, gains)


def back_kernel(
    length, heads, first, c_ref, own_ref, recv_ref, h1_ref, qkv_ref, e_ref, ctxt_ref, linv_ref,
    w_ref, ow_ref, *rest,
):
    if first:
        grads_ref, keep_ref, send_ref, bias_ref = rest[:4]
        prev_ref = None
        scratch = rest[4:]
    else:
        prev_ref, grads_ref, keep_ref, send_ref, bias_ref = rest[:5]
        scratch = rest[5:]
    dx_s, dct_s, dcx_s, da_s, ds_s, dqt_s, dq_s, dk_s, dv_s = scratch
    step = pl.program_id(0)
    half = length // 2
    local = heads * HEAD
    c = c_ref[0]
    own = pl.multiple_of(c * half, half)
    other = pl.multiple_of((1 - c) * half, half)

    @pl.when(step == 0)
    def _():
        dx_s[pl.ds(own, half), :] = own_ref[...]
        dx_s[pl.ds(other, half), :] = recv_ref[...]
        dct = nt(ow_ref[...], dx_s[...]).astype(BF16).astype(F32)
        for h in range(heads):
            lo = h * HEAD
            inv = linv_ref[h : h + 1, :]
            part = dct[lo : lo + HEAD]
            delta = jnp.sum(part * ctxt_ref[lo : lo + HEAD, :].astype(F32), axis=0, keepdims=True) * inv
            high = delta.astype(BF16).astype(F32)
            low = delta - high
            dct_s[lo : lo + HEAD, :] = part * inv
            row = lax.broadcasted_iota(jnp.int32, (HEAD, length), 0)
            feat = jnp.where(row == 0, -high, jnp.where(row == 1, -low, 0.0))
            da_s[h, :HEAD, :] = (part * inv).astype(BF16)
            da_s[h, HEAD:, :] = feat.astype(BF16)
        dcx_s[...] = jnp.transpose(dct_s[...]).astype(BF16)

    def head(h):
        lo = h * HEAD
        lane = lax.broadcasted_iota(jnp.int32, (length, HEAD), 1)
        ones = jnp.where(lane < 2, 1.0, 0.0).astype(BF16)
        v_aug = jnp.concatenate([qkv_ref[2, :, lo : lo + HEAD], ones], axis=1)
        q = qkv_ref[0, :, lo : lo + HEAD]
        k = qkv_ref[1, :, lo : lo + HEAD]
        width = 256
        for t in range(0, length, width):
            w = min(width, length - t)
            dp = nn(v_aug, da_s[h, :, t : t + w])
            ds = (e_ref[0, :, t : t + w].astype(F32) * dp).astype(BF16)
            ds_s[:, t : t + w] = ds
            dqt_s[lo : lo + HEAD, t : t + w] = tn(k, ds) * 0.125
        dv_s[h] = nn(e_ref[0], dcx_s[:, lo : lo + HEAD]).astype(BF16)
        dk_s[h] = nn(ds_s[...], q).astype(BF16)

    for h in range(heads):
        pl.when(step == h)(functools.partial(head, h))

    @pl.when(step == heads - 1)
    def _():
        dq_s[0] = jnp.transpose(dqt_s[...]).astype(BF16)
        dq_s[1] = jnp.concatenate([dk_s[h] for h in range(heads)], axis=1)
        dq_s[2] = jnp.concatenate([dv_s[h] for h in range(heads)], axis=1)
        for dst, ref in ((other, send_ref), (own, keep_ref)):
            rows = pl.ds(dst, half)
            ref[...] = (
                nt(dq_s[0, rows, :], w_ref[0]) + nt(dq_s[1, rows, :], w_ref[1]) + nt(dq_s[2, rows, :], w_ref[2])
            ).astype(BF16)
        bias_ref[...] = jnp.zeros_like(bias_ref)
        bias_ref[0:1, :] = jnp.sum(dq_s[0].astype(F32), axis=0, keepdims=True)
        bias_ref[1:2, :] = jnp.sum(dq_s[2].astype(F32), axis=0, keepdims=True)
        h1 = h1_ref[...]
        parts = [tn(dq_s[i], h1) for i in range(3)]
        parts.append(nn(ctxt_ref[...], dx_s[...]))
        for i, p in enumerate(parts):
            if prev_ref is not None:
                p = p + prev_ref[i * local : (i + 1) * local, :]
            grads_ref[i * local : (i + 1) * local, :] = p.astype(grads_ref.dtype)


def back(length, c, own, recv, h1, qkv, e, ctxt, linv, w, ow, prev):
    half, width = own.shape
    local = w.shape[2]
    heads = local // HEAD
    first = prev is None
    gshape = (4 * local, width)
    return pl.pallas_call(
        functools.partial(back_kernel, length, heads, first),
        grid_spec=pltpu.PrefetchScalarGridSpec(
            num_scalar_prefetch=1,
            grid=(heads,),
            in_specs=[
                whole((half, width)),
                whole((half, width)),
                whole(h1.shape),
                whole(qkv.shape),
                spec((1, length, length), lambda i, *_: (i, 0, 0)),
                whole(ctxt.shape),
                whole(linv.shape),
                whole(w.shape),
                whole(ow.shape),
            ]
            + ([] if first else [whole(gshape)]),
            out_specs=[
                whole(gshape),
                whole((half, width)),
                whole((half, width)),
                whole((8, local)),
            ],
            scratch_shapes=[
                pltpu.VMEM((length, width), BF16),
                pltpu.VMEM((local, length), F32),
                pltpu.VMEM((length, local), BF16),
                pltpu.VMEM((heads, 2 * HEAD, length), BF16),
                pltpu.VMEM((length, length), BF16),
                pltpu.VMEM((local, length), F32),
                pltpu.VMEM((3, length, local), BF16),
                pltpu.VMEM((heads, length, HEAD), BF16),
                pltpu.VMEM((heads, length, HEAD), BF16),
            ],
        ),
        out_shape=[
            struct(gshape, F32 if first else BF16),
            struct((half, width), BF16),
            struct((half, width), BF16),
            struct((8, local), F32),
        ],
        compiler_params=params(),
        name="attend_back",
        cost_estimate=pl.CostEstimate(flops=6 * 10**9, bytes_accessed=12 * 10**6, transcendentals=0),
    )(c, own, recv, h1, qkv, e, ctxt, linv, w, ow, *(() if first else (prev,)))


def last_kernel(c_ref, tok_ref, dx_ref, a_ref, b_ref, gain_ref, out_ref, sums_ref):
    dh1 = a_ref[...].astype(F32) + b_ref[...].astype(F32)
    scaled, factor = normalize(tok_ref[...].astype(F32))
    grad = dx_ref[...] + norm_back(dh1, scaled, factor, gain_ref[0:1, :].astype(F32))
    out_ref[...] = grad.astype(BF16)

    @pl.when(pl.program_id(0) == 0)
    def _():
        sums_ref[...] = jnp.zeros_like(sums_ref)

    sums_ref[0:1, :] += jnp.sum(dh1 * scaled, axis=0, keepdims=True)
    sums_ref[1:2, :] += jnp.sum(dh1, axis=0, keepdims=True)


def last(seq, c, tokens, dx, a, b, gains):
    half, width = a.shape
    n = half // BLOCK
    row = spec((BLOCK, width), lambda i, *_: (i, 0))
    return pl.pallas_call(
        last_kernel,
        grid_spec=pltpu.PrefetchScalarGridSpec(
            num_scalar_prefetch=1,
            grid=(n,),
            in_specs=[
                spec((BLOCK, width), lambda i, c: ((seq * 2 + c[0]) * n + i, 0)),
                row,
                row,
                row,
                whole(gains.shape),
            ],
            out_specs=[row, whole((8, width))],
        ),
        out_shape=[struct((half, width), BF16), struct((8, width), F32)],
        compiler_params=params(),
        name="input_grad",
    )(c, tokens, dx, a, b, gains)


def swap(x, axis, bit, size):
    return lax.ppermute(x, axis, [(i, i ^ bit) for i in range(size)])


def add_low(a, b):
    return (a.astype(F32) + b.astype(F32)).astype(BF16)


def bits_of(size):
    out, bit = [], 1
    while bit < size:
        out.append(bit)
        bit *= 2
    return out


def reduce_over(buf, axis, size):
    me = lax.axis_index(axis)
    cur = buf
    for bit in bits_of(size):
        rows = cur.shape[0] // 2
        mine = (me // bit) % 2
        give = lax.dynamic_slice_in_dim(cur, (1 - mine) * rows, rows, 0)
        keep = lax.dynamic_slice_in_dim(cur, mine * rows, rows, 0)
        cur = add_low(keep, swap(give, axis, bit, size))
    for bit in reversed(bits_of(size)):
        mine = (me // bit) % 2
        got = swap(cur, axis, bit, size)
        cur = jnp.where(mine == 0, jnp.concatenate([cur, got]), jnp.concatenate([got, cur]))
    return cur


def shards(
    n_dp, n_tensor, tokens, clip_starts, cls_index, norm_gains, shifts, qkv_weight, qv_bias,
    out_weight, fc1_weight, fc1_bias, fc2_weight, cotangent,
):
    seqs = clip_starts.shape[0]
    length = tokens.shape[0] // seqs
    half = length // 2
    width = tokens.shape[1]
    core = lax.axis_index("tensor") % 2
    c = core.reshape(1).astype(jnp.int32)
    swap_core = lambda x: swap(x, "tensor", 1, n_tensor)

    def over_chips(x):
        total = None
        for k in range(1, n_tensor // 2):
            got = lax.ppermute(x, "tensor", [(i, (i + 2 * k) % n_tensor) for i in range(n_tensor)])
            total = got if total is None else add_low(total, got)
        return total

    w = jnp.transpose(qkv_weight, (1, 0, 2))
    b1 = fc1_bias.reshape(1, -1)

    h1s, qa, ka, va, es, ctxts, linvs, x1all, h2all = front(
        seqs, length, clip_starts, cls_index, tokens, norm_gains, shifts, w, qv_bias, out_weight
    )
    heads = qa.shape[1]
    join = lambda a, s: jnp.concatenate([a[s, h, :, :HEAD] for h in range(heads)], axis=1)
    fronts = [
        (
            h1s[s],
            jnp.stack([join(qa, s), join(ka, s), join(va, s)]),
            es[s * heads : (s + 1) * heads],
            ctxts[s],
            jnp.pad(linvs[s, :, 0], ((0, 8 - heads), (0, 0))),
        )
        for s in range(seqs)
    ]

    prev = None
    x1s, mlps, dh2s, bias1 = [], [], [], []
    for s in range(seqs):
        x1 = x1all[s]
        h2 = lax.dynamic_slice_in_dim(h2all[s], core * half, half, 0)
        got = lax.dynamic_slice_in_dim(h2all[s], (1 - core) * half, half, 0)
        res = mlp(s, c, h2, got, cotangent, fc1_weight, b1, fc2_weight, prev)
        prev = tuple(res[:3])
        mk, ms, dk, ds, bias = res[3:]
        x1s.append(x1)
        bias1.append(bias)
        mine = add_low(dk, swap_core(ds))
        dh2s.append((mine, over_chips(mine)))
        mlps.append(add_low(mk, swap_core(ms)))
    h2_all, act_all, dpre_all = prev

    fc2_grad = reduce_over(tn(act_all, cotangent).astype(BF16), "dp", n_dp)
    fc1_grad = reduce_over(tn(h2_all, dpre_all).astype(BF16), "dp", n_dp)

    prev = None
    mids, dh1s, qvs = [], [], []
    for s in range(seqs):
        dx, dxr, sums = mid(s, c, cotangent, x1s[s], *dh2s[s], norm_gains)
        got = swap_core(dxr)
        prev, keep, send, qv = back(length, c, dxr, got, *fronts[s], w, out_weight, prev)
        mids.append((dx, sums))
        qvs.append(qv)
        mine = add_low(keep, swap_core(send))
        dh1s.append((mine, over_chips(mine)))
    attn_grad = reduce_over(prev, "dp", n_dp)

    out_halves = []
    for s in range(seqs):
        other = over_chips(mlps[s])
        total = mlps[s].astype(F32) + other.astype(F32)
        out_halves.append((x1s[s] + total + shifts[3].astype(F32)).astype(BF16))

    grad_halves, lasts = [], []
    for s in range(seqs):
        g, sums = last(s, c, tokens, mids[s][0], *dh1s[s], norm_gains)
        grad_halves.append(g)
        lasts.append(sums)

    def joined(halves):
        rows = []
        for own in halves:
            got = swap_core(own)
            rows.append(jnp.where(core == 0, own, got))
            rows.append(jnp.where(core == 0, got, own))
        return jnp.concatenate(rows, axis=0)

    layer_out = joined(out_halves)
    input_grad = joined(grad_halves)

    s_mid = sum(m[1] for m in mids)
    s_last = sum(lasts)
    local = qv_bias.shape[1]
    qv = sum(qvs)[:2]
    qv_row = jnp.pad(qv.reshape(1, 2 * local), ((0, 0), (0, width - 2 * local)))
    hidden = b1.shape[1]
    bias_row = sum(bias1)[0:1]
    small = jnp.concatenate([s_last[0:1], s_mid[0:1], s_last[1:2], s_mid[1:4], bias_row, qv_row], axis=0)
    for bit in bits_of(n_dp):
        small = small + swap(small, "dp", bit, n_dp)
    both = small[:6] + swap_core(small[:6])

    grads = attn_grad.astype(F32).reshape(4, local, width)
    return (
        layer_out,
        input_grad,
        both[:2],
        both[2:6],
        jnp.transpose(grads[:3], (2, 0, 1)),
        small[7, : 2 * local].reshape(2, local),
        grads[3],
        fc1_grad.astype(F32),
        small[6, :hidden],
        fc2_grad.astype(F32),
    )


def solution(mesh):
    row = P("dp", None)
    return jax.shard_map(
        functools.partial(shards, mesh.shape["dp"], mesh.shape["tensor"]),
        mesh=mesh,
        in_specs=(
            row,
            row,
            row,
            P(),
            P(),
            P(None, None, "tensor"),
            P(None, "tensor"),
            P("tensor", None),
            P(None, "tensor"),
            P("tensor"),
            P("tensor", None),
            row,
        ),
        out_specs=(
            row,
            row,
            P(),
            P(),
            P(None, None, "tensor"),
            P(None, "tensor"),
            P("tensor", None),
            P(None, "tensor"),
            P("tensor"),
            P("tensor", None),
        ),
        check_vma=False,
    )
```

```python
import functools

import jax
import jax.numpy as jnp
from jax import lax
from jax.experimental import pallas as pl
from jax.experimental.pallas import tpu as pltpu
from jax.sharding import PartitionSpec as P

HEAD = 64
EPS = 1e-06
F32 = jnp.float32
BF16 = jnp.bfloat16
BLOCK = 112
CHUNKS = 2
MESH = pl.DeviceIdType.MESH


def nn(a, b):
    return lax.dot_general(a, b, (((1,), (0,)), ((), ())), preferred_element_type=F32)


def nt(a, b):
    return lax.dot_general(a, b, (((1,), (1,)), ((), ())), preferred_element_type=F32)


def tn(a, b):
    return lax.dot_general(a, b, (((0,), (0,)), ((), ())), preferred_element_type=F32)


def normalize(x):
    centre = x - jnp.mean(x, axis=-1, keepdims=True)
    factor = lax.rsqrt(jnp.mean(centre * centre, axis=-1, keepdims=True) + EPS)
    return centre * factor, factor


def norm_back(grad, scaled, factor, gain):
    inner = grad * gain
    return factor * (
        inner
        - jnp.mean(inner, axis=-1, keepdims=True)
        - scaled * jnp.mean(inner * scaled, axis=-1, keepdims=True)
    )


def column_sum(x):
    return jnp.sum(x, axis=0, keepdims=True)


def loop(n, body):
    lax.fori_loop(0, n, lambda i, carry: (body(i), carry)[1], 0)


def rows_at(i, size, base=0):
    return pl.ds(pl.multiple_of(base + i * size, 16), size)


def remote(src, dst, send_sem, recv_sem, axis, index):
    return pltpu.make_async_remote_copy(
        src_ref=src, dst_ref=dst, send_sem=send_sem, recv_sem=recv_sem,
        device_id={axis: index}, device_id_type=MESH,
    )


class Pair:
    def __init__(self, send, mine, from_core, from_chip, sems, core, chip):
        self.send, self.mine, self.from_core, self.from_chip = send, mine, from_core, from_chip
        self.to_core = remote(send, from_core, sems.at[0], sems.at[1], "tensor", core)
        self.to_chip = remote(mine, from_chip, sems.at[2], sems.at[3], "tensor", chip)

    def start(self):
        self.to_core.start()

    def gather(self):
        self.to_core.wait()

        def body(i):
            r = rows_at(i, BLOCK)
            self.mine[r, :] = (self.mine[r, :].astype(F32) + self.from_core[r, :].astype(F32)).astype(BF16)

        loop(self.mine.shape[0] // BLOCK, body)

    def middle(self):
        self.gather()
        self.to_chip.start()

    def finish(self):
        self.to_chip.wait()

    def total(self, r):
        return self.mine[r, :].astype(F32) + self.from_chip[r, :].astype(F32)


def layer_kernel(
    seqs, length, heads, n_dp, group, extra,
    st_ref, mk_ref, gain_ref, shift_ref, qvb_ref, b1_ref, tok_h, cot_h, w_h, ow_h, fc1_h, fc2_h,
    out_h, grad_h, gmat_h, small_ref, e_h,
    tok, cot, w_ref, ow_ref, fc1, fc2, h1_ref, qa, ka, va, es, st_s, ct_s, ctxt_ref, linv_ref,
    send, mine, fcore, fchip, x1_ref, dx_ref, h2_ref, dxs, dxr_mine, dxr_other, ds_s, da_s, dcx_s, dq_s,
    dk_s, dv_s, gbuf, rx, rz, re, sv, svr,
    load_sem, e_sem, pair_sem, h2_sem, dx_sem, red_sem, out_sem, small_sem,
):
    half = length // 2
    width = tok.shape[1]
    hidden = fc1.shape[1]
    local = heads * HEAD
    clips = st_ref.shape[1]
    t = lax.axis_index("tensor")
    dp = lax.axis_index("dp")
    c = t % 2
    core = t + 1 - 2 * c
    chip = (t + 2) % 4
    own = pl.multiple_of(c * half, half)
    other = pl.multiple_of((1 - c) * half, half)
    xi = dp % 2
    xpeer = dp + 1 - 2 * xi
    zi = (dp // 2) % group
    zpeers = [dp + 2 * ((zi + k) % group - zi) for k in range(1, group)]
    ebits = [2 * group * 2**k for k in range(extra)]
    epeers = [dp + bit - 2 * bit * ((dp // bit) % 2) for bit in ebits]

    def load(k, src, dst):
        cp = pltpu.make_async_copy(src, dst, load_sem.at[k])
        cp.start()
        return cp

    tok_rows = [pl.ds(s * length, length) for s in range(seqs)]
    load_tok0 = load(0, tok_h.at[tok_rows[0]], tok.at[tok_rows[0]])
    load_w = load(1, w_h, w_ref)
    load_tok1 = load(2, tok_h.at[pl.ds(length, (seqs - 1) * length)], tok.at[pl.ds(length, (seqs - 1) * length)])
    load_ow = load(3, ow_h, ow_ref)
    load_fc1 = load(4, fc1_h, fc1)
    load_cot = load(5, cot_h, cot)
    load_fc2 = load(6, fc2_h, fc2)

    barrier = pltpu.get_barrier_semaphore()
    for peer in (core, chip):
        pl.semaphore_signal(barrier, inc=1, device_id={"tensor": peer}, device_id_type=MESH)
    for peer in [xpeer] + zpeers + epeers:
        pl.semaphore_signal(barrier, inc=1, device_id={"dp": peer}, device_id_type=MESH)
    pl.semaphore_wait(barrier, 3 + len(zpeers) + len(epeers))

    def pair(b, q):
        return Pair(send.at[b], mine.at[q], fcore.at[b], fchip.at[q], pair_sem.at[q], core, chip)

    pair_a = [pair(s, s) for s in range(seqs)]
    pair_d = [pair(seqs + s, seqs + s) for s in range(seqs)]
    pair_m = [pair(2 * seqs, 2 * seqs + s) for s in range(seqs)]
    pair_g = [
        Pair(send.at[s], mine.at[s], fcore.at[s], fchip.at[s], pair_sem.at[3 * seqs + s], core, chip)
        for s in range(seqs)
    ]

    sv[...] = jnp.zeros_like(sv)

    def add_sum(row, value):
        sv[row : row + 1, : value.shape[1]] += value

    def spill(j, slot):
        return pltpu.make_async_copy(es.at[slot], e_h.at[j], e_sem.at[slot])

    def fetch(j, slot):
        return pltpu.make_async_copy(e_h.at[j], es.at[slot], e_sem.at[2 + slot])

    def project(s):
        gain = gain_ref[0:1, :].astype(F32)
        shift = shift_ref[0:1, :].astype(F32)
        qvb = qvb_ref[...].astype(F32)
        size = 128

        def body(i):
            r = rows_at(i, size)
            x = tok[rows_at(i, size, s * length), :].astype(F32)
            scaled, _ = normalize(x)
            h1 = (scaled * gain + shift).astype(BF16)
            h1_ref[s, r, :] = h1
            q = (nn(h1, w_ref[0]) + qvb[0:1]).astype(BF16).astype(F32) * 0.125
            q = q.astype(BF16)
            k = nn(h1, w_ref[1]).astype(BF16)
            v = (nn(h1, w_ref[2]) + qvb[1:2]).astype(BF16)
            pos = lax.broadcasted_iota(jnp.int32, (size, HEAD), 0) + i * size
            lane = lax.broadcasted_iota(jnp.int32, (size, HEAD), 1)
            clip = jnp.zeros((size, HEAD), jnp.int32) - 1
            mark = jnp.zeros((size, HEAD), jnp.int32)
            for n in range(clips):
                clip = clip + jnp.where(pos >= st_ref[s, n], 1, 0)
                mark = mark + jnp.where(pos == mk_ref[s, n], 1, 0)
            qf = jnp.where(lane == clip, 1.0, 0.0).astype(BF16)
            hide = (lane < clips) & (lane != clip) & (mark == 0)
            kf = jnp.where(hide, -1e30, 0.0).astype(BF16)
            vf = jnp.where(lane < 2, 1.0, 0.0).astype(BF16)
            for h in range(heads):
                cols = slice(h * HEAD, h * HEAD + HEAD)
                qa[s, h, r, :] = jnp.concatenate([q[:, cols], qf], axis=1)
                ka[s, h, r, :] = jnp.concatenate([k[:, cols], kf], axis=1)
                va[s, h, r, :] = jnp.concatenate([v[:, cols], vf], axis=1)

        loop(length // size, body)

    spans = [(t0, min(256, length - t0)) for t0 in range(0, length, 256)]

    def attend(s):
        def head(h):
            j = s * heads + h
            slot = lax.rem(j, 2)

            @pl.when(j >= 2)
            def _():
                spill(j, slot).wait()

            v = va[s, h, :, :HEAD]
            for i, (t0, n) in enumerate(spans):
                sl = i % 2
                st_s[sl, :, :n] = nt(ka[s, h], qa[s, h, t0 : t0 + n])
                ch = 64
                m = None
                for u in range(0, length, ch):
                    x = jnp.max(st_s[sl, u : u + ch, :n].reshape(ch // 8, 8, n), axis=0)
                    m = x if m is None else jnp.maximum(m, x)
                m = jnp.max(m, axis=0, keepdims=True)
                tot = None
                for u in range(0, length, ch):
                    x = jnp.exp(st_s[sl, u : u + ch, :n] - m)
                    es[slot, u : u + ch, t0 : t0 + n] = x.astype(BF16)
                    x = jnp.sum(x.reshape(ch // 8, 8, n), axis=0)
                    tot = x if tot is None else tot + x
                inv = 1.0 / jnp.sum(tot, axis=0, keepdims=True)
                linv_ref[s, h, :, t0 : t0 + n] = jnp.broadcast_to(inv, (8, n))
                ct_s[rows_at(h, HEAD), t0 : t0 + n] = tn(v, es[slot, :, t0 : t0 + n]) * inv
            spill(j, slot).start()

        loop(heads, head)
        ctxt_ref[s] = ct_s[...].astype(BF16)
        dq_s[0] = jnp.transpose(ct_s[...]).astype(BF16)

        def rows_out(dst, base):
            def body(i):
                dst[rows_at(i, BLOCK), :] = nn(dq_s[0, rows_at(i, BLOCK, base), :], ow_ref[...]).astype(BF16)

            loop(half // BLOCK, body)

        rows_out(send.at[s], other)
        pair_a[s].start()
        rows_out(mine.at[s], own)

    h2_copies = [
        remote(
            h2_ref.at[s, pl.ds(own, half)], h2_ref.at[s, pl.ds(own, half)], h2_sem.at[s, 0], h2_sem.at[s, 1],
            "tensor", core,
        )
        for s in range(seqs)
    ]

    def norm_two(s):
        pair_a[s].finish()
        g = gain_ref[1:2, :].astype(F32)
        b1 = shift_ref[1:2, :].astype(F32)
        b2 = shift_ref[2:3, :].astype(F32)

        def body(i):
            r = rows_at(i, BLOCK)
            x = tok[rows_at(i, BLOCK, s * length + own), :].astype(F32)
            x1 = x + pair_a[s].total(r) + b2
            x1_ref[s, r, :] = x1
            scaled, _ = normalize(x1)
            h2_ref[s, rows_at(i, BLOCK, own), :] = (scaled * g + b1).astype(BF16)

        loop(half // BLOCK, body)
        h2_copies[s].start()

    act_ref, dpre_ref = ds_s, dxs

    def feed_forward(s, base, mlp_dst, dh2_dst):
        size = BLOCK

        def body(i):
            r = rows_at(i, size, base)
            pre = nn(h2_ref[s, r, :], fc1[...]) + b1_ref[...].astype(F32)
            phi = 0.5 * (1.0 + lax.erf(pre * 0.7071067811865476))
            act = (pre * phi).astype(BF16)
            act_ref[r, :hidden] = act
            slope = phi + pre * (0.3989422804014327 * jnp.exp(-0.5 * pre * pre))
            dact = nt(cot[rows_at(i, size, s * length + base), :], fc2[...])
            dpre = (dact * slope).astype(BF16)
            dpre_ref[r, :hidden] = dpre
            add_sum(6, column_sum(dpre.astype(F32)))
            dh2_dst[rows_at(i, size), :] = nt(dpre, fc1[...]).astype(BF16)
            mlp_dst[rows_at(i, size), :] = nn(act, fc2[...]).astype(BF16)

        loop(half // size, body)

    def fc_grad(m, left, right, s, tile):
        def body(i):
            r = pl.ds(pl.multiple_of(i * tile, tile), tile)
            p = tn(left(r), right())
            if s > 0:
                p = p + gbuf[m, r, :].astype(F32)
            gbuf[m, r, :] = p.astype(BF16)

        loop(width // tile, body)

    def fc2_grad(s):
        fc_grad(0, lambda r: act_ref[:, r], lambda: cot[tok_rows[s], :], s, 256)

    def fc1_grad(s):
        fc_grad(1, lambda r: h2_ref[s, :, r], lambda: dpre_ref[:, :hidden], s, 256)

    piece = gbuf.shape[1] // CHUNKS // 2 // group

    def reduce_job(m, ch):
        job = m * CHUNKS + ch
        base = ch * (gbuf.shape[1] // CHUNKS)
        part = group * piece
        sem = iter(range(red_sem.shape[1]))
        two = lambda: (red_sem.at[job, next(sem)], red_sem.at[job, next(sem)])
        rows = lambda start, n: gbuf.at[m, pl.ds(pl.multiple_of(start, 16), n)]

        def add(start, n, sources):
            size = piece

            def body(i):
                r = rows_at(i, size, start)
                total = gbuf[m, r, :].astype(F32)
                for src in sources:
                    total = total + src[rows_at(i, size), :].astype(F32)
                gbuf[m, r, :] = total.astype(BF16)

            loop(n // size, body)

        mine_at = base + xi * part
        cp = remote(rows(base + (1 - xi) * part, part), rx.at[job], *two(), "dp", xpeer)
        cp.start()
        yield
        cp.wait()
        add(mine_at, part, [rx.at[job]])
        cps = [
            remote(rows(mine_at + ((zi + k + 1) % group) * piece, piece), rz.at[job, k], *two(), "dp", p)
            for k, p in enumerate(zpeers)
        ]
        for cp in cps:
            cp.start()
        yield
        for cp in cps:
            cp.wait()
        piece_at = mine_at + zi * piece
        add(piece_at, piece, [rz.at[job, k] for k in range(group - 1)])
        for k, p in enumerate(epeers):
            cp = remote(rows(piece_at, piece), re.at[job, k], *two(), "dp", p)
            cp.start()
            yield
            cp.wait()
            add(piece_at, piece, [re.at[job, k]])
        done = lambda start, n: gmat_h.at[m, pl.ds(pl.multiple_of(start, 16), n)]
        cps = [remote(rows(piece_at, piece), done(piece_at, piece), *two(), "dp", p) for p in zpeers]
        cps.append(pltpu.make_async_copy(rows(piece_at, piece), done(piece_at, piece), red_sem.at[job, next(sem)]))
        for cp in cps:
            cp.start()
        yield
        for cp in cps:
            cp.wait()
        cp = remote(done(mine_at, part), done(mine_at, part), *two(), "dp", xpeer)
        cp.start()
        yield
        cp.wait()

    def advance(*jobs):
        for job in jobs:
            next(job, None)

    def drain(*jobs):
        live = list(jobs)
        while live:
            live = [job for job in live if next(job, live) is not live]

    dx_copies = [
        remote(dxr_mine.at[s], dxr_other.at[s], dx_sem.at[s, 0], dx_sem.at[s, 1], "tensor", core)
        for s in range(seqs)
    ]

    def mid(s):
        pair_d[s].finish()
        g = gain_ref[1:2, :].astype(F32)

        def body(i):
            r = rows_at(i, BLOCK)
            dh2 = pair_d[s].total(r)
            scaled, factor = normalize(x1_ref[s, r, :])
            dy = cot[rows_at(i, BLOCK, s * length + own), :].astype(F32)
            dx = dy + norm_back(dh2, scaled, factor, g)
            dx_ref[s, r, :] = dx
            dxr_mine[s, r, :] = dx.astype(BF16)
            add_sum(1, column_sum(dh2 * scaled))
            add_sum(3, column_sum(dh2))
            add_sum(4, column_sum(dx))
            add_sum(5, column_sum(dy))

        loop(half // BLOCK, body)
        dx_copies[s].start()

    def back_setup(s):
        dxs[pl.ds(own, half), :] = dxr_mine[s]
        dx_copies[s].wait()
        dxs[pl.ds(other, half), :] = dxr_other[s]
        ct_s[...] = nt(ow_ref[...], dxs[...])
        for h in range(heads):
            lo = h * HEAD
            inv = linv_ref[s, h, 0:1, :]
            part = ct_s[lo : lo + HEAD, :].astype(BF16).astype(F32)
            delta = column_sum(part * ctxt_ref[s, lo : lo + HEAD, :].astype(F32)) * inv
            high = delta.astype(BF16).astype(F32)
            low = delta - high
            row = lax.broadcasted_iota(jnp.int32, (HEAD, length), 0)
            feat = jnp.where(row == 0, -high, jnp.where(row == 1, -low, 0.0))
            part = part * inv
            da_s[h, :HEAD, :] = part.astype(BF16)
            da_s[h, HEAD:, :] = feat.astype(BF16)
            dcx_s[h] = jnp.transpose(part).astype(BF16)

    def back_head(s, h):
        j = s * heads + h
        slot = j % 2
        fetch(j, slot).wait()
        for t0, n in spans:
            dp_t = nn(va[s, h], da_s[h, :, t0 : t0 + n])
            ds = (es[slot, :, t0 : t0 + n].astype(F32) * dp_t).astype(BF16)
            ds_s[:, t0 : t0 + n] = ds
            ct_s[rows_at(h, HEAD), t0 : t0 + n] = tn(ka[s, h, :, :HEAD], ds) * 0.125
        dv_s[h] = nn(es[slot], dcx_s[h]).astype(BF16)
        dk_s[h] = nn(ds_s[...], qa[s, h, :, :HEAD]).astype(BF16)
        if j + 2 < seqs * heads:
            fetch(j + 2, slot).start()

    def back_end(s):
        dq_s[0] = jnp.transpose(ct_s[...]).astype(BF16)
        dq_s[1] = jnp.concatenate([dk_s[h] for h in range(heads)], axis=1)
        dq_s[2] = jnp.concatenate([dv_s[h] for h in range(heads)], axis=1)

        def rows_out(dst, base):
            def body(i):
                r = rows_at(i, BLOCK, base)
                p = nt(dq_s[0, r, :], w_ref[0]) + nt(dq_s[1, r, :], w_ref[1]) + nt(dq_s[2, r, :], w_ref[2])
                dst[rows_at(i, BLOCK), :] = p.astype(BF16)

            loop(half // BLOCK, body)

        rows_out(send.at[s], other)
        pair_g[s].start()
        rows_out(mine.at[s], own)

    def back_grads(s):
        for i in (2, 3, 0, 1):
            p = tn(dq_s[i], h1_ref[s]) if i < 3 else nn(ctxt_ref[s], dxs[...])
            r = slice(i * local, (i + 1) * local)
            if s > 0:
                p = p + gbuf[2, r, :].astype(F32)
            gbuf[2, r, :] = p.astype(BF16)
        add_sum(7, column_sum(dq_s[0].astype(F32)))
        sv[8:9, :local] += column_sum(dq_s[2].astype(F32))

    def place(k, stage, dst_h, s):
        rows = pl.ds(pl.multiple_of(s * length + own, 16), half)
        here = pltpu.make_async_copy(stage, dst_h.at[rows], out_sem.at[k, 0])
        there = remote(stage, dst_h.at[rows], out_sem.at[k, 1], out_sem.at[k, 2], "tensor", core)
        here.start()
        there.start()
        return here, there

    def layer_out(s):
        pair_m[s].finish()
        b3 = shift_ref[3:4, :].astype(F32)
        stage = send.at[2 * seqs]

        def body(i):
            r = rows_at(i, BLOCK)
            stage[r, :] = (x1_ref[s, r, :] + pair_m[s].total(r) + b3).astype(BF16)

        loop(half // BLOCK, body)
        return place(s, stage, out_h, s)

    def input_grad(s):
        pair_g[s].finish()
        g = gain_ref[0:1, :].astype(F32)
        stage = send.at[s]

        def body(i):
            r = rows_at(i, BLOCK)
            dh1 = pair_g[s].total(r)
            scaled, factor = normalize(tok[rows_at(i, BLOCK, s * length + own), :].astype(F32))
            stage[r, :] = (dx_ref[s, r, :] + norm_back(dh1, scaled, factor, g)).astype(BF16)
            add_sum(0, column_sum(dh1 * scaled))
            add_sum(2, column_sum(dh1))

        loop(half // BLOCK, body)
        return place(seqs + s, stage, grad_h, s)

    def small_job():
        sem = iter(range(small_sem.shape[0]))
        two = lambda: (small_sem.at[next(sem)], small_sem.at[next(sem)])
        slot = iter(range(svr.shape[0]))
        k = next(slot)
        cp = remote(sv.at[pl.ds(0, 6)], svr.at[k, pl.ds(0, 6)], *two(), "tensor", core)
        cp.start()
        yield
        cp.wait()
        sv[0:6, :] += svr[k, 0:6, :]
        for p in [xpeer]:
            k = next(slot)
            cp = remote(sv, svr.at[k], *two(), "dp", p)
            cp.start()
            yield
            cp.wait()
            sv[...] += svr[k]
        base = k + 1
        cps = []
        for i, p in enumerate(zpeers):
            cps.append(remote(sv, svr.at[base + zi], *two(), "dp", p))
        for cp in cps:
            cp.start()
        svr[base + zi] = sv[...]
        yield
        for cp in cps:
            cp.wait()
        total = svr[base]
        for i in range(1, group):
            total = total + svr[base + i]
        sv[...] = total
        for i, p in enumerate(epeers):
            k = base + group + i
            cp = remote(sv, svr.at[k], *two(), "dp", p)
            cp.start()
            yield
            cp.wait()
            sv[...] += svr[k]
        small_ref[...] = sv[...]

    load_tok0.wait()
    load_w.wait()
    project(0)
    load_ow.wait()
    attend(0)
    load_tok1.wait()
    for s in range(1, seqs):
        project(s)
        pair_a[s - 1].middle()
        attend(s)
    load_fc1.wait()
    load_cot.wait()
    load_fc2.wait()
    pair_a[seqs - 1].middle()
    for k in (seqs * heads - 2, seqs * heads - 1):
        spill(k, k % 2).wait()
    for k in (0, 1):
        fetch(k, k % 2).start()
    jobs = []
    for s in range(seqs):
        norm_two(s)
        feed_forward(s, own, mine.at[2 * seqs + s], mine.at[seqs + s])
        h2_copies[s].wait()
        feed_forward(s, other, send.at[2 * seqs], send.at[seqs + s])
        pair_d[s].start()
        pair_m[s].start()
        fc2_grad(s)
        pair_d[s].middle()
        if s == seqs - 1:
            jobs += [reduce_job(0, ch) for ch in range(CHUNKS)]
            advance(*jobs)
        pair_m[s].gather()
        fc1_grad(s)
    jobs += [reduce_job(1, ch) for ch in range(CHUNKS)]
    advance(*jobs)
    for s in range(seqs):
        mid(s)
        pair_m[s].to_chip.start()
        back_setup(s)
        for h in range(heads):
            back_head(s, h)
            advance(*jobs)
        back_end(s)
        back_grads(s)
        pair_g[s].middle()
    jobs += [reduce_job(2, ch) for ch in reversed(range(CHUNKS))]
    advance(*jobs)
    copies = []
    for s in range(seqs):
        done = layer_out(s)
        advance(*jobs)
        if s < seqs - 1:
            for cp in done:
                cp.wait()
        else:
            copies += done
    for s in range(seqs):
        copies += input_grad(s)
        advance(*jobs)
    jobs.append(small_job())
    drain(*jobs)
    for cp in copies:
        cp.wait()


def struct(shape, dtype):
    return jax.ShapeDtypeStruct(shape, dtype)


def layer(n_dp, starts, marks, gains, shifts, qvb, b1, tokens, cot, w, ow, fc1, fc2):
    rows, width = tokens.shape
    seqs = starts.shape[0]
    length = rows // seqs
    half = length // 2
    local = w.shape[2]
    heads = local // HEAD
    hidden = fc1.shape[1]
    group = min(4, n_dp // 2)
    extra = (n_dp // (2 * group)).bit_length() - 1
    matrix = 4 * local
    part = matrix // CHUNKS // 2
    piece = part // group
    jobs = 3 * CHUNKS
    smem = pl.BlockSpec(memory_space=pltpu.SMEM)
    vmem = pl.BlockSpec(memory_space=pltpu.VMEM)
    hbm = pl.BlockSpec(memory_space=pl.ANY)
    v = pltpu.VMEM
    dma = pltpu.SemaphoreType.DMA
    small = 9
    return pl.pallas_call(
        functools.partial(layer_kernel, seqs, length, heads, n_dp, group, extra),
        in_specs=[smem, smem, vmem, vmem, vmem, vmem] + [hbm] * 6,
        out_specs=[hbm, hbm, hbm, vmem, hbm],
        scratch_shapes=[
            v((rows, width), BF16),
            v((rows, width), BF16),
            v(w.shape, BF16),
            v(ow.shape, BF16),
            v(fc1.shape, BF16),
            v(fc2.shape, BF16),
            v((seqs, length, width), BF16),
            v((seqs, heads, length, 2 * HEAD), BF16),
            v((seqs, heads, length, 2 * HEAD), BF16),
            v((seqs, heads, length, 2 * HEAD), BF16),
            v((2, length, length), BF16),
            v((2, length, 256), F32),
            v((local, length), F32),
            v((seqs, local, length), BF16),
            v((seqs, heads, 8, length), F32),
            v((2 * seqs + 1, half, width), BF16),
            v((3 * seqs, half, width), BF16),
            v((2 * seqs + 1, half, width), BF16),
            v((3 * seqs, half, width), BF16),
            v((seqs, half, width), F32),
            v((seqs, half, width), F32),
            v((seqs, length, width), BF16),
            v((length, width), BF16),
            v((seqs, half, width), BF16),
            v((seqs, half, width), BF16),
            v((length, length), BF16),
            v((heads, 2 * HEAD, length), BF16),
            v((heads, length, HEAD), BF16),
            v((3, length, local), BF16),
            v((heads, length, HEAD), BF16),
            v((heads, length, HEAD), BF16),
            v((3, matrix, width), BF16),
            v((jobs, part, width), BF16),
            v((jobs, group - 1, piece, width), BF16),
            v((jobs, max(extra, 1), piece, width), BF16),
            v((small, width), F32),
            v((2 + group + extra, small, width), F32),
            dma((7,)),
            dma((4,)),
            dma((4 * seqs, 4)),
            dma((seqs, 2)),
            dma((seqs, 2)),
            dma((jobs, 5 + 4 * (group - 1) + 2 * extra)),
            dma((2 * seqs, 3)),
            dma((4 + 2 * (group - 1) + 2 * extra,)),
        ],
        out_shape=[
            struct((rows, width), BF16),
            struct((rows, width), BF16),
            struct((3, matrix, width), BF16),
            struct((small, width), F32),
            struct((seqs * heads, length, length), BF16),
        ],
        compiler_params=pltpu.CompilerParams(
            collective_id=1, has_side_effects=True, vmem_limit_bytes=63 * 1024 * 1024
        ),
        name="layer",
        cost_estimate=pl.CostEstimate(flops=24 * 10**9, bytes_accessed=50 * 10**6, transcendentals=8 * 10**6),
    )(starts, marks, gains, shifts, qvb, b1, tokens, cot, w, ow, fc1, fc2)


def shards(
    n_dp, tokens, clip_starts, cls_index, norm_gains, shifts, qkv_weight, qv_bias,
    out_weight, fc1_weight, fc1_bias, fc2_weight, cotangent,
):
    width = tokens.shape[1]
    local = qv_bias.shape[1]
    w = jnp.transpose(qkv_weight, (1, 0, 2))
    layer_out, input_grad, mats, small, _ = layer(
        n_dp, clip_starts, cls_index, norm_gains, shifts, qv_bias, fc1_bias.reshape(1, -1), tokens, cotangent,
        w, out_weight, fc1_weight, fc2_weight,
    )
    attn = mats[2].astype(F32).reshape(4, local, width)
    return (
        layer_out,
        input_grad,
        small[0:2],
        small[2:6],
        jnp.transpose(attn[:3], (2, 0, 1)),
        small[7:9, :local],
        attn[3],
        mats[1].astype(F32),
        small[6],
        mats[0].astype(F32),
    )


def solution(mesh):
    row = P("dp", None)
    return jax.shard_map(
        functools.partial(shards, mesh.shape["dp"]),
        mesh=mesh,
        in_specs=(
            row,
            row,
            row,
            P(),
            P(),
            P(None, None, "tensor"),
            P(None, "tensor"),
            P("tensor", None),
            P(None, "tensor"),
            P("tensor"),
            P("tensor", None),
            row,
        ),
        out_specs=(
            row,
            row,
            P(),
            P(),
            P(None, None, "tensor"),
            P(None, "tensor"),
            P("tensor", None),
            P(None, "tensor"),
            P("tensor"),
            P("tensor", None),
        ),
        check_vma=False,
    )
```

```python
import functools

import jax
import jax.numpy as jnp
from jax import lax
from jax.experimental import pallas as pl
from jax.experimental.pallas import tpu as pltpu
from jax.sharding import PartitionSpec as P

HEAD = 64
EPS = 1e-06
F32 = jnp.float32
BF16 = jnp.bfloat16
BLOCK = 112
ROW_CHUNKS = 2
COLUMN_CHUNKS = 1
CHUNKS = ROW_CHUNKS * COLUMN_CHUNKS
TICKS = (1, 0, 1, 1, 1, 1, 2, 1, 1, 1, 3, 2, 3, 3)
MESH = pl.DeviceIdType.MESH


def nn(a, b):
    return lax.dot_general(a, b, (((1,), (0,)), ((), ())), preferred_element_type=F32)


def nt(a, b):
    return lax.dot_general(a, b, (((1,), (1,)), ((), ())), preferred_element_type=F32)


def tn(a, b):
    return lax.dot_general(a, b, (((0,), (0,)), ((), ())), preferred_element_type=F32)


def normalize(x):
    centre = x - jnp.mean(x, axis=-1, keepdims=True)
    factor = lax.rsqrt(jnp.mean(centre * centre, axis=-1, keepdims=True) + EPS)
    return centre * factor, factor


def norm_back(grad, scaled, factor, gain):
    inner = grad * gain
    return factor * (
        inner
        - jnp.mean(inner, axis=-1, keepdims=True)
        - scaled * jnp.mean(inner * scaled, axis=-1, keepdims=True)
    )


def column_sum(x):
    return jnp.sum(x, axis=0, keepdims=True)


def loop(n, body):
    lax.fori_loop(0, n, lambda i, carry: (body(i), carry)[1], 0)


def rows_at(i, size, base=0):
    return pl.ds(pl.multiple_of(base + i * size, 16), size)


def remote(src, dst, send_sem, recv_sem, axis, index):
    return pltpu.make_async_remote_copy(
        src_ref=src, dst_ref=dst, send_sem=send_sem, recv_sem=recv_sem,
        device_id={axis: index}, device_id_type=MESH,
    )


class Pair:
    def __init__(self, send, mine, from_core, from_chip, sems, core, chip):
        self.send, self.mine, self.from_core, self.from_chip = send, mine, from_core, from_chip
        self.to_core = remote(send, from_core, sems.at[0], sems.at[1], "tensor", core)
        self.to_chip = remote(mine, from_chip, sems.at[2], sems.at[3], "tensor", chip)

    def start(self):
        self.to_core.start()

    def gather(self):
        self.to_core.wait()

        def body(i):
            r = rows_at(i, BLOCK)
            self.mine[r, :] = (self.mine[r, :].astype(F32) + self.from_core[r, :].astype(F32)).astype(BF16)

        loop(self.mine.shape[0] // BLOCK, body)

    def middle(self):
        self.gather()
        self.to_chip.start()

    def finish(self):
        self.to_chip.wait()

    def total(self, r):
        return self.mine[r, :].astype(F32) + self.from_chip[r, :].astype(F32)


class Links:
    def __init__(self):
        self.ready, self.flying = ([], []), ([], [])
        self.turn = 0

    def add(self, *jobs):
        for job in jobs:
            axis = next(job, None)
            if axis is not None:
                self.ready[axis].append(job)
        self.fill()

    def fill(self):
        for axis in (0, 1):
            while self.ready[axis] and len(self.flying[axis]) < 2:
                job = self.ready[axis].pop(0)
                next(job)
                self.flying[axis].append(job)

    def tick(self, times=1):
        for _ in range(times):
            axis = self.turn if self.flying[self.turn] else 1 - self.turn
            if not self.flying[axis]:
                return False
            self.turn = 1 - axis
            self.add(self.flying[axis].pop(0))
        return True


def layer_kernel(
    seqs, length, heads, n_dp, group, extra,
    st_ref, mk_ref, gain_ref, shift_ref, qvb_ref, b1_ref, tok_h, cot_h, w_h, ow_h, fc1_h, fc2_h,
    out_h, grad_h, gmat_h, small_ref, e_h,
    tok, cot, ow_ref, fc1, fc2, h1_ref, qa, ka, va, es, ct_s, ctxt_ref, linv_ref,
    bank, fcore, fchip, x1_ref, dx_ref, h2_ref, dxs, dxr_mine, dxr_other, ds_s, da_s, dcx_s, dq_s,
    wt_s, gbuf, rx, rz, re, sv, svr,
    load_sem, e_sem, pair_sem, h2_sem, dx_sem, red_sem, out_sem, small_sem,
):
    half = length // 2
    width = tok.shape[1]
    hidden = fc1.shape[1]
    local = heads * HEAD
    clips = st_ref.shape[1]
    t = lax.axis_index("tensor")
    dp = lax.axis_index("dp")
    c = t % 2
    core = t + 1 - 2 * c
    chip = (t + 2) % 4
    own = pl.multiple_of(c * half, half)
    other = pl.multiple_of((1 - c) * half, half)
    xi = dp % 2
    xpeer = dp + 1 - 2 * xi
    zi = (dp // 2) % group
    zpeers = [dp + 2 * ((zi + k) % group - zi) for k in range(1, group)]
    ebits = [2 * group * 2**k for k in range(extra)]
    epeers = [dp + bit - 2 * bit * ((dp // bit) % 2) for bit in ebits]

    def load(k, src, dst):
        cp = pltpu.make_async_copy(src, dst, load_sem.at[k])
        cp.start()
        return cp

    tok_rows = [pl.ds(s * length, length) for s in range(seqs)]
    load_tok0 = load(0, tok_h.at[tok_rows[0]], tok.at[tok_rows[0]])
    load_w = load(1, w_h, wt_s)
    load_tok1 = load(2, tok_h.at[pl.ds(length, (seqs - 1) * length)], tok.at[pl.ds(length, (seqs - 1) * length)])
    load_ow = load(3, ow_h, ow_ref)
    load_fc1 = load(4, fc1_h, fc1)
    load_cot = load(5, cot_h, cot)
    load_fc2 = load(6, fc2_h, fc2)

    barrier = pltpu.get_barrier_semaphore()
    for peer in (core, chip):
        pl.semaphore_signal(barrier, inc=1, device_id={"tensor": peer}, device_id_type=MESH)
    for peer in [xpeer] + zpeers + epeers:
        pl.semaphore_signal(barrier, inc=1, device_id={"dp": peer}, device_id_type=MESH)
    pl.semaphore_wait(barrier, 3 + len(zpeers) + len(epeers))

    send_a, mine_a, send_d, mine_d, mine_m = (list(range(k * seqs, (k + 1) * seqs)) for k in range(5))
    send_m = [5 * seqs] * seqs

    def pair(give, keep, core_slot, chip_slot, sem):
        return Pair(
            bank.at[give], bank.at[keep], fcore.at[core_slot], fchip.at[chip_slot], pair_sem.at[sem], core, chip
        )

    pair_a = [pair(send_a[s], mine_a[s], s, s, s) for s in range(seqs)]
    pair_d = [pair(send_d[s], mine_d[s], seqs + s, seqs + s, seqs + s) for s in range(seqs)]
    pair_m = [pair(send_m[s], mine_m[s], 2 * seqs, 2 * seqs + s, 2 * seqs + s) for s in range(seqs)]
    pair_g = [pair(send_a[s], mine_a[s], s, s, 3 * seqs + s) for s in range(seqs)]

    sv[...] = jnp.zeros_like(sv)

    def add_sum(row, value):
        sv[row : row + 1, : value.shape[1]] += value

    def spill(j, slot):
        return pltpu.make_async_copy(es.at[slot], e_h.at[j], e_sem.at[slot])

    def fetch(j, slot):
        return pltpu.make_async_copy(e_h.at[j], es.at[slot], e_sem.at[2 + slot])

    def project(s):
        gain = gain_ref[0:1, :].astype(F32)
        shift = shift_ref[0:1, :].astype(F32)
        qvb = qvb_ref[...].astype(F32)
        size = 128

        def norm(i):
            x = tok[rows_at(i, size, s * length), :].astype(F32)
            scaled, _ = normalize(x)
            h1_ref[s, rows_at(i, size), :] = (scaled * gain + shift).astype(BF16)

        loop(length // size, norm)
        block = half

        def body(i):
            r = rows_at(i, block)
            h1 = h1_ref[s, r, :]
            q = (nt(h1, wt_s[:local]) + qvb[0:1]).astype(BF16).astype(F32) * 0.125
            q = q.astype(BF16)
            k = nt(h1, wt_s[local : 2 * local]).astype(BF16)
            v = (nt(h1, wt_s[2 * local :]) + qvb[1:2]).astype(BF16)
            pos = lax.broadcasted_iota(jnp.int32, (block, HEAD), 0) + i * block
            lane = lax.broadcasted_iota(jnp.int32, (block, HEAD), 1)
            clip = jnp.zeros((block, HEAD), jnp.int32) - 1
            mark = jnp.zeros((block, HEAD), jnp.int32)
            for n in range(clips):
                clip = clip + jnp.where(pos >= st_ref[s, n], 1, 0)
                mark = mark + jnp.where(pos == mk_ref[s, n], 1, 0)
            qf = jnp.where(lane == clip, 1.0, 0.0).astype(BF16)
            hide = (lane < clips) & (lane != clip) & (mark == 0)
            kf = jnp.where(hide, -1e30, 0.0).astype(BF16)
            vf = jnp.where(lane < 2, 1.0, 0.0).astype(BF16)
            for h in range(heads):
                cols = slice(h * HEAD, h * HEAD + HEAD)
                qa[s, h, r, :] = jnp.concatenate([q[:, cols], qf], axis=1)
                ka[s, h, r, :] = jnp.concatenate([k[:, cols], kf], axis=1)
                va[s, h, r, :] = jnp.concatenate([v[:, cols], vf], axis=1)

        loop(length // block, body)

    spans = [(t0, min(256, length - t0)) for t0 in range(0, length, 256)]

    def attend(s):
        def head(h):
            j = s * heads + h
            slot = lax.rem(j, 2)

            @pl.when(j >= 2)
            def _():
                spill(j, slot).wait()

            v = va[s, h, :, :HEAD]
            for i, (t0, n) in enumerate(spans):
                sl = i % 2
                score = nt(ka[s, h], qa[s, h, t0 : t0 + n])
                dx_ref[sl, :, :n] = score[:half]
                dx_ref[sl, :, 256 : 256 + n] = score[half:]
                scores = lambda u, ch: dx_ref[sl, u % half : u % half + ch, (u // half) * 256 : (u // half) * 256 + n]
                ch = 64
                m = None
                for u in range(0, length, ch):
                    x = jnp.max(scores(u, ch).reshape(ch // 8, 8, n), axis=0)
                    m = x if m is None else jnp.maximum(m, x)
                m = jnp.max(m, axis=0, keepdims=True)
                tot = None
                for u in range(0, length, ch):
                    x = jnp.exp(scores(u, ch) - m)
                    es[slot, u : u + ch, t0 : t0 + n] = x.astype(BF16)
                    x = jnp.sum(x.reshape(ch // 8, 8, n), axis=0)
                    tot = x if tot is None else tot + x
                inv = 1.0 / jnp.sum(tot, axis=0, keepdims=True)
                linv_ref[s, h, :, t0 : t0 + n] = jnp.broadcast_to(inv, (8, n))
                ct_s[rows_at(h, HEAD), t0 : t0 + n] = tn(v, es[slot, :, t0 : t0 + n]) * inv
            spill(j, slot).start()

        loop(heads, head)
        ctxt_ref[s] = ct_s[...].astype(BF16)
        dq_s[:, :local] = jnp.transpose(ct_s[...]).astype(BF16)

        def rows_out(dst, base):
            bank[dst] = nn(dq_s[pl.ds(base, half), :local], ow_ref[...]).astype(BF16)

        rows_out(send_a[s], other)
        pair_a[s].start()
        rows_out(mine_a[s], own)

    h2_copies = [
        remote(
            h2_ref.at[s, pl.ds(own, half)], h2_ref.at[s, pl.ds(own, half)], h2_sem.at[s, 0], h2_sem.at[s, 1],
            "tensor", core,
        )
        for s in range(seqs)
    ]

    def norm_two(s):
        pair_a[s].finish()
        g = gain_ref[1:2, :].astype(F32)
        b1 = shift_ref[1:2, :].astype(F32)
        b2 = shift_ref[2:3, :].astype(F32)

        def body(i):
            r = rows_at(i, BLOCK)
            x = tok[rows_at(i, BLOCK, s * length + own), :].astype(F32)
            x1 = x + pair_a[s].total(r) + b2
            x1_ref[s, r, :] = x1
            scaled, _ = normalize(x1)
            h2_ref[s, rows_at(i, BLOCK, own), :] = (scaled * g + b1).astype(BF16)

        loop(half // BLOCK, body)
        h2_copies[s].start()

    act_ref, dpre_ref = ds_s, dxs

    def feed_forward(s):
        size = half // 2
        n = length // size
        b1 = b1_ref[...].astype(F32).reshape(1, hidden)
        at = lambda i: own + (i // 2) * (other - own) + (i % 2) * size
        rows = lambda i, base=0: pl.ds(pl.multiple_of(base + at(i), 16), size)

        def first(i):
            dx_ref[i % 2, :size, :] = nn(h2_ref[s, rows(i), :], fc1[...]) + b1

        def second(i):
            dact = nt(cot[rows(i, s * length), :], fc2[...])
            pre = dx_ref[i % 2, :size, :]
            phi = 0.5 * (1.0 + lax.erf(pre * 0.7071067811865476))
            act_ref[rows(i), :hidden] = (pre * phi).astype(BF16)
            slope = phi + pre * (0.3989422804014327 * jnp.exp(-0.5 * pre * pre))
            dpre = (dact * slope).astype(BF16)
            dpre_ref[rows(i), :hidden] = dpre
            add_sum(6, column_sum(dpre.astype(F32)))

        def third(i):
            far = i // 2
            r = pl.ds(pl.multiple_of((i % 2) * size, size), size)
            bank[mine_m[s] + far * (send_m[s] - mine_m[s]), r, :] = nn(act_ref[rows(i), :hidden], fc2[...]).astype(BF16)
            bank[mine_d[s] + far * (send_d[s] - mine_d[s]), r, :] = nt(dpre_ref[rows(i), :hidden], fc1[...]).astype(BF16)

        first(0)
        first(1)
        second(0)

        def body(k):
            i = k + 1

            @pl.when(k == 0)
            def _():
                h2_copies[s].wait()

            third(i - 1)
            first(i + 1)
            second(i)

        loop(n - 2, body)
        third(n - 2)
        second(n - 1)
        third(n - 1)

    def fc_grad(m, left, right, s, tile):
        def body(i):
            r = pl.ds(pl.multiple_of(i * tile, tile), tile)
            p = tn(left(r), right())
            if s > 0:
                p = p + gbuf[m, r, :].astype(F32)
            gbuf[m, r, :] = p.astype(BF16)

        loop(width // tile, body)

    def fc2_grad(s):
        fc_grad(0, lambda r: act_ref[:, r], lambda: cot[tok_rows[s], :], s, 256)

    def fc1_grad(s):
        fc_grad(1, lambda r: h2_ref[s, :, r], lambda: dpre_ref[:, :hidden], s, 256)

    piece = gbuf.shape[1] // ROW_CHUNKS // 2 // group
    span = width // COLUMN_CHUNKS

    def reduce_job(m, ch):
        job = m * CHUNKS + ch
        base = (ch // COLUMN_CHUNKS) * (gbuf.shape[1] // ROW_CHUNKS)
        cols = pl.ds((ch % COLUMN_CHUNKS) * span, span)
        part = group * piece
        sem = iter(range(red_sem.shape[1]))
        two = lambda: (red_sem.at[job, next(sem)], red_sem.at[job, next(sem)])
        rows = lambda start, n: gbuf.at[m, pl.ds(pl.multiple_of(start, 16), n), cols]

        def add(start, n, sources):
            size = piece

            def body(i):
                r = rows_at(i, size, start)
                total = gbuf[m, r, cols].astype(F32)
                for src in sources:
                    total = total + src[rows_at(i, size), :].astype(F32)
                gbuf[m, r, cols] = total.astype(BF16)

            loop(n // size, body)

        mine_at = base + xi * part
        cp = remote(rows(base + (1 - xi) * part, part), rx.at[job], *two(), "dp", xpeer)
        yield 0
        cp.start()
        yield
        cp.wait()
        add(mine_at, part, [rx.at[job]])
        cps = [
            remote(rows(mine_at + ((zi + k + 1) % group) * piece, piece), rz.at[job, k], *two(), "dp", p)
            for k, p in enumerate(zpeers)
        ]
        yield 1
        for cp in cps:
            cp.start()
        yield
        for cp in cps:
            cp.wait()
        piece_at = mine_at + zi * piece
        add(piece_at, piece, [rz.at[job, k] for k in range(group - 1)])
        for k, p in enumerate(epeers):
            cp = remote(rows(piece_at, piece), re.at[job, k], *two(), "dp", p)
            yield 1
            cp.start()
            yield
            cp.wait()
            add(piece_at, piece, [re.at[job, k]])
        done = lambda start, n: gmat_h.at[m, pl.ds(pl.multiple_of(start, 16), n), cols]
        cps = [remote(rows(piece_at, piece), done(piece_at, piece), *two(), "dp", p) for p in zpeers]
        cps.append(pltpu.make_async_copy(rows(piece_at, piece), done(piece_at, piece), red_sem.at[job, next(sem)]))
        yield 1
        for cp in cps:
            cp.start()
        yield
        for cp in cps:
            cp.wait()
        cp = remote(done(mine_at, part), done(mine_at, part), *two(), "dp", xpeer)
        yield 0
        cp.start()
        yield
        cp.wait()

    links = Links()

    dx_copies = [
        remote(dxr_mine.at[s], dxr_other.at[s], dx_sem.at[s, 0], dx_sem.at[s, 1], "tensor", core)
        for s in range(seqs)
    ]

    def mid(s):
        pair_d[s].finish()
        g = gain_ref[1:2, :].astype(F32)

        def body(i):
            r = rows_at(i, BLOCK)
            dh2 = pair_d[s].total(r)
            scaled, factor = normalize(x1_ref[s, r, :])
            dy = cot[rows_at(i, BLOCK, s * length + own), :].astype(F32)
            dx = dy + norm_back(dh2, scaled, factor, g)
            dx_ref[s, r, :] = dx
            dxr_mine[s, r, :] = dx.astype(BF16)
            add_sum(1, column_sum(dh2 * scaled))
            add_sum(3, column_sum(dh2))
            add_sum(4, column_sum(dx))
            add_sum(5, column_sum(dy))

        loop(half // BLOCK, body)
        dx_copies[s].start()

    def back_setup(s):
        dxs[pl.ds(own, half), :] = dxr_mine[s]
        dx_copies[s].wait()
        dxs[pl.ds(other, half), :] = dxr_other[s]
        ct_s[...] = nt(ow_ref[...], dxs[...])
        for h in range(heads):
            lo = h * HEAD
            inv = linv_ref[s, h, 0:1, :]
            part = ct_s[lo : lo + HEAD, :].astype(BF16).astype(F32)
            delta = column_sum(part * ctxt_ref[s, lo : lo + HEAD, :].astype(F32)) * inv
            high = delta.astype(BF16).astype(F32)
            low = delta - high
            row = lax.broadcasted_iota(jnp.int32, (HEAD, length), 0)
            feat = jnp.where(row == 0, -high, jnp.where(row == 1, -low, 0.0))
            part = part * inv
            da_s[h, :HEAD, :] = part.astype(BF16)
            da_s[h, HEAD:, :] = feat.astype(BF16)
            dcx_s[h] = jnp.transpose(part).astype(BF16)

    def back_head(s, h):
        j = s * heads + h
        slot = j % 2
        fetch(j, slot).wait()
        for t0, n in spans:
            dp_t = nn(va[s, h], da_s[h, :, t0 : t0 + n])
            ds = (es[slot, :, t0 : t0 + n].astype(F32) * dp_t).astype(BF16)
            ds_s[:, t0 : t0 + n] = ds
            ct_s[rows_at(h, HEAD), t0 : t0 + n] = tn(ka[s, h, :, :HEAD], ds) * 0.125
        lo = h * HEAD
        dq_s[:, 2 * local + lo : 2 * local + lo + HEAD] = nn(es[slot], dcx_s[h]).astype(BF16)
        dq_s[:, local + lo : local + lo + HEAD] = nn(ds_s[...], qa[s, h, :, :HEAD]).astype(BF16)
        if j + 2 < seqs * heads:
            fetch(j + 2, slot).start()

    def back_end(s):
        dq_s[:, :local] = jnp.transpose(ct_s[...]).astype(BF16)

        def rows_out(dst, base):
            bank[dst] = nn(dq_s[pl.ds(base, half), : 3 * local], wt_s[...]).astype(BF16)

        rows_out(send_a[s], other)
        pair_g[s].start()
        rows_out(mine_a[s], own)

    def back_grads(s):
        h1 = h1_ref[s]
        for i in (2, 3, 0, 1):
            p = tn(dq_s[:, i * local : (i + 1) * local], h1) if i < 3 else nn(ctxt_ref[s], dxs[...])
            r = slice(i * local, (i + 1) * local)
            if s > 0:
                p = p + gbuf[2, r, :].astype(F32)
            gbuf[2, r, :] = p.astype(BF16)
        add_sum(7, column_sum(dq_s[:, :local].astype(F32)))
        sv[8:9, :local] += column_sum(dq_s[:, 2 * local : 3 * local].astype(F32))

    def place(k, stage, dst_h, s):
        rows = pl.ds(pl.multiple_of(s * length + own, 16), half)
        here = pltpu.make_async_copy(stage, dst_h.at[rows], out_sem.at[k, 0])
        there = remote(stage, dst_h.at[rows], out_sem.at[k, 1], out_sem.at[k, 2], "tensor", core)
        here.start()
        there.start()
        return here, there

    def layer_out(s):
        pair_m[s].finish()
        b3 = shift_ref[3:4, :].astype(F32)
        stage = bank.at[send_m[s]]

        def body(i):
            r = rows_at(i, BLOCK)
            stage[r, :] = (x1_ref[s, r, :] + pair_m[s].total(r) + b3).astype(BF16)

        loop(half // BLOCK, body)
        return place(s, stage, out_h, s)

    def input_grad(s):
        pair_g[s].finish()
        g = gain_ref[0:1, :].astype(F32)
        stage = bank.at[send_a[s]]

        def body(i):
            r = rows_at(i, BLOCK)
            dh1 = pair_g[s].total(r)
            scaled, factor = normalize(tok[rows_at(i, BLOCK, s * length + own), :].astype(F32))
            stage[r, :] = (dx_ref[s, r, :] + norm_back(dh1, scaled, factor, g)).astype(BF16)
            add_sum(0, column_sum(dh1 * scaled))
            add_sum(2, column_sum(dh1))

        loop(half // BLOCK, body)
        return place(seqs + s, stage, grad_h, s)

    def small_job():
        sem = iter(range(small_sem.shape[0]))
        two = lambda: (small_sem.at[next(sem)], small_sem.at[next(sem)])
        slot = iter(range(svr.shape[0]))
        k = next(slot)
        cp = remote(sv.at[pl.ds(0, 6)], svr.at[k, pl.ds(0, 6)], *two(), "tensor", core)
        cp.start()
        yield
        cp.wait()
        sv[0:6, :] += svr[k, 0:6, :]
        for p in [xpeer]:
            k = next(slot)
            cp = remote(sv, svr.at[k], *two(), "dp", p)
            cp.start()
            yield
            cp.wait()
            sv[...] += svr[k]
        base = k + 1
        cps = []
        for i, p in enumerate(zpeers):
            cps.append(remote(sv, svr.at[base + zi], *two(), "dp", p))
        for cp in cps:
            cp.start()
        svr[base + zi] = sv[...]
        yield
        for cp in cps:
            cp.wait()
        total = svr[base]
        for i in range(1, group):
            total = total + svr[base + i]
        sv[...] = total
        for i, p in enumerate(epeers):
            k = base + group + i
            cp = remote(sv, svr.at[k], *two(), "dp", p)
            cp.start()
            yield
            cp.wait()
            sv[...] += svr[k]
        small_ref[...] = sv[...]

    load_tok0.wait()
    load_w.wait()
    project(0)
    load_ow.wait()
    attend(0)
    load_tok1.wait()
    for s in range(1, seqs):
        project(s)
        pair_a[s - 1].middle()
        attend(s)
    load_fc1.wait()
    load_cot.wait()
    load_fc2.wait()
    pair_a[seqs - 1].middle()
    for k in (seqs * heads - 2, seqs * heads - 1):
        spill(k, k % 2).wait()
    for k in (0, 1):
        fetch(k, k % 2).start()
    end = seqs - 1
    for s in range(seqs):
        norm_two(s)
        feed_forward(s)
        pair_d[s].start()
        pair_m[s].start()
        fc2_grad(s)
        pair_d[s].middle()
        if s == end:
            links.add(*[reduce_job(0, ch) for ch in range(CHUNKS)])
        pair_m[s].gather()
        fc1_grad(s)
    links.add(*[reduce_job(1, ch) for ch in range(CHUNKS)])
    tick = lambda k: links.tick(TICKS[k])
    for s in range(seqs):
        last = int(s == end)
        if s > 0:
            tick(0)
        mid(s)
        tick(1 + last)
        back_setup(s)
        for h in range(heads):
            back_head(s, h)
            tick(3 + 3 * last + min(h, 2))
            if h == 1:
                pair_m[s].to_chip.start()
        back_end(s)
        back_grads(s)
        pair_g[s].middle()
        if s == end:
            links.add(*[reduce_job(2, ch) for ch in reversed(range(CHUNKS))])
        tick(9 + last)
    copies = []
    for s in range(end):
        copies += input_grad(s)
        tick(11)
        for cp in layer_out(s):
            cp.wait()
        tick(12)
    copies += input_grad(end)
    small = small_job()
    next(small)
    tick(13)
    next(small, None)
    copies += layer_out(end)
    while links.tick():
        next(small, None)
    for _ in small:
        pass
    for cp in copies:
        cp.wait()


def struct(shape, dtype):
    return jax.ShapeDtypeStruct(shape, dtype)


def layer(n_dp, starts, marks, gains, shifts, qvb, b1, tokens, cot, w, ow, fc1, fc2):
    rows, width = tokens.shape
    seqs = starts.shape[0]
    length = rows // seqs
    half = length // 2
    local = w.shape[0] // 3
    heads = local // HEAD
    hidden = fc1.shape[1]
    group = min(4, n_dp // 2)
    extra = (n_dp // (2 * group)).bit_length() - 1
    matrix = 4 * local
    part = matrix // ROW_CHUNKS // 2
    span = width // COLUMN_CHUNKS
    piece = part // group
    jobs = 3 * CHUNKS
    smem = pl.BlockSpec(memory_space=pltpu.SMEM)
    vmem = pl.BlockSpec(memory_space=pltpu.VMEM)
    hbm = pl.BlockSpec(memory_space=pl.ANY)
    v = pltpu.VMEM
    dma = pltpu.SemaphoreType.DMA
    small = 9
    return pl.pallas_call(
        functools.partial(layer_kernel, seqs, length, heads, n_dp, group, extra),
        in_specs=[smem, smem, vmem, vmem, vmem, vmem] + [hbm] * 6,
        out_specs=[hbm, hbm, hbm, vmem, hbm],
        scratch_shapes=[
            v((rows, width), BF16),
            v((rows, width), BF16),
            v(ow.shape, BF16),
            v(fc1.shape, BF16),
            v(fc2.shape, BF16),
            v((seqs, length, width), BF16),
            v((seqs, heads, length, 2 * HEAD), BF16),
            v((seqs, heads, length, 2 * HEAD), BF16),
            v((seqs, heads, length, 2 * HEAD), BF16),
            v((2, length, length), BF16),
            v((local, length), F32),
            v((seqs, local, length), BF16),
            v((seqs, heads, 8, length), F32),
            v((5 * seqs + 1, half, width), BF16),
            v((2 * seqs + 1, half, width), BF16),
            v((3 * seqs, half, width), BF16),
            v((seqs, half, width), F32),
            v((seqs, half, width), F32),
            v((seqs, length, width), BF16),
            v((length, width), BF16),
            v((seqs, half, width), BF16),
            v((seqs, half, width), BF16),
            v((length, length), BF16),
            v((heads, 2 * HEAD, length), BF16),
            v((heads, length, HEAD), BF16),
            v((length, 3 * local), BF16),
            v((3 * local, width), BF16),
            v((3, matrix, width), BF16),
            v((jobs, part, span), BF16),
            v((jobs, group - 1, piece, span), BF16),
            v((jobs, max(extra, 1), piece, span), BF16),
            v((small, width), F32),
            v((2 + group + extra, small, width), F32),
            dma((7,)),
            dma((4,)),
            dma((4 * seqs, 4)),
            dma((seqs, 2)),
            dma((seqs, 2)),
            dma((jobs, 5 + 4 * (group - 1) + 2 * extra)),
            dma((2 * seqs, 3)),
            dma((4 + 2 * (group - 1) + 2 * extra,)),
        ],
        out_shape=[
            struct((rows, width), BF16),
            struct((rows, width), BF16),
            struct((3, matrix, width), BF16),
            struct((small, width), F32),
            struct((seqs * heads, length, length), BF16),
        ],
        compiler_params=pltpu.CompilerParams(
            collective_id=1, has_side_effects=True, vmem_limit_bytes=63 * 1024 * 1024
        ),
        name="layer",
        cost_estimate=pl.CostEstimate(flops=24 * 10**9, bytes_accessed=50 * 10**6, transcendentals=8 * 10**6),
    )(starts, marks, gains, shifts, qvb, b1, tokens, cot, w, ow, fc1, fc2)


def finish_kernel(
    out_h, grad_h, mats_h, small_ref, out_o, grad_o, gain_o, shift_o, qkv_o, qvb_o, ow_o, fc1_o, b1_o, fc2_o,
    low, wide, rows, load_sem, store_sem,
):
    local = qvb_o.shape[1]
    loads = [pltpu.make_async_copy(mats_h.at[m], low.at[m], load_sem.at[m]) for m in range(3)]
    for k, ref in enumerate((out_h, grad_h)):
        loads.append(pltpu.make_async_copy(ref, rows.at[k], load_sem.at[3 + k]))
    for cp in loads:
        cp.start()
    stores = []
    gain_o[...] = small_ref[0:2, :]
    shift_o[...] = small_ref[2:6, :]
    b1_o[...] = small_ref[6, : b1_o.shape[0]]
    qvb_o[...] = small_ref[7:9, :local]
    targets = ([(fc2_o, 0, fc2_o.shape[0])], [(fc1_o, 0, fc1_o.shape[0])], [(qkv_o, 0, 3 * local), (ow_o, 3 * local, local)])
    for m in range(3):
        loads[m].wait()
        wide[m] = low[m].astype(F32)
        for k, (ref, start, n) in enumerate(targets[m]):
            cp = pltpu.make_async_copy(wide.at[m, pl.ds(start, n)], ref, store_sem.at[2 + m + k])
            cp.start()
            stores.append(cp)
    for k, ref in enumerate((out_o, grad_o)):
        loads[3 + k].wait()
        cp = pltpu.make_async_copy(rows.at[k], ref, store_sem.at[k])
        cp.start()
        stores.append(cp)
    for cp in stores:
        cp.wait()


def finish(local, hidden, layer_out, input_grad, mats, small):
    rows, width = layer_out.shape
    vmem = pl.BlockSpec(memory_space=pltpu.VMEM)
    hbm = pl.BlockSpec(memory_space=pltpu.HBM)
    return pl.pallas_call(
        finish_kernel,
        in_specs=[hbm, hbm, hbm, vmem],
        out_specs=[hbm, hbm, vmem, vmem, hbm, vmem, hbm, hbm, vmem, hbm],
        scratch_shapes=[
            pltpu.VMEM(mats.shape, BF16),
            pltpu.VMEM(mats.shape, F32),
            pltpu.VMEM((2, rows, width), BF16),
            pltpu.SemaphoreType.DMA((5,)),
            pltpu.SemaphoreType.DMA((6,)),
        ],
        out_shape=[
            struct((rows, width), BF16),
            struct((rows, width), BF16),
            struct((2, width), F32),
            struct((4, width), F32),
            struct((3 * local, width), F32),
            struct((2, local), F32),
            struct((local, width), F32),
            struct((width, hidden), F32),
            struct((hidden,), F32),
            struct((hidden, width), F32),
        ],
        compiler_params=pltpu.CompilerParams(vmem_limit_bytes=63 * 1024 * 1024),
        name="finish",
    )(layer_out, input_grad, mats, small)


def shards(
    n_dp, tokens, clip_starts, cls_index, norm_gains, shifts, qkv_weight, qv_bias,
    out_weight, fc1_weight, fc1_bias, fc2_weight, cotangent,
):
    width = tokens.shape[1]
    local = qv_bias.shape[1]
    hidden = fc1_bias.shape[0]
    w = jnp.transpose(qkv_weight, (1, 2, 0)).reshape(3 * local, width)
    layer_out, input_grad, mats, small, _ = layer(
        n_dp, clip_starts, cls_index, norm_gains, shifts, qv_bias, fc1_bias, tokens, cotangent,
        w, out_weight, fc1_weight, fc2_weight,
    )
    out, grad, gain, shift, qkv, qvb, ow, fc1, b1, fc2 = finish(local, hidden, layer_out, input_grad, mats, small)
    qkv = jnp.transpose(qkv.reshape(3, local, width), (2, 0, 1))
    return out, grad, gain, shift, qkv, qvb, ow, fc1, b1, fc2


def solution(mesh):
    row = P("dp", None)
    return jax.shard_map(
        functools.partial(shards, mesh.shape["dp"]),
        mesh=mesh,
        in_specs=(
            row,
            row,
            row,
            P(),
            P(),
            P(None, None, "tensor"),
            P(None, "tensor"),
            P("tensor", None),
            P(None, "tensor"),
            P("tensor"),
            P("tensor", None),
            row,
        ),
        out_specs=(
            row,
            row,
            P(),
            P(),
            P(None, None, "tensor"),
            P(None, "tensor"),
            P("tensor", None),
            P(None, "tensor"),
            P("tensor"),
            P("tensor", None),
        ),
        check_vma=False,
    )
```

```python
import functools

import jax
import jax.numpy as jnp
from jax import lax
from jax.experimental import pallas as pl
from jax.experimental.pallas import tpu as pltpu
from jax.sharding import PartitionSpec as P

HEAD = 64
EPS = 1e-06
F32 = jnp.float32
BF16 = jnp.bfloat16
BLOCK = 112
ROW_CHUNKS = 2
COLUMN_CHUNKS = 1
CHUNKS = ROW_CHUNKS * COLUMN_CHUNKS
TICKS = (1, 0, 1, 0, 1, 1, 1, 1, 1, 1, 2, 3, 4, 4)
MESH = pl.DeviceIdType.MESH


def nn(a, b):
    return lax.dot_general(a, b, (((1,), (0,)), ((), ())), preferred_element_type=F32)


def nt(a, b):
    return lax.dot_general(a, b, (((1,), (1,)), ((), ())), preferred_element_type=F32)


def tn(a, b):
    return lax.dot_general(a, b, (((0,), (0,)), ((), ())), preferred_element_type=F32)


def normalize(x):
    centre = x - jnp.mean(x, axis=-1, keepdims=True)
    factor = lax.rsqrt(jnp.mean(centre * centre, axis=-1, keepdims=True) + EPS)
    return centre * factor, factor


def norm_back(grad, scaled, factor, gain):
    inner = grad * gain
    return factor * (
        inner
        - jnp.mean(inner, axis=-1, keepdims=True)
        - scaled * jnp.mean(inner * scaled, axis=-1, keepdims=True)
    )


def column_sum(x):
    return jnp.sum(x, axis=0, keepdims=True)


def loop(n, body):
    lax.fori_loop(0, n, lambda i, carry: (body(i), carry)[1], 0)


def rows_at(i, size, base=0):
    return pl.ds(pl.multiple_of(base + i * size, 16), size)


def remote(src, dst, send_sem, recv_sem, axis, index):
    return pltpu.make_async_remote_copy(
        src_ref=src, dst_ref=dst, send_sem=send_sem, recv_sem=recv_sem,
        device_id={axis: index}, device_id_type=MESH,
    )


class Pair:
    def __init__(self, send, mine, from_core, from_chip, sems, core, chip):
        self.send, self.mine, self.from_core, self.from_chip = send, mine, from_core, from_chip
        self.to_core = remote(send, from_core, sems.at[0], sems.at[1], "tensor", core)
        self.to_chip = remote(mine, from_chip, sems.at[2], sems.at[3], "tensor", chip)

    def start(self):
        self.to_core.start()

    def gather(self):
        self.to_core.wait()

        def body(i):
            r = rows_at(i, BLOCK)
            self.mine[r, :] = (self.mine[r, :].astype(F32) + self.from_core[r, :].astype(F32)).astype(BF16)

        loop(self.mine.shape[0] // BLOCK, body)

    def middle(self):
        self.gather()
        self.to_chip.start()

    def finish(self):
        self.to_chip.wait()

    def total(self, r):
        return self.mine[r, :].astype(F32) + self.from_chip[r, :].astype(F32)


class Links:
    def __init__(self):
        self.ready, self.flying = ([], []), ([], [])
        self.turn = 0

    def add(self, *jobs):
        for job in jobs:
            axis = next(job, None)
            if axis is not None:
                self.ready[axis].append(job)
        self.fill()

    def fill(self):
        for axis in (0, 1):
            while self.ready[axis] and len(self.flying[axis]) < 2:
                job = self.ready[axis].pop(0)
                next(job)
                self.flying[axis].append(job)

    def tick(self, times=1):
        for _ in range(times):
            axis = self.turn if self.flying[self.turn] else 1 - self.turn
            if not self.flying[axis]:
                return False
            self.turn = 1 - axis
            self.add(self.flying[axis].pop(0))
        return True


def layer_kernel(
    seqs, length, heads, n_dp, group, extra,
    st_ref, mk_ref, gain_ref, shift_ref, qvb_ref, b1_ref, tok_h, cot_h, w_h, ow_h, fc1_h, fc2_h,
    out_h, grad_h, gmat_h, small_ref, e_h,
    tok, cot, ow_ref, fc1, fc2, h1_ref, qa, ka, va, es, ct_s, ctxt_ref, linv_ref,
    bank, fcore, fchip, ctx_n, ctx_g, x1_ref, dx_ref, h2_ref, dxs, dxr_other, ds_s, da_s, dcx_s, dq_s,
    wt_s, gbuf, rx, rz, re, sv, svr,
    load_sem, e_sem, ctx_sem, ow_sem, pair_sem, h2_sem, dx_sem, red_sem, out_sem, small_sem,
):
    half = length // 2
    width = tok.shape[1]
    hidden = fc1.shape[1]
    local = heads * HEAD
    clips = st_ref.shape[1]
    t = lax.axis_index("tensor")
    dp = lax.axis_index("dp")
    c = t % 2
    core = t + 1 - 2 * c
    chip = (t + 2) % 4
    diag = chip + 1 - 2 * (chip % 2)
    groups = ctx_g.shape[1]
    own = pl.multiple_of(c * half, half)
    other = pl.multiple_of((1 - c) * half, half)
    xi = dp % 2
    xpeer = dp + 1 - 2 * xi
    zi = (dp // 2) % group
    zpeers = [dp + 2 * ((zi + k) % group - zi) for k in range(1, group)]
    ebits = [2 * group * 2**k for k in range(extra)]
    epeers = [dp + bit - 2 * bit * ((dp // bit) % 2) for bit in ebits]

    def load(k, src, dst):
        cp = pltpu.make_async_copy(src, dst, load_sem.at[k])
        cp.start()
        return cp

    tok_rows = [pl.ds(s * length, length) for s in range(seqs)]
    load_tok0 = load(0, tok_h.at[tok_rows[0]], tok.at[tok_rows[0]])
    load_w = load(1, w_h, wt_s)
    load_tok1 = load(2, tok_h.at[pl.ds(length, (seqs - 1) * length)], tok.at[pl.ds(length, (seqs - 1) * length)])
    group_rows = lambda g: pl.ds(pl.multiple_of(g * local, 16), local)
    load_ow = load(3, ow_h, ow_ref.at[group_rows(t)])
    load_fc1 = load(4, fc1_h, fc1)
    load_cot = load(5, cot_h, cot)
    load_fc2 = load(6, fc2_h, fc2)

    barrier = pltpu.get_barrier_semaphore()
    for peer in (core, chip, diag):
        pl.semaphore_signal(barrier, inc=1, device_id={"tensor": peer}, device_id_type=MESH)
    for peer in [xpeer] + zpeers + epeers:
        pl.semaphore_signal(barrier, inc=1, device_id={"dp": peer}, device_id_type=MESH)
    pl.semaphore_wait(barrier, 4 + len(zpeers) + len(epeers))

    send_d, mine_d, mine_m = (list(range(k * seqs, (k + 1) * seqs)) for k in range(3))
    send_m = [3 * seqs] * seqs

    def pair(give, keep, core_slot, chip_slot, sem):
        return Pair(
            bank.at[give], bank.at[keep], fcore.at[core_slot], fchip.at[chip_slot], pair_sem.at[sem], core, chip
        )

    ow_copies = [
        remote(ow_ref.at[group_rows(g)], ow_ref.at[group_rows(g)], ow_sem.at[k, 0], ow_sem.at[k, 1], "tensor", p)
        for k, (g, p) in enumerate(((t, core), (t, chip), (chip, core)))
    ]
    ctx_copies = [
        [
            remote(
                ctx_n.at[s, pl.ds(start, half)], ctx_g.at[s, t], ctx_sem.at[s, k, 0], ctx_sem.at[s, k, 1], "tensor", p
            )
            for k, (p, start) in enumerate(((diag, other), (chip, own), (core, other)))
        ]
        for s in range(seqs)
    ]
    pair_d = [pair(send_d[s], mine_d[s], s, seqs + s, seqs + s) for s in range(seqs)]
    pair_m = [pair(send_m[s], mine_m[s], seqs, 2 * seqs + s, 2 * seqs + s) for s in range(seqs)]
    pair_g = [pair(send_d[s], mine_d[s], s, s, 3 * seqs + s) for s in range(seqs)]

    sv[...] = jnp.zeros_like(sv)

    def add_sum(row, value):
        sv[row : row + 1, : value.shape[1]] += value

    def spill(j, slot):
        return pltpu.make_async_copy(es.at[slot], e_h.at[j], e_sem.at[slot])

    def fetch(j, slot):
        return pltpu.make_async_copy(e_h.at[j], es.at[slot], e_sem.at[2 + slot])

    def project(s):
        gain = gain_ref[0:1, :].astype(F32)
        shift = shift_ref[0:1, :].astype(F32)
        qvb = qvb_ref[...].astype(F32)
        size = 128

        def norm(i):
            x = tok[rows_at(i, size, s * length), :].astype(F32)
            scaled, _ = normalize(x)
            h1_ref[s, rows_at(i, size), :] = (scaled * gain + shift).astype(BF16)

        loop(length // size, norm)
        block = half

        def body(i):
            r = rows_at(i, block)
            h1 = h1_ref[s, r, :]
            q = (nt(h1, wt_s[:local]) + qvb[0:1]).astype(BF16).astype(F32) * 0.125
            q = q.astype(BF16)
            k = nt(h1, wt_s[local : 2 * local]).astype(BF16)
            v = (nt(h1, wt_s[2 * local :]) + qvb[1:2]).astype(BF16)
            pos = lax.broadcasted_iota(jnp.int32, (block, HEAD), 0) + i * block
            lane = lax.broadcasted_iota(jnp.int32, (block, HEAD), 1)
            clip = jnp.zeros((block, HEAD), jnp.int32) - 1
            mark = jnp.zeros((block, HEAD), jnp.int32)
            for n in range(clips):
                clip = clip + jnp.where(pos >= st_ref[s, n], 1, 0)
                mark = mark + jnp.where(pos == mk_ref[s, n], 1, 0)
            qf = jnp.where(lane == clip, 1.0, 0.0).astype(BF16)
            hide = (lane < clips) & (lane != clip) & (mark == 0)
            kf = jnp.where(hide, -1e30, 0.0).astype(BF16)
            vf = jnp.where(lane < 2, 1.0, 0.0).astype(BF16)
            for h in range(heads):
                cols = slice(h * HEAD, h * HEAD + HEAD)
                qa[s, h, r, :] = jnp.concatenate([q[:, cols], qf], axis=1)
                ka[s, h, r, :] = jnp.concatenate([k[:, cols], kf], axis=1)
                va[s, h, r, :] = jnp.concatenate([v[:, cols], vf], axis=1)

        loop(length // block, body)

    spans = [(t0, min(256, length - t0)) for t0 in range(0, length, 256)]

    def attend(s):
        def head(h):
            j = s * heads + h
            slot = lax.rem(j, 2)

            @pl.when(j >= 2)
            def _():
                spill(j, slot).wait()

            v = va[s, h, :, :HEAD]
            for i, (t0, n) in enumerate(spans):
                sl = i % 2
                score = nt(ka[s, h], qa[s, h, t0 : t0 + n])
                dx_ref[sl, :, :n] = score[:half]
                dx_ref[sl, :, 256 : 256 + n] = score[half:]
                scores = lambda u, ch: dx_ref[sl, u % half : u % half + ch, (u // half) * 256 : (u // half) * 256 + n]
                ch = 64
                m = None
                for u in range(0, length, ch):
                    x = jnp.max(scores(u, ch).reshape(ch // 8, 8, n), axis=0)
                    m = x if m is None else jnp.maximum(m, x)
                m = jnp.max(m, axis=0, keepdims=True)
                tot = None
                for u in range(0, length, ch):
                    x = jnp.exp(scores(u, ch) - m)
                    es[slot, u : u + ch, t0 : t0 + n] = x.astype(BF16)
                    x = jnp.sum(x.reshape(ch // 8, 8, n), axis=0)
                    tot = x if tot is None else tot + x
                inv = 1.0 / jnp.sum(tot, axis=0, keepdims=True)
                linv_ref[s, h, :, t0 : t0 + n] = jnp.broadcast_to(inv, (8, n))
                ct_s[rows_at(h, HEAD), t0 : t0 + n] = tn(v, es[slot, :, t0 : t0 + n]) * inv
            spill(j, slot).start()

        loop(heads, head)
        ctxt_ref[s] = ct_s[...].astype(BF16)
        ctx_n[s] = jnp.transpose(ct_s[...]).astype(BF16)
        for cp in ctx_copies[s]:
            cp.start()
        ctx_g[s, t] = ctx_n[s, pl.ds(own, half), :]

    h2_copies = [
        remote(
            h2_ref.at[s, pl.ds(own, half)], h2_ref.at[s, pl.ds(own, half)], h2_sem.at[s, 0], h2_sem.at[s, 1],
            "tensor", core,
        )
        for s in range(seqs)
    ]

    def norm_two(s):
        for cp in ctx_copies[s]:
            cp.wait()
        gain = gain_ref[1:2, :].astype(F32)
        b1 = shift_ref[1:2, :].astype(F32)
        b2 = shift_ref[2:3, :].astype(F32)
        size = half // 2

        def body(i):
            r = rows_at(i, size)
            x1 = tok[rows_at(i, size, s * length + own), :].astype(F32) + b2
            for g in range(groups):
                x1 = x1 + nn(ctx_g[s, g, r, :], ow_ref[g * local : (g + 1) * local, :])
            x1_ref[s, r, :] = x1
            scaled, _ = normalize(x1)
            h2_ref[s, rows_at(i, size, own), :] = (scaled * gain + b1).astype(BF16)

        loop(half // size, body)
        h2_copies[s].start()

    act_ref, dpre_ref = ds_s, dxs

    def feed_forward(s):
        size = half // 2
        n = length // size
        b1 = b1_ref[...].astype(F32).reshape(1, hidden)
        at = lambda i: own + (i // 2) * (other - own) + (i % 2) * size
        rows = lambda i, base=0: pl.ds(pl.multiple_of(base + at(i), 16), size)

        def first(i):
            dx_ref[i % 2, :size, :] = nn(h2_ref[s, rows(i), :], fc1[...]) + b1

        def second(i):
            dact = nt(cot[rows(i, s * length), :], fc2[...])
            pre = dx_ref[i % 2, :size, :]
            phi = 0.5 * (1.0 + lax.erf(pre * 0.7071067811865476))
            act_ref[rows(i), :hidden] = (pre * phi).astype(BF16)
            slope = phi + pre * (0.3989422804014327 * jnp.exp(-0.5 * pre * pre))
            dpre = (dact * slope).astype(BF16)
            dpre_ref[rows(i), :hidden] = dpre
            add_sum(6, column_sum(dpre.astype(F32)))

        def third(i):
            far = i // 2
            r = pl.ds(pl.multiple_of((i % 2) * size, size), size)
            bank[mine_m[s] + far * (send_m[s] - mine_m[s]), r, :] = nn(act_ref[rows(i), :hidden], fc2[...]).astype(BF16)
            bank[mine_d[s] + far * (send_d[s] - mine_d[s]), r, :] = nt(dpre_ref[rows(i), :hidden], fc1[...]).astype(BF16)

        first(0)
        first(1)
        second(0)

        def body(k):
            i = k + 1

            @pl.when(k == 0)
            def _():
                h2_copies[s].wait()

            third(i - 1)
            first(i + 1)
            second(i)

        loop(n - 2, body)
        third(n - 2)
        second(n - 1)
        third(n - 1)

    def fc_grad(m, left, right, s, tile):
        def body(i):
            r = pl.ds(pl.multiple_of(i * tile, tile), tile)
            p = tn(left(r), right())
            if s > 0:
                p = p + gbuf[m, r, :].astype(F32)
            gbuf[m, r, :] = p.astype(BF16)

        loop(width // tile, body)

    def fc2_grad(s):
        fc_grad(0, lambda r: act_ref[:, r], lambda: cot[tok_rows[s], :], s, 256)

    def fc1_grad(s):
        fc_grad(1, lambda r: h2_ref[s, :, r], lambda: dpre_ref[:, :hidden], s, 256)

    piece = gbuf.shape[1] // ROW_CHUNKS // 2 // group
    span = width // COLUMN_CHUNKS

    def reduce_job(m, ch):
        job = m * CHUNKS + ch
        base = (ch // COLUMN_CHUNKS) * (gbuf.shape[1] // ROW_CHUNKS)
        cols = pl.ds((ch % COLUMN_CHUNKS) * span, span)
        part = group * piece
        sem = iter(range(red_sem.shape[1]))
        two = lambda: (red_sem.at[job, next(sem)], red_sem.at[job, next(sem)])
        rows = lambda start, n: gbuf.at[m, pl.ds(pl.multiple_of(start, 16), n), cols]

        def add(start, n, sources):
            size = piece

            def body(i):
                r = rows_at(i, size, start)
                total = gbuf[m, r, cols].astype(F32)
                for src in sources:
                    total = total + src[rows_at(i, size), :].astype(F32)
                gbuf[m, r, cols] = total.astype(BF16)

            loop(n // size, body)

        mine_at = base + xi * part
        cp = remote(rows(base + (1 - xi) * part, part), rx.at[job], *two(), "dp", xpeer)
        yield 0
        cp.start()
        yield
        cp.wait()
        add(mine_at, part, [rx.at[job]])
        cps = [
            remote(rows(mine_at + ((zi + k + 1) % group) * piece, piece), rz.at[job, k], *two(), "dp", p)
            for k, p in enumerate(zpeers)
        ]
        yield 1
        for cp in cps:
            cp.start()
        yield
        for cp in cps:
            cp.wait()
        piece_at = mine_at + zi * piece
        add(piece_at, piece, [rz.at[job, k] for k in range(group - 1)])
        for k, p in enumerate(epeers):
            cp = remote(rows(piece_at, piece), re.at[job, k], *two(), "dp", p)
            yield 1
            cp.start()
            yield
            cp.wait()
            add(piece_at, piece, [re.at[job, k]])
        done = lambda start, n: gmat_h.at[m, pl.ds(pl.multiple_of(start, 16), n), cols]
        cps = [remote(rows(piece_at, piece), done(piece_at, piece), *two(), "dp", p) for p in zpeers]
        cps.append(pltpu.make_async_copy(rows(piece_at, piece), done(piece_at, piece), red_sem.at[job, next(sem)]))
        yield 1
        for cp in cps:
            cp.start()
        yield
        for cp in cps:
            cp.wait()
        cp = remote(done(mine_at, part), done(mine_at, part), *two(), "dp", xpeer)
        yield 0
        cp.start()
        yield
        cp.wait()

    links = Links()

    dx_copies = [
        remote(dxs.at[pl.ds(own, half)], dxr_other.at[s], dx_sem.at[s, 0], dx_sem.at[s, 1], "tensor", core)
        for s in range(seqs)
    ]

    def mid(s):
        pair_d[s].finish()
        g = gain_ref[1:2, :].astype(F32)

        def body(i):
            r = rows_at(i, BLOCK)
            dh2 = pair_d[s].total(r)
            scaled, factor = normalize(x1_ref[s, r, :])
            dy = cot[rows_at(i, BLOCK, s * length + own), :].astype(F32)
            dx = dy + norm_back(dh2, scaled, factor, g)
            dx_ref[s, r, :] = dx
            dxs[rows_at(i, BLOCK, own), :] = dx.astype(BF16)
            add_sum(1, column_sum(dh2 * scaled))
            add_sum(3, column_sum(dh2))
            add_sum(4, column_sum(dx))
            add_sum(5, column_sum(dy))

        loop(half // BLOCK, body)
        dx_copies[s].start()

    def back_setup(s):
        dx_copies[s].wait()
        dxs[pl.ds(other, half), :] = dxr_other[s]
        ct_s[...] = nt(ow_ref[group_rows(t), :], dxs[...])
        for h in range(heads):
            lo = h * HEAD
            inv = linv_ref[s, h, 0:1, :]
            part = ct_s[lo : lo + HEAD, :].astype(BF16).astype(F32)
            delta = column_sum(part * ctxt_ref[s, lo : lo + HEAD, :].astype(F32)) * inv
            high = delta.astype(BF16).astype(F32)
            low = delta - high
            row = lax.broadcasted_iota(jnp.int32, (HEAD, length), 0)
            feat = jnp.where(row == 0, -high, jnp.where(row == 1, -low, 0.0))
            part = part * inv
            da_s[h, :HEAD, :] = part.astype(BF16)
            da_s[h, HEAD:, :] = feat.astype(BF16)
            dcx_s[h] = jnp.transpose(part).astype(BF16)

    def back_head(s, h):
        j = s * heads + h
        slot = j % 2
        fetch(j, slot).wait()
        for t0, n in spans:
            dp_t = nn(va[s, h], da_s[h, :, t0 : t0 + n])
            ds = (es[slot, :, t0 : t0 + n].astype(F32) * dp_t).astype(BF16)
            ds_s[:, t0 : t0 + n] = ds
            ct_s[rows_at(h, HEAD), t0 : t0 + n] = tn(ka[s, h, :, :HEAD], ds) * 0.125
        lo = h * HEAD
        dq_s[:, 2 * local + lo : 2 * local + lo + HEAD] = nn(es[slot], dcx_s[h]).astype(BF16)
        dq_s[:, local + lo : local + lo + HEAD] = nn(ds_s[...], qa[s, h, :, :HEAD]).astype(BF16)
        if j + 2 < seqs * heads:
            fetch(j + 2, slot).start()

    def back_end(s):
        dq_s[:, :local] = jnp.transpose(ct_s[...]).astype(BF16)

        def rows_out(dst, base):
            bank[dst] = nn(dq_s[pl.ds(base, half), : 3 * local], wt_s[...]).astype(BF16)

        rows_out(send_d[s], other)
        pair_g[s].start()
        rows_out(mine_d[s], own)

    def back_grads(s):
        h1 = h1_ref[s]
        for i in (2, 3, 0, 1):
            p = tn(dq_s[:, i * local : (i + 1) * local], h1) if i < 3 else nn(ctxt_ref[s], dxs[...])
            r = slice(i * local, (i + 1) * local)
            if s > 0:
                p = p + gbuf[2, r, :].astype(F32)
            gbuf[2, r, :] = p.astype(BF16)
        add_sum(7, column_sum(dq_s[:, :local].astype(F32)))
        sv[8:9, :local] += column_sum(dq_s[:, 2 * local : 3 * local].astype(F32))

    def place(k, stage, dst_h, s):
        rows = pl.ds(pl.multiple_of(s * length + own, 16), half)
        here = pltpu.make_async_copy(stage, dst_h.at[rows], out_sem.at[k, 0])
        there = remote(stage, dst_h.at[rows], out_sem.at[k, 1], out_sem.at[k, 2], "tensor", core)
        here.start()
        there.start()
        return here, there

    def layer_out(s):
        pair_m[s].finish()
        b3 = shift_ref[3:4, :].astype(F32)
        stage = bank.at[send_m[s]]

        def body(i):
            r = rows_at(i, BLOCK)
            stage[r, :] = (x1_ref[s, r, :] + pair_m[s].total(r) + b3).astype(BF16)

        loop(half // BLOCK, body)
        return place(s, stage, out_h, s)

    def input_grad(s):
        pair_g[s].finish()
        g = gain_ref[0:1, :].astype(F32)
        stage = bank.at[send_d[s]]

        def body(i):
            r = rows_at(i, BLOCK)
            dh1 = pair_g[s].total(r)
            scaled, factor = normalize(tok[rows_at(i, BLOCK, s * length + own), :].astype(F32))
            stage[r, :] = (dx_ref[s, r, :] + norm_back(dh1, scaled, factor, g)).astype(BF16)
            add_sum(0, column_sum(dh1 * scaled))
            add_sum(2, column_sum(dh1))

        loop(half // BLOCK, body)
        return place(seqs + s, stage, grad_h, s)

    def small_job():
        sem = iter(range(small_sem.shape[0]))
        two = lambda: (small_sem.at[next(sem)], small_sem.at[next(sem)])
        slot = iter(range(svr.shape[0]))
        k = next(slot)
        cp = remote(sv.at[pl.ds(0, 6)], svr.at[k, pl.ds(0, 6)], *two(), "tensor", core)
        cp.start()
        yield
        cp.wait()
        sv[0:6, :] += svr[k, 0:6, :]
        for p in [xpeer]:
            k = next(slot)
            cp = remote(sv, svr.at[k], *two(), "dp", p)
            cp.start()
            yield
            cp.wait()
            sv[...] += svr[k]
        base = k + 1
        cps = []
        for i, p in enumerate(zpeers):
            cps.append(remote(sv, svr.at[base + zi], *two(), "dp", p))
        for cp in cps:
            cp.start()
        svr[base + zi] = sv[...]
        yield
        for cp in cps:
            cp.wait()
        total = svr[base]
        for i in range(1, group):
            total = total + svr[base + i]
        sv[...] = total
        for i, p in enumerate(epeers):
            k = base + group + i
            cp = remote(sv, svr.at[k], *two(), "dp", p)
            cp.start()
            yield
            cp.wait()
            sv[...] += svr[k]
        small_ref[...] = sv[...]

    load_tok0.wait()
    load_w.wait()
    load_ow.wait()
    ow_copies[0].start()
    ow_copies[1].start()
    project(0)
    attend(0)
    ow_copies[1].wait()
    ow_copies[2].start()
    load_tok1.wait()
    for s in range(1, seqs):
        project(s)
        attend(s)
    ow_copies[0].wait()
    ow_copies[2].wait()
    load_fc1.wait()
    load_cot.wait()
    load_fc2.wait()
    for k in (seqs * heads - 2, seqs * heads - 1):
        spill(k, k % 2).wait()
    for k in (0, 1):
        fetch(k, k % 2).start()
    end = seqs - 1
    for s in range(seqs):
        norm_two(s)
        feed_forward(s)
        pair_d[s].start()
        pair_m[s].start()
        fc2_grad(s)
        pair_d[s].middle()
        if s == end:
            links.add(*[reduce_job(0, ch) for ch in range(CHUNKS)])
        pair_m[s].gather()
        fc1_grad(s)
    links.add(*[reduce_job(1, ch) for ch in range(CHUNKS)])
    tick = lambda k: links.tick(TICKS[k])
    for s in range(seqs):
        last = int(s == end)
        if s > 0:
            tick(0)
        mid(s)
        tick(1 + last)
        back_setup(s)
        for h in range(heads):
            back_head(s, h)
            tick(3 + 3 * last + min(h, 2))
            if h == 1:
                pair_m[s].to_chip.start()
        back_end(s)
        back_grads(s)
        pair_g[s].middle()
        if s == end:
            links.add(*[reduce_job(2, ch) for ch in reversed(range(CHUNKS))])
        tick(9 + last)
    copies = []
    for s in range(end):
        copies += input_grad(s)
        tick(11)
        for cp in layer_out(s):
            cp.wait()
        tick(12)
    copies += input_grad(end)
    small = small_job()
    next(small)
    tick(13)
    next(small, None)
    copies += layer_out(end)
    while links.tick():
        next(small, None)
    for _ in small:
        pass
    for cp in copies:
        cp.wait()


def struct(shape, dtype):
    return jax.ShapeDtypeStruct(shape, dtype)


def layer(n_dp, starts, marks, gains, shifts, qvb, b1, tokens, cot, w, ow, fc1, fc2):
    rows, width = tokens.shape
    seqs = starts.shape[0]
    length = rows // seqs
    half = length // 2
    local = w.shape[0] // 3
    heads = local // HEAD
    hidden = fc1.shape[1]
    group = min(4, n_dp // 2)
    extra = (n_dp // (2 * group)).bit_length() - 1
    matrix = 4 * local
    part = matrix // ROW_CHUNKS // 2
    span = width // COLUMN_CHUNKS
    piece = part // group
    jobs = 3 * CHUNKS
    smem = pl.BlockSpec(memory_space=pltpu.SMEM)
    vmem = pl.BlockSpec(memory_space=pltpu.VMEM)
    hbm = pl.BlockSpec(memory_space=pl.ANY)
    v = pltpu.VMEM
    dma = pltpu.SemaphoreType.DMA
    small = 9
    return pl.pallas_call(
        functools.partial(layer_kernel, seqs, length, heads, n_dp, group, extra),
        in_specs=[smem, smem, vmem, vmem, vmem, vmem] + [hbm] * 6,
        out_specs=[hbm, hbm, hbm, vmem, hbm],
        scratch_shapes=[
            v((rows, width), BF16),
            v((rows, width), BF16),
            v((4 * local, width), BF16),
            v(fc1.shape, BF16),
            v(fc2.shape, BF16),
            v((seqs, length, width), BF16),
            v((seqs, heads, length, 2 * HEAD), BF16),
            v((seqs, heads, length, 2 * HEAD), BF16),
            v((seqs, heads, length, 2 * HEAD), BF16),
            v((2, length, length), BF16),
            v((local, length), F32),
            v((seqs, local, length), BF16),
            v((seqs, heads, 8, length), F32),
            v((3 * seqs + 1, half, width), BF16),
            v((seqs + 1, half, width), BF16),
            v((3 * seqs, half, width), BF16),
            v((seqs, length, local), BF16),
            v((seqs, 4, half, local), BF16),
            v((seqs, half, width), F32),
            v((seqs, half, width), F32),
            v((seqs, length, width), BF16),
            v((length, width), BF16),
            v((seqs, half, width), BF16),
            v((length, length), BF16),
            v((heads, 2 * HEAD, length), BF16),
            v((heads, length, HEAD), BF16),
            v((length, 3 * local), BF16),
            v((3 * local, width), BF16),
            v((3, matrix, width), BF16),
            v((jobs, part, span), BF16),
            v((jobs, group - 1, piece, span), BF16),
            v((jobs, max(extra, 1), piece, span), BF16),
            v((small, width), F32),
            v((2 + group + extra, small, width), F32),
            dma((7,)),
            dma((4,)),
            dma((seqs, 3, 2)),
            dma((3, 2)),
            dma((4 * seqs, 4)),
            dma((seqs, 2)),
            dma((seqs, 2)),
            dma((jobs, 5 + 4 * (group - 1) + 2 * extra)),
            dma((2 * seqs, 3)),
            dma((4 + 2 * (group - 1) + 2 * extra,)),
        ],
        out_shape=[
            struct((rows, width), BF16),
            struct((rows, width), BF16),
            struct((3, matrix, width), BF16),
            struct((small, width), F32),
            struct((seqs * heads, length, length), BF16),
        ],
        compiler_params=pltpu.CompilerParams(
            collective_id=1, has_side_effects=True, vmem_limit_bytes=63 * 1024 * 1024
        ),
        name="layer",
        cost_estimate=pl.CostEstimate(flops=24 * 10**9, bytes_accessed=50 * 10**6, transcendentals=8 * 10**6),
    )(starts, marks, gains, shifts, qvb, b1, tokens, cot, w, ow, fc1, fc2)


def finish_kernel(
    out_h, grad_h, mats_h, small_ref, out_o, grad_o, gain_o, shift_o, qkv_o, qvb_o, ow_o, fc1_o, b1_o, fc2_o,
    low, wide, rows, load_sem, store_sem,
):
    local = qvb_o.shape[1]
    loads = [pltpu.make_async_copy(mats_h.at[m], low.at[m], load_sem.at[m]) for m in range(3)]
    for k, ref in enumerate((out_h, grad_h)):
        loads.append(pltpu.make_async_copy(ref, rows.at[k], load_sem.at[3 + k]))
    for cp in loads:
        cp.start()
    stores = []
    gain_o[...] = small_ref[0:2, :]
    shift_o[...] = small_ref[2:6, :]
    b1_o[...] = small_ref[6, : b1_o.shape[0]]
    qvb_o[...] = small_ref[7:9, :local]
    targets = ([(fc2_o, 0, fc2_o.shape[0])], [(fc1_o, 0, fc1_o.shape[0])], [(qkv_o, 0, 3 * local), (ow_o, 3 * local, local)])
    for m in range(3):
        loads[m].wait()
        wide[m] = low[m].astype(F32)
        for k, (ref, start, n) in enumerate(targets[m]):
            cp = pltpu.make_async_copy(wide.at[m, pl.ds(start, n)], ref, store_sem.at[2 + m + k])
            cp.start()
            stores.append(cp)
    for k, ref in enumerate((out_o, grad_o)):
        loads[3 + k].wait()
        cp = pltpu.make_async_copy(rows.at[k], ref, store_sem.at[k])
        cp.start()
        stores.append(cp)
    for cp in stores:
        cp.wait()


def finish(local, hidden, layer_out, input_grad, mats, small):
    rows, width = layer_out.shape
    vmem = pl.BlockSpec(memory_space=pltpu.VMEM)
    hbm = pl.BlockSpec(memory_space=pltpu.HBM)
    return pl.pallas_call(
        finish_kernel,
        in_specs=[hbm, hbm, hbm, vmem],
        out_specs=[hbm, hbm, vmem, vmem, hbm, vmem, hbm, hbm, vmem, hbm],
        scratch_shapes=[
            pltpu.VMEM(mats.shape, BF16),
            pltpu.VMEM(mats.shape, F32),
            pltpu.VMEM((2, rows, width), BF16),
            pltpu.SemaphoreType.DMA((5,)),
            pltpu.SemaphoreType.DMA((6,)),
        ],
        out_shape=[
            struct((rows, width), BF16),
            struct((rows, width), BF16),
            struct((2, width), F32),
            struct((4, width), F32),
            struct((3 * local, width), F32),
            struct((2, local), F32),
            struct((local, width), F32),
            struct((width, hidden), F32),
            struct((hidden,), F32),
            struct((hidden, width), F32),
        ],
        compiler_params=pltpu.CompilerParams(vmem_limit_bytes=63 * 1024 * 1024),
        name="finish",
    )(layer_out, input_grad, mats, small)


def shards(
    n_dp, tokens, clip_starts, cls_index, norm_gains, shifts, qkv_weight, qv_bias,
    out_weight, fc1_weight, fc1_bias, fc2_weight, cotangent,
):
    width = tokens.shape[1]
    local = qv_bias.shape[1]
    hidden = fc1_bias.shape[0]
    w = jnp.transpose(qkv_weight, (1, 2, 0)).reshape(3 * local, width)
    layer_out, input_grad, mats, small, _ = layer(
        n_dp, clip_starts, cls_index, norm_gains, shifts, qv_bias, fc1_bias, tokens, cotangent,
        w, out_weight, fc1_weight, fc2_weight,
    )
    out, grad, gain, shift, qkv, qvb, ow, fc1, b1, fc2 = finish(local, hidden, layer_out, input_grad, mats, small)
    qkv = jnp.transpose(qkv.reshape(3, local, width), (2, 0, 1))
    return out, grad, gain, shift, qkv, qvb, ow, fc1, b1, fc2


def solution(mesh):
    row = P("dp", None)
    return jax.shard_map(
        functools.partial(shards, mesh.shape["dp"]),
        mesh=mesh,
        in_specs=(
            row,
            row,
            row,
            P(),
            P(),
            P(None, None, "tensor"),
            P(None, "tensor"),
            P("tensor", None),
            P(None, "tensor"),
            P("tensor"),
            P("tensor", None),
            row,
        ),
        out_specs=(
            row,
            row,
            P(),
            P(),
            P(None, None, "tensor"),
            P(None, "tensor"),
            P("tensor", None),
            P(None, "tensor"),
            P("tensor"),
            P("tensor", None),
        ),
        check_vma=False,
    )
```

```python
import functools

import jax
import jax.numpy as jnp
from jax import lax
from jax.experimental import pallas as pl
from jax.experimental.pallas import tpu as pltpu
from jax.sharding import PartitionSpec as P

HEAD = 64
EPS = 1e-06
F32 = jnp.float32
BF16 = jnp.bfloat16
BLOCK = 112
ROW_CHUNKS = 2
COLUMN_CHUNKS = 1
CHUNKS = ROW_CHUNKS * COLUMN_CHUNKS
TICKS = (1, 0, 1, 0, 1, 1, 1, 1, 1, 1, 2, 3, 4, 4)
MESH = pl.DeviceIdType.MESH


def nn(a, b):
    return lax.dot_general(a, b, (((1,), (0,)), ((), ())), preferred_element_type=F32)


def nt(a, b):
    return lax.dot_general(a, b, (((1,), (1,)), ((), ())), preferred_element_type=F32)


def tn(a, b):
    return lax.dot_general(a, b, (((0,), (0,)), ((), ())), preferred_element_type=F32)


def normalize(x):
    centre = x - jnp.mean(x, axis=-1, keepdims=True)
    factor = lax.rsqrt(jnp.mean(centre * centre, axis=-1, keepdims=True) + EPS)
    return centre * factor, factor


def norm_back(grad, scaled, factor, gain):
    inner = grad * gain
    return factor * (
        inner
        - jnp.mean(inner, axis=-1, keepdims=True)
        - scaled * jnp.mean(inner * scaled, axis=-1, keepdims=True)
    )


def column_sum(x):
    return jnp.sum(x, axis=0, keepdims=True)


def loop(n, body):
    lax.fori_loop(0, n, lambda i, carry: (body(i), carry)[1], 0)


def rows_at(i, size, base=0):
    return pl.ds(pl.multiple_of(base + i * size, 16), size)


def remote(src, dst, send_sem, recv_sem, axis, index):
    return pltpu.make_async_remote_copy(
        src_ref=src, dst_ref=dst, send_sem=send_sem, recv_sem=recv_sem,
        device_id={axis: index}, device_id_type=MESH,
    )


class Pair:
    def __init__(self, send, mine, from_core, from_chip, sems, core, chip):
        self.send, self.mine, self.from_core, self.from_chip = send, mine, from_core, from_chip
        self.to_core = remote(send, from_core, sems.at[0], sems.at[1], "tensor", core)
        self.to_chip = remote(mine, from_chip, sems.at[2], sems.at[3], "tensor", chip)

    def start(self):
        self.to_core.start()

    def gather(self):
        self.to_core.wait()

        def body(i):
            r = rows_at(i, BLOCK)
            self.mine[r, :] = (self.mine[r, :].astype(F32) + self.from_core[r, :].astype(F32)).astype(BF16)

        loop(self.mine.shape[0] // BLOCK, body)

    def middle(self):
        self.gather()
        self.to_chip.start()

    def finish(self):
        self.to_chip.wait()

    def total(self, r):
        return self.mine[r, :].astype(F32) + self.from_chip[r, :].astype(F32)


class Links:
    def __init__(self):
        self.ready, self.flying = ([], []), ([], [])
        self.turn = 0

    def add(self, *jobs):
        for job in jobs:
            axis = next(job, None)
            if axis is not None:
                self.ready[axis].append(job)
        self.fill()

    def fill(self):
        for axis in (0, 1):
            while self.ready[axis] and len(self.flying[axis]) < 2:
                job = self.ready[axis].pop(0)
                next(job)
                self.flying[axis].append(job)

    def tick(self, times=1):
        for _ in range(times):
            axis = self.turn if self.flying[self.turn] else 1 - self.turn
            if not self.flying[axis]:
                return False
            self.turn = 1 - axis
            self.add(self.flying[axis].pop(0))
        return True


def layer_kernel(
    seqs, length, heads, n_dp, group, extra,
    st_ref, mk_ref, gain_ref, shift_ref, qvb_ref, b1_ref, tok_h, cot_h, w_h, ow_h, fc1_h, fc2_h,
    out_h, grad_h, gmat_h, small_ref, e_h,
    tok, cot, ow_ref, fc1, fc2, h1_ref, qa, ka, va, es, ct_s, ctxt_ref, linv_ref,
    bank, fcore, fchip, ctx_n, ctx_g, x1_ref, dx_ref, h2_ref, dxs, dxr_other, ds_s, da_s, dcx_s, dq_s,
    wt_s, gbuf, rx, rz, re, sv, svr,
    load_sem, e_sem, ctx_sem, ow_sem, pair_sem, h2_sem, dx_sem, red_sem, out_sem, small_sem,
):
    half = length // 2
    width = tok.shape[1]
    hidden = fc1.shape[1]
    local = heads * HEAD
    clips = st_ref.shape[1]
    t = lax.axis_index("tensor")
    dp = lax.axis_index("dp")
    c = t % 2
    core = t + 1 - 2 * c
    chip = (t + 2) % 4
    diag = chip + 1 - 2 * (chip % 2)
    groups = ctx_g.shape[1]
    own = pl.multiple_of(c * half, half)
    other = pl.multiple_of((1 - c) * half, half)
    xi = dp % 2
    xpeer = dp + 1 - 2 * xi
    zi = (dp // 2) % group
    zpeers = [dp + 2 * ((zi + k) % group - zi) for k in range(1, group)]
    ebits = [2 * group * 2**k for k in range(extra)]
    epeers = [dp + bit - 2 * bit * ((dp // bit) % 2) for bit in ebits]

    def load(k, src, dst):
        cp = pltpu.make_async_copy(src, dst, load_sem.at[k])
        cp.start()
        return cp

    tok_rows = [pl.ds(s * length, length) for s in range(seqs)]
    load_tok0 = load(0, tok_h.at[tok_rows[0]], tok.at[tok_rows[0]])
    load_w = load(1, w_h, wt_s)
    load_tok1 = load(2, tok_h.at[pl.ds(length, (seqs - 1) * length)], tok.at[pl.ds(length, (seqs - 1) * length)])
    group_rows = lambda g: pl.ds(pl.multiple_of(g * local, 16), local)
    load_ow = load(3, ow_h, ow_ref.at[group_rows(t)])
    load_fc1 = load(4, fc1_h, fc1)
    load_cot = load(5, cot_h, cot)
    load_fc2 = load(6, fc2_h, fc2)

    barrier = pltpu.get_barrier_semaphore()
    for peer in (core, chip, diag):
        pl.semaphore_signal(barrier, inc=1, device_id={"tensor": peer}, device_id_type=MESH)
    for peer in [xpeer] + zpeers + epeers:
        pl.semaphore_signal(barrier, inc=1, device_id={"dp": peer}, device_id_type=MESH)
    pl.semaphore_wait(barrier, 4 + len(zpeers) + len(epeers))

    send_d, mine_d, mine_m = (list(range(k * seqs, (k + 1) * seqs)) for k in range(3))
    send_m = [3 * seqs] * seqs

    def pair(give, keep, core_slot, chip_slot, sem):
        return Pair(
            bank.at[give], bank.at[keep], fcore.at[core_slot], fchip.at[chip_slot], pair_sem.at[sem], core, chip
        )

    ow_copies = [
        remote(ow_ref.at[group_rows(g)], ow_ref.at[group_rows(g)], ow_sem.at[k, 0], ow_sem.at[k, 1], "tensor", p)
        for k, (g, p) in enumerate(((t, core), (t, chip), (chip, core)))
    ]
    ctx_copies = [
        [
            remote(
                ctx_n.at[s, pl.ds(start, half)], ctx_g.at[s, t], ctx_sem.at[s, k, 0], ctx_sem.at[s, k, 1], "tensor", p
            )
            for k, (p, start) in enumerate(((diag, other), (chip, own), (core, other)))
        ]
        for s in range(seqs)
    ]
    pair_d = [pair(send_d[s], mine_d[s], s, seqs + s, seqs + s) for s in range(seqs)]
    pair_m = [pair(send_m[s], mine_m[s], seqs, 2 * seqs + s, 2 * seqs + s) for s in range(seqs)]
    pair_g = [pair(send_d[s], mine_d[s], s, s, 3 * seqs + s) for s in range(seqs)]

    sv[...] = jnp.zeros_like(sv)

    def add_sum(row, value):
        sv[row : row + 1, : value.shape[1]] += value

    def spill(j, slot):
        return pltpu.make_async_copy(es.at[slot], e_h.at[j], e_sem.at[slot])

    def fetch(j, slot):
        return pltpu.make_async_copy(e_h.at[j], es.at[slot], e_sem.at[2 + slot])

    def project(s):
        gain = gain_ref[0:1, :].astype(F32)
        shift = shift_ref[0:1, :].astype(F32)
        qvb = qvb_ref[...].astype(F32)
        size = 128

        def norm(i):
            x = tok[rows_at(i, size, s * length), :].astype(F32)
            scaled, _ = normalize(x)
            h1_ref[s, rows_at(i, size), :] = (scaled * gain + shift).astype(BF16)

        loop(length // size, norm)
        block = half

        def body(i):
            r = rows_at(i, block)
            h1 = h1_ref[s, r, :]
            q = (nt(h1, wt_s[:local]) + qvb[0:1]).astype(BF16).astype(F32) * 0.125
            q = q.astype(BF16)
            k = nt(h1, wt_s[local : 2 * local]).astype(BF16)
            v = (nt(h1, wt_s[2 * local :]) + qvb[1:2]).astype(BF16)
            pos = lax.broadcasted_iota(jnp.int32, (block, HEAD), 0) + i * block
            lane = lax.broadcasted_iota(jnp.int32, (block, HEAD), 1)
            clip = jnp.zeros((block, HEAD), jnp.int32) - 1
            mark = jnp.zeros((block, HEAD), jnp.int32)
            for n in range(clips):
                clip = clip + jnp.where(pos >= st_ref[s, n], 1, 0)
                mark = mark + jnp.where(pos == mk_ref[s, n], 1, 0)
            qf = jnp.where(lane == clip, 1.0, 0.0).astype(BF16)
            hide = (lane < clips) & (lane != clip) & (mark == 0)
            kf = jnp.where(hide, -1e30, 0.0).astype(BF16)
            vf = jnp.where(lane < 2, 1.0, 0.0).astype(BF16)
            for h in range(heads):
                cols = slice(h * HEAD, h * HEAD + HEAD)
                qa[s, h, r, :] = jnp.concatenate([q[:, cols], qf], axis=1)
                ka[s, h, r, :] = jnp.concatenate([k[:, cols], kf], axis=1)
                va[s, h, r, :] = jnp.concatenate([v[:, cols], vf], axis=1)

        loop(length // block, body)

    spans = [(t0, min(256, length - t0)) for t0 in range(0, length, 256)]

    def attend(s):
        def head(h):
            j = s * heads + h
            slot = lax.rem(j, 2)

            @pl.when(j >= 2)
            def _():
                spill(j, slot).wait()

            v = va[s, h, :, :HEAD]
            for i, (t0, n) in enumerate(spans):
                sl = i % 2
                score = nt(ka[s, h], qa[s, h, t0 : t0 + n])
                dx_ref[sl, :, :n] = score[:half]
                dx_ref[sl, :, 256 : 256 + n] = score[half:]
                scores = lambda u, ch: dx_ref[sl, u % half : u % half + ch, (u // half) * 256 : (u // half) * 256 + n]
                ch = 64
                m = None
                for u in range(0, length, ch):
                    x = jnp.max(scores(u, ch).reshape(ch // 8, 8, n), axis=0)
                    m = x if m is None else jnp.maximum(m, x)
                m = jnp.max(m, axis=0, keepdims=True)
                tot = None
                for u in range(0, length, ch):
                    x = jnp.exp(scores(u, ch) - m)
                    es[slot, u : u + ch, t0 : t0 + n] = x.astype(BF16)
                    x = jnp.sum(x.reshape(ch // 8, 8, n), axis=0)
                    tot = x if tot is None else tot + x
                inv = 1.0 / jnp.sum(tot, axis=0, keepdims=True)
                linv_ref[s, h, :, t0 : t0 + n] = jnp.broadcast_to(inv, (8, n))
                ct_s[rows_at(h, HEAD), t0 : t0 + n] = tn(v, es[slot, :, t0 : t0 + n]) * inv
            spill(j, slot).start()

        loop(heads, head)
        ctxt_ref[s] = ct_s[...].astype(BF16)
        ctx_n[s] = jnp.transpose(ct_s[...]).astype(BF16)
        for cp in ctx_copies[s]:
            cp.start()
        ctx_g[s, t] = ctx_n[s, pl.ds(own, half), :]

    h2_copies = [
        remote(
            h2_ref.at[s, pl.ds(own, half)], h2_ref.at[s, pl.ds(own, half)], h2_sem.at[s, 0], h2_sem.at[s, 1],
            "tensor", core,
        )
        for s in range(seqs)
    ]

    def norm_two(s):
        for cp in ctx_copies[s]:
            cp.wait()
        gain = gain_ref[1:2, :].astype(F32)
        b1 = shift_ref[1:2, :].astype(F32)
        b2 = shift_ref[2:3, :].astype(F32)
        size = half // 2

        def body(i):
            r = rows_at(i, size)
            x1 = tok[rows_at(i, size, s * length + own), :].astype(F32) + b2
            for g in range(groups):
                x1 = x1 + nn(ctx_g[s, g, r, :], ow_ref[g * local : (g + 1) * local, :])
            x1_ref[s, r, :] = x1
            scaled, _ = normalize(x1)
            h2_ref[s, rows_at(i, size, own), :] = (scaled * gain + b1).astype(BF16)

        loop(half // size, body)
        h2_copies[s].start()

    act_ref, dpre_ref = ds_s, dxs

    def feed_forward(s):
        size = half // 2
        n = length // size
        b1 = b1_ref[...].astype(F32).reshape(1, hidden)
        at = lambda i: own + (i // 2) * (other - own) + (i % 2) * size
        rows = lambda i, base=0: pl.ds(pl.multiple_of(base + at(i), 16), size)

        def first(i):
            dx_ref[i % 2, :size, :] = nn(h2_ref[s, rows(i), :], fc1[...]) + b1

        def second(i):
            dact = nt(cot[rows(i, s * length), :], fc2[...])
            pre = dx_ref[i % 2, :size, :]
            phi = 0.5 * (1.0 + lax.erf(pre * 0.7071067811865476))
            act_ref[rows(i), :hidden] = (pre * phi).astype(BF16)
            slope = phi + pre * (0.3989422804014327 * jnp.exp(-0.5 * pre * pre))
            dpre = (dact * slope).astype(BF16)
            dpre_ref[rows(i), :hidden] = dpre
            add_sum(6, column_sum(dpre.astype(F32)))

        def third(i):
            far = i // 2
            r = pl.ds(pl.multiple_of((i % 2) * size, size), size)
            bank[mine_m[s] + far * (send_m[s] - mine_m[s]), r, :] = nn(act_ref[rows(i), :hidden], fc2[...]).astype(BF16)
            bank[mine_d[s] + far * (send_d[s] - mine_d[s]), r, :] = nt(dpre_ref[rows(i), :hidden], fc1[...]).astype(BF16)

        first(0)
        first(1)
        second(0)

        def body(k):
            i = k + 1

            @pl.when(k == 0)
            def _():
                h2_copies[s].wait()

            third(i - 1)
            first(i + 1)
            second(i)

        loop(n - 2, body)
        third(n - 2)
        second(n - 1)
        third(n - 1)

    def fc_grad(m, left, right, s, tile):
        def body(i):
            r = pl.ds(pl.multiple_of(i * tile, tile), tile)
            p = tn(left(r), right())
            if s > 0:
                p = p + gbuf[m, r, :].astype(F32)
            gbuf[m, r, :] = p.astype(BF16)

        loop(width // tile, body)

    def fc2_grad(s):
        fc_grad(0, lambda r: act_ref[:, r], lambda: cot[tok_rows[s], :], s, 256)

    def fc1_grad(s):
        fc_grad(1, lambda r: h2_ref[s, :, r], lambda: dpre_ref[:, :hidden], s, 256)

    piece = gbuf.shape[1] // ROW_CHUNKS // 2 // group
    span = width // COLUMN_CHUNKS

    def reduce_job(m, ch):
        job = m * CHUNKS + ch
        base = (ch // COLUMN_CHUNKS) * (gbuf.shape[1] // ROW_CHUNKS)
        cols = pl.ds((ch % COLUMN_CHUNKS) * span, span)
        part = group * piece
        sem = iter(range(red_sem.shape[1]))
        two = lambda: (red_sem.at[job, next(sem)], red_sem.at[job, next(sem)])
        rows = lambda start, n: gbuf.at[m, pl.ds(pl.multiple_of(start, 16), n), cols]

        def add(start, n, sources):
            size = piece

            def body(i):
                r = rows_at(i, size, start)
                total = gbuf[m, r, cols].astype(F32)
                for src in sources:
                    total = total + src[rows_at(i, size), :].astype(F32)
                gbuf[m, r, cols] = total.astype(BF16)

            loop(n // size, body)

        mine_at = base + xi * part
        cp = remote(rows(base + (1 - xi) * part, part), rx.at[job], *two(), "dp", xpeer)
        yield 0
        cp.start()
        yield
        cp.wait()
        add(mine_at, part, [rx.at[job]])
        cps = [
            remote(rows(mine_at + ((zi + k + 1) % group) * piece, piece), rz.at[job, k], *two(), "dp", p)
            for k, p in enumerate(zpeers)
        ]
        yield 1
        for cp in cps:
            cp.start()
        yield
        for cp in cps:
            cp.wait()
        piece_at = mine_at + zi * piece
        add(piece_at, piece, [rz.at[job, k] for k in range(group - 1)])
        for k, p in enumerate(epeers):
            cp = remote(rows(piece_at, piece), re.at[job, k], *two(), "dp", p)
            yield 1
            cp.start()
            yield
            cp.wait()
            add(piece_at, piece, [re.at[job, k]])
        done = lambda start, n: gmat_h.at[m, pl.ds(pl.multiple_of(start, 16), n), cols]
        cps = [remote(rows(piece_at, piece), done(piece_at, piece), *two(), "dp", p) for p in zpeers]
        cps.append(pltpu.make_async_copy(rows(piece_at, piece), done(piece_at, piece), red_sem.at[job, next(sem)]))
        yield 1
        for cp in cps:
            cp.start()
        yield
        for cp in cps:
            cp.wait()
        cp = remote(done(mine_at, part), done(mine_at, part), *two(), "dp", xpeer)
        yield 0
        cp.start()
        yield
        cp.wait()

    links = Links()

    dx_copies = [
        remote(dxs.at[pl.ds(own, half)], dxr_other.at[s], dx_sem.at[s, 0], dx_sem.at[s, 1], "tensor", core)
        for s in range(seqs)
    ]

    def mid(s):
        pair_d[s].finish()
        g = gain_ref[1:2, :].astype(F32)

        def body(i):
            r = rows_at(i, BLOCK)
            dh2 = pair_d[s].total(r)
            scaled, factor = normalize(x1_ref[s, r, :])
            dy = cot[rows_at(i, BLOCK, s * length + own), :].astype(F32)
            dx = dy + norm_back(dh2, scaled, factor, g)
            dx_ref[s, r, :] = dx
            dxs[rows_at(i, BLOCK, own), :] = dx.astype(BF16)
            add_sum(1, column_sum(dh2 * scaled))
            add_sum(3, column_sum(dh2))
            add_sum(4, column_sum(dx))
            add_sum(5, column_sum(dy))

        loop(half // BLOCK, body)
        dx_copies[s].start()

    def back_setup(s):
        dx_copies[s].wait()
        dxs[pl.ds(other, half), :] = dxr_other[s]
        ct_s[...] = nt(ow_ref[group_rows(t), :], dxs[...])
        for h in range(heads):
            lo = h * HEAD
            inv = linv_ref[s, h, 0:1, :]
            part = ct_s[lo : lo + HEAD, :].astype(BF16).astype(F32)
            delta = column_sum(part * ctxt_ref[s, lo : lo + HEAD, :].astype(F32)) * inv
            high = delta.astype(BF16).astype(F32)
            low = delta - high
            row = lax.broadcasted_iota(jnp.int32, (HEAD, length), 0)
            feat = jnp.where(row == 0, -high, jnp.where(row == 1, -low, 0.0))
            part = part * inv
            da_s[h, :HEAD, :] = part.astype(BF16)
            da_s[h, HEAD:, :] = feat.astype(BF16)
            dcx_s[h] = jnp.transpose(part).astype(BF16)

    def back_head(s, h):
        j = s * heads + h
        slot = j % 2
        fetch(j, slot).wait()
        for t0, n in spans:
            dp_t = nn(va[s, h], da_s[h, :, t0 : t0 + n])
            ds = (es[slot, :, t0 : t0 + n].astype(F32) * dp_t).astype(BF16)
            ds_s[:, t0 : t0 + n] = ds
            ct_s[rows_at(h, HEAD), t0 : t0 + n] = tn(ka[s, h, :, :HEAD], ds) * 0.125
        lo = h * HEAD
        dq_s[:, 2 * local + lo : 2 * local + lo + HEAD] = nn(es[slot], dcx_s[h]).astype(BF16)
        dq_s[:, local + lo : local + lo + HEAD] = nn(ds_s[...], qa[s, h, :, :HEAD]).astype(BF16)
        if j + 2 < seqs * heads:
            fetch(j + 2, slot).start()

    def back_end(s):
        dq_s[:, :local] = jnp.transpose(ct_s[...]).astype(BF16)

        def rows_out(dst, base):
            bank[dst] = nn(dq_s[pl.ds(base, half), : 3 * local], wt_s[...]).astype(BF16)

        rows_out(send_d[s], other)
        pair_g[s].start()
        rows_out(mine_d[s], own)

    def back_grads(s):
        h1 = h1_ref[s]
        for i in (2, 3, 0, 1):
            p = tn(dq_s[:, i * local : (i + 1) * local], h1) if i < 3 else nn(ctxt_ref[s], dxs[...])
            r = slice(i * local, (i + 1) * local)
            if s > 0:
                p = p + gbuf[2, r, :].astype(F32)
            gbuf[2, r, :] = p.astype(BF16)
        add_sum(7, column_sum(dq_s[:, :local].astype(F32)))
        sv[8:9, :local] += column_sum(dq_s[:, 2 * local : 3 * local].astype(F32))

    def place(k, stage, dst_h, s):
        rows = pl.ds(pl.multiple_of(s * length + own, 16), half)
        here = pltpu.make_async_copy(stage, dst_h.at[rows], out_sem.at[k, 0])
        there = remote(stage, dst_h.at[rows], out_sem.at[k, 1], out_sem.at[k, 2], "tensor", core)
        here.start()
        there.start()
        return here, there

    def layer_out(s):
        pair_m[s].finish()
        b3 = shift_ref[3:4, :].astype(F32)
        stage = bank.at[send_m[s]]

        def body(i):
            r = rows_at(i, BLOCK)
            stage[r, :] = (x1_ref[s, r, :] + pair_m[s].total(r) + b3).astype(BF16)

        loop(half // BLOCK, body)
        return place(s, stage, out_h, s)

    def input_grad(s):
        pair_g[s].finish()
        g = gain_ref[0:1, :].astype(F32)
        stage = bank.at[send_d[s]]

        def body(i):
            r = rows_at(i, BLOCK)
            dh1 = pair_g[s].total(r)
            scaled, factor = normalize(tok[rows_at(i, BLOCK, s * length + own), :].astype(F32))
            stage[r, :] = (dx_ref[s, r, :] + norm_back(dh1, scaled, factor, g)).astype(BF16)
            add_sum(0, column_sum(dh1 * scaled))
            add_sum(2, column_sum(dh1))

        loop(half // BLOCK, body)
        return place(seqs + s, stage, grad_h, s)

    def small_job():
        sem = iter(range(small_sem.shape[0]))
        two = lambda: (small_sem.at[next(sem)], small_sem.at[next(sem)])
        slot = iter(range(svr.shape[0]))
        k = next(slot)
        cp = remote(sv.at[pl.ds(0, 6)], svr.at[k, pl.ds(0, 6)], *two(), "tensor", core)
        cp.start()
        yield
        cp.wait()
        sv[0:6, :] += svr[k, 0:6, :]
        for p in [xpeer]:
            k = next(slot)
            cp = remote(sv, svr.at[k], *two(), "dp", p)
            cp.start()
            yield
            cp.wait()
            sv[...] += svr[k]
        base = k + 1
        cps = []
        for i, p in enumerate(zpeers):
            cps.append(remote(sv, svr.at[base + zi], *two(), "dp", p))
        for cp in cps:
            cp.start()
        svr[base + zi] = sv[...]
        yield
        for cp in cps:
            cp.wait()
        total = svr[base]
        for i in range(1, group):
            total = total + svr[base + i]
        sv[...] = total
        for i, p in enumerate(epeers):
            k = base + group + i
            cp = remote(sv, svr.at[k], *two(), "dp", p)
            cp.start()
            yield
            cp.wait()
            sv[...] += svr[k]
        small_ref[...] = sv[...]

    load_tok0.wait()
    load_w.wait()
    load_ow.wait()
    ow_copies[0].start()
    ow_copies[1].start()
    project(0)
    attend(0)
    ow_copies[1].wait()
    ow_copies[2].start()
    load_tok1.wait()
    for s in range(1, seqs):
        project(s)
        attend(s)
    ow_copies[0].wait()
    ow_copies[2].wait()
    load_fc1.wait()
    load_cot.wait()
    load_fc2.wait()
    for k in (seqs * heads - 2, seqs * heads - 1):
        spill(k, k % 2).wait()
    for k in (0, 1):
        fetch(k, k % 2).start()
    end = seqs - 1
    for s in range(seqs):
        norm_two(s)
        feed_forward(s)
        pair_d[s].start()
        pair_m[s].start()
        fc2_grad(s)
        pair_d[s].middle()
        if s == end:
            links.add(*[reduce_job(0, ch) for ch in range(CHUNKS)])
        pair_m[s].gather()
        fc1_grad(s)
    links.add(*[reduce_job(1, ch) for ch in range(CHUNKS)])
    tick = lambda k: links.tick(TICKS[k])
    for s in range(seqs):
        last = int(s == end)
        if s > 0:
            tick(0)
        mid(s)
        tick(1 + last)
        back_setup(s)
        for h in range(heads):
            back_head(s, h)
            tick(3 + 3 * last + min(h, 2))
            if h == 0:
                pair_m[s].to_chip.start()
        back_end(s)
        back_grads(s)
        pair_g[s].middle()
        if s == end:
            links.add(*[reduce_job(2, ch) for ch in reversed(range(CHUNKS))])
        tick(9 + last)
    copies = []
    for s in range(end):
        copies += input_grad(s)
        tick(11)
        for cp in layer_out(s):
            cp.wait()
        tick(12)
    copies += input_grad(end)
    small = small_job()
    next(small)
    tick(13)
    next(small, None)
    copies += layer_out(end)
    while links.tick():
        next(small, None)
    for _ in small:
        pass
    for cp in copies:
        cp.wait()


def struct(shape, dtype):
    return jax.ShapeDtypeStruct(shape, dtype)


def layer(n_dp, starts, marks, gains, shifts, qvb, b1, tokens, cot, w, ow, fc1, fc2):
    rows, width = tokens.shape
    seqs = starts.shape[0]
    length = rows // seqs
    half = length // 2
    local = w.shape[0] // 3
    heads = local // HEAD
    hidden = fc1.shape[1]
    group = min(4, n_dp // 2)
    extra = (n_dp // (2 * group)).bit_length() - 1
    matrix = 4 * local
    part = matrix // ROW_CHUNKS // 2
    span = width // COLUMN_CHUNKS
    piece = part // group
    jobs = 3 * CHUNKS
    smem = pl.BlockSpec(memory_space=pltpu.SMEM)
    vmem = pl.BlockSpec(memory_space=pltpu.VMEM)
    hbm = pl.BlockSpec(memory_space=pl.ANY)
    v = pltpu.VMEM
    dma = pltpu.SemaphoreType.DMA
    small = 9
    return pl.pallas_call(
        functools.partial(layer_kernel, seqs, length, heads, n_dp, group, extra),
        in_specs=[smem, smem, vmem, vmem, vmem, vmem] + [hbm] * 6,
        out_specs=[hbm, hbm, hbm, vmem, hbm],
        scratch_shapes=[
            v((rows, width), BF16),
            v((rows, width), BF16),
            v((4 * local, width), BF16),
            v(fc1.shape, BF16),
            v(fc2.shape, BF16),
            v((seqs, length, width), BF16),
            v((seqs, heads, length, 2 * HEAD), BF16),
            v((seqs, heads, length, 2 * HEAD), BF16),
            v((seqs, heads, length, 2 * HEAD), BF16),
            v((2, length, length), BF16),
            v((local, length), F32),
            v((seqs, local, length), BF16),
            v((seqs, heads, 8, length), F32),
            v((3 * seqs + 1, half, width), BF16),
            v((seqs + 1, half, width), BF16),
            v((3 * seqs, half, width), BF16),
            v((seqs, length, local), BF16),
            v((seqs, 4, half, local), BF16),
            v((seqs, half, width), F32),
            v((seqs, half, width), F32),
            v((seqs, length, width), BF16),
            v((length, width), BF16),
            v((seqs, half, width), BF16),
            v((length, length), BF16),
            v((heads, 2 * HEAD, length), BF16),
            v((heads, length, HEAD), BF16),
            v((length, 3 * local), BF16),
            v((3 * local, width), BF16),
            v((3, matrix, width), BF16),
            v((jobs, part, span), BF16),
            v((jobs, group - 1, piece, span), BF16),
            v((jobs, max(extra, 1), piece, span), BF16),
            v((small, width), F32),
            v((2 + group + extra, small, width), F32),
            dma((7,)),
            dma((4,)),
            dma((seqs, 3, 2)),
            dma((3, 2)),
            dma((4 * seqs, 4)),
            dma((seqs, 2)),
            dma((seqs, 2)),
            dma((jobs, 5 + 4 * (group - 1) + 2 * extra)),
            dma((2 * seqs, 3)),
            dma((4 + 2 * (group - 1) + 2 * extra,)),
        ],
        out_shape=[
            struct((rows, width), BF16),
            struct((rows, width), BF16),
            struct((3, matrix, width), BF16),
            struct((small, width), F32),
            struct((seqs * heads, length, length), BF16),
        ],
        compiler_params=pltpu.CompilerParams(
            collective_id=1, has_side_effects=True, vmem_limit_bytes=63 * 1024 * 1024
        ),
        name="layer",
        cost_estimate=pl.CostEstimate(flops=24 * 10**9, bytes_accessed=50 * 10**6, transcendentals=8 * 10**6),
    )(starts, marks, gains, shifts, qvb, b1, tokens, cot, w, ow, fc1, fc2)


def finish_kernel(
    out_h, grad_h, mats_h, small_ref, out_o, grad_o, gain_o, shift_o, qkv_o, qvb_o, ow_o, fc1_o, b1_o, fc2_o,
    low, wide, rows, load_sem, store_sem,
):
    local = qvb_o.shape[1]
    whole_rows = [pltpu.make_async_copy(ref, rows.at[k], load_sem.at[3 + k]) for k, ref in enumerate((out_h, grad_h))]
    loads = [pltpu.make_async_copy(mats_h.at[m], low.at[m], load_sem.at[m]) for m in range(3)]
    for cp in loads + whole_rows:
        cp.start()
    gain_o[...] = small_ref[0:2, :]
    shift_o[...] = small_ref[2:6, :]
    b1_o[...] = small_ref[6, : b1_o.shape[0]]
    qvb_o[...] = small_ref[7:9, :local]
    stores = []
    for m in range(3):
        loads[m].wait()
        for k in range(4):
            r = pl.ds(k * local, local)
            wide[m, r, :] = low[m, r, :].astype(F32)
            target = (fc2_o.at[r], fc1_o.at[r], qkv_o.at[r] if k < 3 else ow_o)[m]
            stores.append(pltpu.make_async_copy(wide.at[m, r], target, store_sem.at[2 + 4 * m + k]))
            stores[-1].start()
        if m < 2:
            whole_rows[m].wait()
            stores.append(pltpu.make_async_copy(rows.at[m], (out_o, grad_o)[m], store_sem.at[m]))
            stores[-1].start()
    for cp in stores:
        cp.wait()


def finish(local, hidden, layer_out, input_grad, mats, small):
    rows, width = layer_out.shape
    vmem = pl.BlockSpec(memory_space=pltpu.VMEM)
    hbm = pl.BlockSpec(memory_space=pltpu.HBM)
    return pl.pallas_call(
        finish_kernel,
        in_specs=[hbm, hbm, hbm, vmem],
        out_specs=[hbm, hbm, vmem, vmem, hbm, vmem, hbm, hbm, vmem, hbm],
        scratch_shapes=[
            pltpu.VMEM(mats.shape, BF16),
            pltpu.VMEM(mats.shape, F32),
            pltpu.VMEM((2, rows, width), BF16),
            pltpu.SemaphoreType.DMA((5,)),
            pltpu.SemaphoreType.DMA((14,)),
        ],
        out_shape=[
            struct((rows, width), BF16),
            struct((rows, width), BF16),
            struct((2, width), F32),
            struct((4, width), F32),
            struct((3 * local, width), F32),
            struct((2, local), F32),
            struct((local, width), F32),
            struct((width, hidden), F32),
            struct((hidden,), F32),
            struct((hidden, width), F32),
        ],
        compiler_params=pltpu.CompilerParams(vmem_limit_bytes=63 * 1024 * 1024),
        name="finish",
    )(layer_out, input_grad, mats, small)


def shards(
    n_dp, tokens, clip_starts, cls_index, norm_gains, shifts, qkv_weight, qv_bias,
    out_weight, fc1_weight, fc1_bias, fc2_weight, cotangent,
):
    width = tokens.shape[1]
    local = qv_bias.shape[1]
    hidden = fc1_bias.shape[0]
    w = jnp.transpose(qkv_weight, (1, 2, 0)).reshape(3 * local, width)
    layer_out, input_grad, mats, small, _ = layer(
        n_dp, clip_starts, cls_index, norm_gains, shifts, qv_bias, fc1_bias, tokens, cotangent,
        w, out_weight, fc1_weight, fc2_weight,
    )
    out, grad, gain, shift, qkv, qvb, ow, fc1, b1, fc2 = finish(local, hidden, layer_out, input_grad, mats, small)
    qkv = jnp.transpose(qkv.reshape(3, local, width), (2, 0, 1))
    return out, grad, gain, shift, qkv, qvb, ow, fc1, b1, fc2


def solution(mesh):
    row = P("dp", None)
    return jax.shard_map(
        functools.partial(shards, mesh.shape["dp"]),
        mesh=mesh,
        in_specs=(
            row,
            row,
            row,
            P(),
            P(),
            P(None, None, "tensor"),
            P(None, "tensor"),
            P("tensor", None),
            P(None, "tensor"),
            P("tensor"),
            P("tensor", None),
            row,
        ),
        out_specs=(
            row,
            row,
            P(),
            P(),
            P(None, None, "tensor"),
            P(None, "tensor"),
            P("tensor", None),
            P(None, "tensor"),
            P("tensor"),
            P("tensor", None),
        ),
        check_vma=False,
    )
```
